32 devices in a mesh: fsdp: 32 (over z, y, x, core).
Axes of the slice: x: 2, y: 2, z: 4, core: 2. Of those that a mesh axis runs over, the one named last changes fastest.
Arguments:
- tokens: bfloat16 [8192, 2048], P('fsdp'), may hold values from -6 to 6
- per_layer: bfloat16 [8192, 256], P('fsdp'), may hold values from -6 to 6
- cotangent: bfloat16 [8192, 2048], P('fsdp'), may hold values from -6 to 6
- seq_lengths: int32 [5], replicated, may hold values from 1024 to 2048, as said below
- seq_order: int32 [5], replicated, may hold values from 0 to 4, each once
- qkv_weight: bfloat16 [2048, 3072], P('fsdp'), may hold values from -0.125 to 0.125
- out_weight: bfloat16 [2048, 2048], P('fsdp'), may hold values from -2 to 2
- ffn_weights: bfloat16 [8192, 3, 2048], P('fsdp'), may hold values from -0.125 to 0.125
- side_weights: bfloat16 [2048, 640], P('fsdp'), may hold values from -0.125 to 0.125
- norm_gains: bfloat16 [4608], P('fsdp'), may hold values from 0.25 to 1.75
Outputs:
- output: bfloat16 [8192, 2048], P('fsdp')
- input_grad: bfloat16 [8192, 2048], P('fsdp')
- per_layer_grad: bfloat16 [8192, 256], P('fsdp')
- qkv_grad: float32 [2048, 3072], P('fsdp')
- out_grad: float32 [2048, 2048], P('fsdp')
- ffn_grad: float32 [8192, 3, 2048], P('fsdp')
- side_grad: float32 [2048, 640], P('fsdp')
- gains_grad: float32 [4608], P('fsdp')
The draws below stay inside these ranges and needn't reach their ends.
Inputs may be any that keep to these rules, and one draw needn't show every extreme that they name: `seq_lengths`: each length is a multiple of 128, from 1024 to 2048, and they sum to 8192; the longest is exactly 2048 and the shortest exactly 1024. The i-th sequence in the stream is the one whose length is seq_lengths[seq_order[i]].
All inputs are finite; a program needn't handle non-finite values.
Results may differ from the reference program's by a relative error of at most 0.019.
Values may be sent and summed in bfloat16 or wider, within the bound.
A program may use at most 704 MiB of HBM per device.

```python
import math
import jax
import jax.numpy as jnp
from jax import lax

D = 2048
HQ = 8
KVH = 2
HD = 256
FF = 8192
PL = 256
RANK = 64
WINDOW = 512
BLK = 128
QKV = 3072
TOKENS = 8192
NBLK = 64
SEQS = 5


def draw_seq_lengths(key, part):
    key = jax.random.fold_in(key, 11)
    pair_count = NBLK // 24
    leftover = NBLK - 24 * pair_count
    shift_key, order_key = jax.random.split(key)
    shifts = jax.random.randint(shift_key, (pair_count,), 0, 5).astype(jnp.int32)
    shifts = shifts.at[0].set(4)
    extra_block = jnp.full((min(leftover, 1),), leftover, jnp.int32)
    blocks = jnp.concatenate([12 + shifts, 12 - shifts, extra_block]).astype(jnp.int32)
    blocks = jax.random.permutation(order_key, blocks)
    return (blocks * BLK).astype(jnp.int32)


def block_scale(own_key, shape, shards, low, top_value):
    level = 1.0
    for dim, shards_of in shards:
        heights = jax.random.uniform(jax.random.fold_in(jax.random.fold_in(own_key, 6), dim), (shards_of,), jnp.float32, low / len(shards), top_value / len(shards))
        level = level * jnp.repeat(jnp.exp(heights), shape[dim] // shards_of).reshape((-1,) + (1,) * (len(shape) - 1 - dim))
    return level


def bell_draw(stream_key, shape, spread, bound, cuts=(), held_as=jnp.bfloat16):
    values = spread * jax.random.normal(stream_key, shape, jnp.float32)
    if cuts:
        values = values * block_scale(stream_key, shape, cuts, -0.22, 0.18)
    return jnp.clip(values, -bound, bound).astype(held_as)


def setup_inputs(seed: int = 0) -> dict:
    key_of = jax.random.split(jax.random.key(seed), 11)
    tokens = bell_draw(key_of[0], (TOKENS, D), 1.0, 6.0, ((0, 32),))
    per_layer = bell_draw(key_of[1], (TOKENS, PL), 1.0, 6.0, ((0, 32),))
    cotangent = bell_draw(key_of[2], (TOKENS, D), 1.0, 6.0, ((0, 32),))
    seq_lengths = draw_seq_lengths(jax.random.fold_in(key_of[10], 71), 0)
    seq_order = jax.random.permutation(key_of[4], SEQS).astype(jnp.int32)
    qkv_weight = bell_draw(key_of[5], (D, QKV), D ** -0.5, 0.125, ((0, 32),))
    out_weight = bell_draw(key_of[6], (HQ * HD, D), (max(HQ * HD * 2 // WINDOW, 1)) ** -0.5, 2.0, ((0, 32),))
    ffn_weights = bell_draw(key_of[7], (FF, 3, D), D ** -0.5, 0.125, ((0, 32),))
    side_weights = bell_draw(key_of[8], (D, 2 * (PL + RANK)), D ** -0.5, 0.125, ((0, 32),))
    norm_gains = jnp.clip(1.0 + 0.15 * jax.random.normal(key_of[9], (2 * D + 2 * HD,), jnp.float32), 0.25, 1.75).astype(jnp.bfloat16)
    return {"tokens": tokens, "per_layer": per_layer, "cotangent": cotangent, "seq_lengths": seq_lengths, "seq_order": seq_order, "qkv_weight": qkv_weight, "out_weight": out_weight, "ffn_weights": ffn_weights, "side_weights": side_weights, "norm_gains": norm_gains}


@jax.custom_vjp
def low(v):
    return lax.optimization_barrier(v.astype(jnp.bfloat16)).astype(jnp.float32)

@jax.custom_vjp
def low_back(v):
    return v

def low_keep(v):
    return (low(v), None)

def low_pass(kept, grad):
    return (grad,)

def back_keep(v):
    return (v, None)

def back_low(kept, grad):
    return (low(grad),)
low.defvjp(low_keep, low_pass)
low_back.defvjp(back_keep, back_low)
EPSILON = 1e-06
NEGATIVE = -1e+30
ROPE_BASE = 10000.0
HIGHEST = lax.Precision.HIGHEST

def inv_rms(field):
    return lax.rsqrt(lax.optimization_barrier(jnp.mean(field * field, axis=-1, keepdims=True)) + EPSILON)

def gelu_tanh(field):
    return jax.nn.gelu(field, approximate=True)

def layout(seq_lengths, seq_order, token_index):
    slot_ids = jnp.arange(seq_lengths.shape[0], dtype=jnp.int32)
    packed = lax.optimization_barrier(jnp.sum(jnp.where(seq_order[:, None] == slot_ids[None, :], seq_lengths[None, :], 0), axis=1)).astype(jnp.int32)
    starts = (jnp.cumsum(packed) - packed).astype(jnp.int32)
    segment = lax.optimization_barrier(jnp.sum((token_index[:, None] >= starts[None, :]).astype(jnp.int32), axis=1)).astype(jnp.int32) - 1
    offset = lax.optimization_barrier(jnp.max(jnp.where(starts[None, :] <= token_index[:, None], starts[None, :], 0), axis=1)).astype(jnp.int32)
    return (segment, token_index - offset)

def angles(position):
    half_width = HD // 2
    freq = ROPE_BASE ** (-2.0 * jnp.arange(half_width, dtype=jnp.float32) / HD)
    phase = position.astype(jnp.float32)[:, None] * freq[None, :]
    phase = jnp.concatenate([phase, phase], axis=-1)
    return (jnp.cos(phase)[:, None, :], jnp.sin(phase)[:, None, :])

def rotate(field, cosine, sine):
    half_width = field.shape[-1] // 2
    turned = jnp.concatenate([-field[..., half_width:], field[..., :half_width]], axis=-1)
    return field * cosine + turned * sine

def attend(query_rot, key_rot, value_low, segment):
    token_count = query_rot.shape[0]
    block_rows = math.gcd(token_count, 512)
    group_size = HQ // KVH
    pad_keys = jnp.concatenate([jnp.zeros((WINDOW, KVH, HD), jnp.float32), key_rot])
    pad_values = jnp.concatenate([jnp.zeros((WINDOW, KVH, HD), jnp.float32), value_low])
    pad_segment = jnp.concatenate([jnp.full((WINDOW,), -1, jnp.int32), segment])

    def one_block(block_id):
        first_row = block_id * block_rows
        query_part = lax.dynamic_slice_in_dim(query_rot, first_row, block_rows, 0).reshape(block_rows, KVH, group_size, HD)
        key_part = lax.dynamic_slice_in_dim(pad_keys, first_row, block_rows + WINDOW, 0)
        value_part = lax.dynamic_slice_in_dim(pad_values, first_row, block_rows + WINDOW, 0)
        query_seg = lax.dynamic_slice_in_dim(segment, first_row, block_rows, 0)
        key_seg = lax.dynamic_slice_in_dim(pad_segment, first_row, block_rows + WINDOW, 0)
        key_gap = jnp.arange(block_rows, dtype=jnp.int32)[:, None] + WINDOW - jnp.arange(block_rows + WINDOW, dtype=jnp.int32)[None, :]
        allowed = (query_seg[:, None] == key_seg[None, :]) & (key_gap >= 0) & (key_gap < WINDOW)
        scores = low_back(jnp.einsum('qkgd,nkd->kgqn', query_part, key_part, precision=HIGHEST) * HD ** (-0.5))
        scores = jnp.where(allowed[None, None], scores, NEGATIVE)
        highest = lax.optimization_barrier(jnp.max(scores, axis=-1, keepdims=True))
        exponent = jnp.exp(scores - highest)
        probs = exponent / lax.optimization_barrier(jnp.sum(exponent, axis=-1, keepdims=True))
        mixed = jnp.einsum('kgqn,nkd->qkgd', low(probs), value_part, precision=HIGHEST)
        return mixed.reshape(block_rows, HQ * HD)
    blocks = lax.map(jax.checkpoint(one_block), jnp.arange(token_count // block_rows, dtype=jnp.int32))
    return blocks.reshape(token_count, HQ * HD)

def feed_forward(normed_two, ffn_all):
    token_count = normed_two.shape[0]
    block_rows = math.gcd(token_count, 1024)
    gate_rows = ffn_all[:, 0, :]
    up_rows = ffn_all[:, 1, :]
    down_rows = ffn_all[:, 2, :]

    def one_block(rows_in):
        gate_out = low_back(jnp.dot(rows_in, gate_rows.T, precision=HIGHEST))
        up_out = low_back(jnp.dot(rows_in, up_rows.T, precision=HIGHEST))
        act_out = low_back(low(gelu_tanh(gate_out) * up_out))
        return low_back(jnp.dot(act_out, down_rows, precision=HIGHEST))
    blocks = lax.map(jax.checkpoint(one_block), normed_two.reshape(token_count // block_rows, block_rows, D))
    return blocks.reshape(token_count, D)

def forward(tokens_f, per_f, qkv_w, out_w, ffn_w, side_w, gain_w, segment, cosine, sine):
    token_count = tokens_f.shape[0]
    attn_gain = gain_w[:D]
    ffn_gain = gain_w[D:2 * D]
    query_gain = gain_w[2 * D:2 * D + HD]
    key_gain = gain_w[2 * D + HD:]
    normed = low(tokens_f * inv_rms(tokens_f) * attn_gain)
    projected = low_back(jnp.dot(normed, qkv_w, precision=HIGHEST))
    query = projected[:, :HQ * HD].reshape(token_count, HQ, HD)
    key_raw = projected[:, HQ * HD:(HQ + KVH) * HD].reshape(token_count, KVH, HD)
    value_raw = projected[:, (HQ + KVH) * HD:].reshape(token_count, KVH, HD)
    query_rot = low(rotate(query * inv_rms(query) * query_gain, cosine, sine))
    key_rot = low(rotate(key_raw * inv_rms(key_raw) * key_gain, cosine, sine))
    mixed = low_back(low(attend(query_rot, key_rot, low(value_raw), segment)))
    first_sum = tokens_f + low_back(jnp.dot(mixed, out_w, precision=HIGHEST))
    normed_two = low(first_sum * inv_rms(first_sum) * ffn_gain)
    second_sum = first_sum + feed_forward(normed_two, ffn_w)
    side_in = low_back(jnp.dot(low(second_sum), side_w[:, :PL + RANK], precision=HIGHEST))
    combined = jnp.concatenate([low(gelu_tanh(side_in[:, :PL]) * per_f), low(side_in[:, PL:])], axis=1)
    return second_sum + low_back(jnp.dot(combined, side_w[:, PL + RANK:].T, precision=HIGHEST))

def reference(tokens, per_layer, cotangent, seq_lengths, seq_order, qkv_weight, out_weight, ffn_weights, side_weights, norm_gains):
    token_index = jnp.arange(TOKENS, dtype=jnp.int32)
    segment, position = layout(seq_lengths, seq_order, token_index)
    cosine, sine = angles(position)

    def run(tokens_f, per_f, qkv_w, out_w, ffn_w, side_w, gain_w):
        return forward(tokens_f, per_f, qkv_w, out_w, ffn_w, side_w, gain_w, segment, cosine, sine)
    primals = tuple((array_in.astype(jnp.float32) for array_in in (tokens, per_layer, qkv_weight, out_weight, ffn_weights, side_weights, norm_gains)))
    result, pull_back = jax.vjp(run, *primals)
    gradients = pull_back(cotangent.astype(jnp.float32))
    return (result.astype(jnp.bfloat16), gradients[0].astype(jnp.bfloat16), gradients[1].astype(jnp.bfloat16), gradients[2], gradients[3], gradients[4], gradients[5], gradients[6])
```

```python
import jax
import jax.numpy as jnp
from jax import lax
from jax.sharding import PartitionSpec as P

D = 2048
HQ = 8
KVH = 2
HD = 256
PL = 256
RANK = 64
WINDOW = 512


EPSILON = 1e-06
NEGATIVE = -1e30
ROPE_BASE = 10000.0


GROUP = 8


def token_groups(count):
    return [[g * GROUP + i for i in range(GROUP)] for g in range(count // GROUP)]


def weight_groups(count):
    return [[g * GROUP + i for g in range(count // GROUP)] for i in range(GROUP)]


def passed_along(block, axis, distance):
    devices = range(lax.axis_size(axis))
    route = [(i - distance, i) for i in devices if i - distance in devices]
    return lax.ppermute(block, axis, route)


def inv_rms(field):
    return lax.rsqrt(jnp.mean(field * field, axis=-1, keepdims=True) + EPSILON)


def gelu_tanh(field):
    return jax.nn.gelu(field, approximate=True)


def layout(seq_lengths, seq_order, token_index):
    slot_ids = jnp.arange(seq_lengths.shape[0], dtype=jnp.int32)
    packed = jnp.sum(
        jnp.where(seq_order[:, None] == slot_ids[None, :], seq_lengths[None, :], 0), axis=1
    )
    starts = jnp.sum(jnp.where(slot_ids[None, :] < slot_ids[:, None], packed[None, :], 0), axis=1)
    segment = jnp.sum((token_index[:, None] >= starts[None, :]).astype(jnp.int32), axis=1) - 1
    offset = jnp.max(jnp.where(starts[None, :] <= token_index[:, None], starts[None, :], 0), axis=1)
    return (segment, token_index - offset)


def angles(position):
    half_width = HD // 2
    freq = ROPE_BASE ** (-2.0 * jnp.arange(half_width, dtype=jnp.float32) / HD)
    phase = position.astype(jnp.float32)[:, None] * freq[None, :]
    phase = jnp.concatenate([phase, phase], axis=-1)
    return (jnp.cos(phase)[:, None, :], jnp.sin(phase)[:, None, :])


def rotate(field, cosine, sine):
    half_width = field.shape[-1] // 2
    turned = jnp.concatenate([-field[..., half_width:], field[..., :half_width]], axis=-1)
    return field * cosine + turned * sine


def rotate_back(grad_in, cosine, sine):
    half_width = grad_in.shape[-1] // 2
    shifted = grad_in * sine
    return grad_in * cosine + jnp.concatenate(
        [shifted[..., half_width:], -shifted[..., :half_width]], axis=-1
    )


def norm_back(grad_out, field, scale_inv, gain):
    weighted = grad_out * gain
    return scale_inv * weighted - field * scale_inv**3 * jnp.mean(
        weighted * field, axis=-1, keepdims=True
    )


def contract_rows(left_op, right_op):
    return lax.dot_general(
        left_op, right_op, (((0,), (0,)), ((), ())), preferred_element_type=jnp.float32
    )


def contract_cols(left_op, right_op):
    return lax.dot_general(
        left_op, right_op, (((1,), (1,)), ((), ())), preferred_element_type=jnp.float32
    )


def split_gains(gain_all):
    gain_f = gain_all.astype(jnp.float32)
    return (gain_f[:D], gain_f[D : 2 * D], gain_f[2 * D : 2 * D + HD], gain_f[2 * D + HD :])


def soft_weights(query_four, key_rows, allowed, score_scale):
    scores = (
        jnp.einsum("qkgd,nkd->kgqn", query_four, key_rows, preferred_element_type=jnp.float32)
        * score_scale
    )
    scores = jnp.where(allowed[None, None], scores, NEGATIVE)
    highest = jnp.max(scores, axis=-1, keepdims=True)
    exponent = jnp.exp(scores - highest)
    return exponent / jnp.sum(exponent, axis=-1, keepdims=True)


def local(
    tokens,
    per_layer,
    cotangent,
    seq_lengths,
    seq_order,
    qkv_weight,
    out_weight,
    ffn_weights,
    side_weights,
    norm_gains,
):
    tok_rows = tokens.shape[0]
    my_index = lax.axis_index("fsdp")
    token_index = my_index * tok_rows + jnp.arange(tok_rows, dtype=jnp.int32)
    segment, position = layout(seq_lengths, seq_order, token_index)
    cosine, sine = angles(position)
    reach = (WINDOW + tok_rows - 2) // tok_rows
    key_index = jnp.concatenate(
        [token_index - distance * tok_rows for distance in range(reach, 0, -1)] + [token_index]
    )
    key_segment, unused_pos = layout(seq_lengths, seq_order, key_index)
    key_gap = token_index[:, None] - key_index[None, :]
    allowed = (segment[:, None] == key_segment[None, :]) & (key_gap >= 0) & (key_gap < WINDOW)
    score_scale = HD ** (-0.5)
    split_at = PL + RANK
    group_size = HQ // KVH
    query_width = HQ * HD
    kv_width = KVH * HD
    qkv_all, out_all, side_all, gain_all = (
        lax.all_gather(qkv_weight, "fsdp", axis=0, tiled=True),
        lax.all_gather(out_weight, "fsdp", axis=0, tiled=True),
        lax.all_gather(side_weights, "fsdp", axis=0, tiled=True),
        lax.all_gather(norm_gains, "fsdp", axis=0, tiled=True),
    )
    attn_gain, ffn_gain, query_gain, key_gain = split_gains(gain_all)
    tokens_f = tokens.astype(jnp.float32)
    rms_one = inv_rms(tokens_f)
    normed_b = (tokens_f * rms_one * attn_gain).astype(jnp.bfloat16)
    projected = jnp.dot(normed_b, qkv_all, preferred_element_type=jnp.float32)
    query = projected[:, :query_width].reshape(tok_rows, HQ, HD)
    key_raw = projected[:, query_width : query_width + kv_width].reshape(tok_rows, KVH, HD)
    value_raw = projected[:, query_width + kv_width :].reshape(tok_rows, KVH, HD)
    rms_query = inv_rms(query)
    rms_key = inv_rms(key_raw)
    query_b = rotate(query * rms_query * query_gain, cosine, sine).astype(jnp.bfloat16)
    key_b = rotate(key_raw * rms_key * key_gain, cosine, sine).astype(jnp.bfloat16)
    value_b = value_raw.astype(jnp.bfloat16)
    key_parts = []
    value_parts = []
    for distance in range(reach, 0, -1):
        moved_keys, moved_values = passed_along((key_b, value_b), "fsdp", distance)
        key_parts.append(moved_keys)
        value_parts.append(moved_values)
    key_rows = jnp.concatenate(key_parts + [key_b], axis=0)
    value_rows = jnp.concatenate(value_parts + [value_b], axis=0)
    query_four = query_b.reshape(tok_rows, KVH, group_size, HD)
    probs = soft_weights(query_four, key_rows, allowed, score_scale)
    probs_b = probs.astype(jnp.bfloat16)
    mixed = jnp.einsum("kgqn,nkd->qkgd", probs_b, value_rows, preferred_element_type=jnp.float32)
    mixed_b = mixed.reshape(tok_rows, query_width).astype(jnp.bfloat16)
    first_sum = tokens_f + jnp.dot(mixed_b, out_all, preferred_element_type=jnp.float32)
    rms_two = inv_rms(first_sum)
    normed_two = (first_sum * rms_two * ffn_gain).astype(jnp.bfloat16)
    count = lax.axis_size("fsdp")
    by_token, by_weight = token_groups(count), weight_groups(count)
    gate_w, up_w, down_w = (
        lax.all_gather(
            ffn_weights[:, i, :], "fsdp", axis=0, tiled=True, axis_index_groups=by_weight
        )
        for i in range(3)
    )
    normed_all = lax.all_gather(
        normed_two, "fsdp", axis=0, tiled=True, axis_index_groups=by_token
    )
    gate_out = contract_cols(normed_all, gate_w)
    up_out = contract_cols(normed_all, up_w)
    gelu_gate, pull_gate = jax.vjp(gelu_tanh, gate_out)
    act_b = (gelu_gate * up_out).astype(jnp.bfloat16)
    ffn_part = jnp.dot(act_b, down_w, preferred_element_type=jnp.float32).astype(jnp.bfloat16)
    ffn_out = lax.psum_scatter(
        ffn_part, "fsdp", scatter_dimension=0, tiled=True, axis_index_groups=by_token
    ).astype(jnp.float32)
    second_sum = first_sum + ffn_out
    second_b = second_sum.astype(jnp.bfloat16)
    side_in = jnp.dot(second_b, side_all[:, :split_at], preferred_element_type=jnp.float32)
    per_f = per_layer.astype(jnp.float32)
    gelu_per, pull_per = jax.vjp(gelu_tanh, side_in[:, :PL])
    combined = jnp.concatenate(
        [(gelu_per * per_f).astype(jnp.bfloat16), side_in[:, PL:].astype(jnp.bfloat16)], axis=1
    )
    output = (second_sum + contract_cols(combined, side_all[:, split_at:])).astype(jnp.bfloat16)
    back_qkv, back_out, back_side = qkv_all, out_all, side_all
    grad_y = cotangent.astype(jnp.float32)
    grad_comb = jnp.dot(cotangent, back_side[:, split_at:], preferred_element_type=jnp.float32)
    side_out_grad = contract_rows(cotangent, combined)
    per_layer_grad = (grad_comb[:, :PL] * gelu_per).astype(jnp.bfloat16)
    grad_per = pull_per(grad_comb[:, :PL] * per_f)[0]
    grad_side = jnp.concatenate([grad_per, grad_comb[:, PL:]], axis=1).astype(jnp.bfloat16)
    side_in_grad = contract_rows(second_b, grad_side)
    side_grad_full = jnp.concatenate([side_in_grad, side_out_grad], axis=1)
    grad_two = grad_y + contract_cols(grad_side, back_side[:, :split_at])
    grad_two_b = grad_two.astype(jnp.bfloat16)
    grad_two_all = lax.all_gather(
        grad_two_b, "fsdp", axis=0, tiled=True, axis_index_groups=by_token
    )
    grad_act_b = contract_cols(grad_two_all, down_w).astype(jnp.bfloat16)
    grad_gate_b = pull_gate(grad_act_b * up_out)[0].astype(jnp.bfloat16)
    grad_up_b = (grad_act_b * gelu_gate).astype(jnp.bfloat16)
    grad_h2 = jnp.dot(grad_gate_b, gate_w, preferred_element_type=jnp.float32)
    grad_h2 = grad_h2 + jnp.dot(grad_up_b, up_w, preferred_element_type=jnp.float32)
    grad_h2 = lax.psum_scatter(
        grad_h2.astype(jnp.bfloat16),
        "fsdp",
        scatter_dimension=0,
        tiled=True,
        axis_index_groups=by_token,
    ).astype(jnp.float32)
    ffn_grad = jnp.stack(
        [
            lax.psum_scatter(
                contract_rows(left, right).astype(jnp.bfloat16),
                "fsdp",
                scatter_dimension=0,
                tiled=True,
                axis_index_groups=by_weight,
            ).astype(jnp.float32)
            for left, right in (
                (grad_gate_b, normed_all),
                (grad_up_b, normed_all),
                (act_b, grad_two_all),
            )
        ],
        axis=1,
    )
    ffn_gain_grad = jnp.sum(grad_h2 * first_sum * rms_two, axis=0)
    grad_one = grad_two + norm_back(grad_h2, first_sum, rms_two, ffn_gain)
    grad_one_b = grad_one.astype(jnp.bfloat16)
    out_grad_full = contract_rows(mixed_b, grad_one_b)
    grad_mixed_b = contract_cols(grad_one_b, back_out).astype(jnp.bfloat16)
    grad_mixed_four = grad_mixed_b.reshape(tok_rows, KVH, group_size, HD)
    probs_again = soft_weights(query_four, key_rows, allowed, score_scale)
    probs_again_b = probs_again.astype(jnp.bfloat16)
    grad_probs = jnp.einsum(
        "qkgd,nkd->kgqn", grad_mixed_four, value_rows, preferred_element_type=jnp.float32
    )
    row_delta = jnp.sum(probs_again * grad_probs, axis=-1, keepdims=True)
    grad_scores_b = (probs_again * (grad_probs - row_delta)).astype(jnp.bfloat16)
    grad_query_rot = (
        jnp.einsum("kgqn,nkd->qkgd", grad_scores_b, key_rows, preferred_element_type=jnp.float32)
        * score_scale
    )
    grad_keys = (
        jnp.einsum("kgqn,qkgd->nkd", grad_scores_b, query_four, preferred_element_type=jnp.float32)
        * score_scale
    )
    grad_values = jnp.einsum(
        "kgqn,qkgd->nkd", probs_again_b, grad_mixed_four, preferred_element_type=jnp.float32
    )
    local_keys = grad_keys[reach * tok_rows :]
    local_values = grad_values[reach * tok_rows :]
    for distance in range(1, reach + 1):
        first_row = (reach - distance) * tok_rows
        back_keys, back_values = (
            passed_along(
                grad_keys[first_row : first_row + tok_rows].astype(jnp.bfloat16), "fsdp", -distance
            ).astype(jnp.float32),
            passed_along(
                grad_values[first_row : first_row + tok_rows].astype(jnp.bfloat16),
                "fsdp",
                -distance,
            ).astype(jnp.float32),
        )
        local_keys = local_keys + back_keys
        local_values = local_values + back_values
    grad_query_norm = rotate_back(grad_query_rot.reshape(tok_rows, HQ, HD), cosine, sine)
    query_gain_grad = jnp.sum(grad_query_norm * query * rms_query, axis=(0, 1))
    grad_query = norm_back(grad_query_norm, query, rms_query, query_gain)
    grad_key_norm = rotate_back(local_keys, cosine, sine)
    key_gain_grad = jnp.sum(grad_key_norm * key_raw * rms_key, axis=(0, 1))
    grad_key = norm_back(grad_key_norm, key_raw, rms_key, key_gain)
    grad_projected = jnp.concatenate(
        [
            grad_query.reshape(tok_rows, query_width),
            grad_key.reshape(tok_rows, kv_width),
            local_values.reshape(tok_rows, kv_width),
        ],
        axis=1,
    ).astype(jnp.bfloat16)
    qkv_grad_full = contract_rows(normed_b, grad_projected)
    grad_normed = contract_cols(grad_projected, back_qkv)
    attn_gain_grad = jnp.sum(grad_normed * tokens_f * rms_one, axis=0)
    input_grad = (grad_one + norm_back(grad_normed, tokens_f, rms_one, attn_gain)).astype(
        jnp.bfloat16
    )
    gains_grad_full = jnp.concatenate(
        [attn_gain_grad, ffn_gain_grad, query_gain_grad, key_gain_grad]
    )
    qkv_grad, out_grad, side_grad = (
        lax.psum_scatter(
            full.astype(jnp.bfloat16), "fsdp", scatter_dimension=0, tiled=True
        ).astype(jnp.float32)
        for full in (qkv_grad_full, out_grad_full, side_grad_full)
    )
    gains_grad = lax.psum_scatter(gains_grad_full, "fsdp", scatter_dimension=0, tiled=True)
    return (output, input_grad, per_layer_grad, qkv_grad, out_grad, ffn_grad, side_grad, gains_grad)


def solution(mesh):
    return jax.shard_map(
        local,
        mesh=mesh,
        in_specs=(
            P("fsdp", None),
            P("fsdp", None),
            P("fsdp", None),
            P(),
            P(),
            P("fsdp", None),
            P("fsdp", None),
            P("fsdp", None, None),
            P("fsdp", None),
            P("fsdp"),
        ),
        out_specs=(
            P("fsdp", None),
            P("fsdp", None),
            P("fsdp", None),
            P("fsdp", None),
            P("fsdp", None),
            P("fsdp", None, None),
            P("fsdp", None),
            P("fsdp"),
        ),
        check_vma=False,
    )
```

```python
import functools

import jax
import jax.numpy as jnp
from jax import lax
from jax.experimental import pallas as pl
from jax.experimental.pallas import tpu as pltpu
from jax.sharding import PartitionSpec as P

D = 2048
HQ = 8
KVH = 2
HD = 256
PL = 256
RANK = 64
WINDOW = 512


EPSILON = 1e-06
NEGATIVE = -1e30
ROPE_BASE = 10000.0


PLANE = 8
LANES = 128
MESH = pl.DeviceIdType.MESH
BF16 = jnp.bfloat16
F32 = jnp.float32


def flipped(index, bit):
    return index + bit - 2 * bit * lax.rem(lax.div(index, bit), 2)


def swapped(block, bit):
    route = [(i, i ^ bit) for i in range(lax.axis_size("fsdp"))]
    return lax.ppermute(block, "fsdp", route)


def weight_bits(count):
    return [8] + [1 << i for i in range(5, count.bit_length() - 1)] + [1]


def greet(partners):
    barrier = pltpu.get_barrier_semaphore()
    for partner in partners:
        pl.semaphore_signal(barrier, inc=1, device_id=(partner,), device_id_type=MESH)
    pl.semaphore_wait(barrier, len(partners))


def remote(src, dst, send, recv, device):
    return pltpu.make_async_remote_copy(
        src_ref=src,
        dst_ref=dst,
        send_sem=send,
        recv_sem=recv,
        device_id=(device,),
        device_id_type=MESH,
    )


def half_split(width):
    return (width // LANES + 1) // 2 * LANES


def gather_kernel(chain, own_a, own_b, out_a, out_b, *sems):
    me = lax.axis_index("fsdp")
    core, x_at, y_at = lax.rem(me, 2), lax.rem(lax.div(me, 2), 2), lax.rem(lax.div(me, 4), 2)
    z_at = lax.div(me, PLANE)
    next_x, next_y, next_c = flipped(me, 2), flipped(me, 4), flipped(me, 1)
    z_peers = [me + (lax.rem(z_at + s, chain) - z_at) * PLANE for s in range(1, chain)]
    greet([next_x, next_y, next_c] + z_peers)
    waves = []
    for own, out, (local, zs, zr, xs, xr, ys, yr, a_s, ar, bs, br, cs, cr) in (
        (own_a, out_a, sems[:13]),
        (own_b, out_b, sems[13:]),
    ):
        cut = half_split(own.shape[-1])
        ops = {"own": pltpu.make_async_copy(own, out.at[z_at, y_at, x_at, core], local)}
        ops["z"] = [
            remote(own, out.at[z_at, y_at, x_at, core], zs.at[s], zr.at[s], z_peers[s - 1])
            for s in range(1, chain)
        ]
        steps = []
        for s in range(chain):
            k = lax.rem(z_at + chain - s, chain)
            here = out.at[k, y_at, x_at, core]
            src = own if s == 0 else here
            from_x = out.at[k, y_at, 1 - x_at, core]
            from_y = out.at[k, 1 - y_at, x_at, core]
            left, right = pl.ds(0, cut), pl.ds(cut, own.shape[-1] - cut)
            steps.append(
                {
                    "x": remote(src, here, xs.at[s], xr.at[s], next_x),
                    "y": remote(src, here, ys.at[s], yr.at[s], next_y),
                    "a": remote(
                        from_x.at[:, left], from_x.at[:, left], a_s.at[s], ar.at[s], next_y
                    ),
                    "b": remote(
                        from_y.at[:, right], from_y.at[:, right], bs.at[s], br.at[s], next_x
                    ),
                    "c": remote(
                        out.at[k, :, :, core], out.at[k, :, :, core], cs.at[s], cr.at[s], next_c
                    ),
                }
            )
        ops["steps"] = steps
        waves.append(ops)
    flat = [(w, s) for w in range(2) for s in range(chain)]

    def spread(w, s):
        ops = waves[w]
        if s == 0:
            for copy in [ops["own"]] + ops["z"]:
                copy.start()
        else:
            ops["z"][s - 1].wait_recv()
        ops["steps"][s]["x"].start()
        ops["steps"][s]["y"].start()

    def pass_on(w, s):
        step = waves[w]["steps"][s]
        step["x"].wait_recv()
        step["a"].start()
        step["y"].wait_recv()
        step["b"].start()

    def across(w, s):
        step = waves[w]["steps"][s]
        step["a"].wait_recv()
        step["b"].wait_recv()
        if s == 0:
            waves[w]["own"].wait()
        step["c"].start()

    for i in range(len(flat) + 2):
        if i < len(flat):
            spread(*flat[i])
        if 1 <= i <= len(flat):
            pass_on(*flat[i - 1])
        if i >= 2:
            across(*flat[i - 2])
    for ops in waves:
        for copy in ops["z"]:
            copy.wait_send()
        for step in ops["steps"]:
            for name in "xyab":
                step[name].wait_send()
            step["c"].wait()


def gather_weights(own_a, own_b):
    count = lax.axis_size("fsdp")
    chain = count // PLANE
    dma = pltpu.SemaphoreType.DMA
    sems = [dma] + [dma((chain,))] * 12
    outs = [
        jax.ShapeDtypeStruct((chain, 2, 2, 2) + own.shape, own.dtype) for own in (own_a, own_b)
    ]
    moved = sum(o.size * 2 for o in outs)
    full_a, full_b = pl.pallas_call(
        functools.partial(gather_kernel, chain),
        out_shape=outs,
        in_specs=[pl.BlockSpec(memory_space=pl.ANY)] * 2,
        out_specs=[pl.BlockSpec(memory_space=pl.ANY)] * 2,
        scratch_shapes=sems * 2,
        compiler_params=pltpu.CompilerParams(collective_id=0, has_side_effects=True),
        cost_estimate=pl.CostEstimate(flops=0, bytes_accessed=moved * 16, transcendentals=0),
        name="gather_weights",
    )(own_a, own_b)
    return (full_a.reshape(-1, own_a.shape[1]), full_b.reshape(-1, own_b.shape[1]))


def add_into(target, *terms):
    rows = target.shape[0]
    tile = 16

    @pl.loop(0, rows // tile)
    def _(i):
        at = pl.ds(pl.multiple_of(i * tile, tile), tile)
        total = target[at].astype(F32)
        for term in terms:
            total = total + term[at].astype(F32)
        target[at] = total.astype(target.dtype)


def scatter_kernel(chain, part_a, part_b, out_a, out_b, *scratch):
    me = lax.axis_index("fsdp")
    core, x_at, y_at = lax.rem(me, 2), lax.rem(lax.div(me, 2), 2), lax.rem(lax.div(me, 4), 2)
    z_at = lax.div(me, PLANE)
    next_x, next_y, next_c = flipped(me, 2), flipped(me, 4), flipped(me, 1)
    z_peers = [me + (lax.rem(z_at + s, chain) - z_at) * PLANE for s in range(1, chain)]
    greet([next_x, next_y, next_c] + z_peers)
    waves = []
    half = len(scratch) // 2
    for part, out, held in ((part_a, out_a, scratch[:half]), (part_b, out_b, scratch[half:])):
        mine, sibling, in_a, in_b, in_x, in_y, in_z = held[:7]
        local, cs, cr, a_s, ar, bs, br, xs, xr, ys, yr, zs, zr = held[7:]
        width = out.shape[-1]
        cut = half_split(width)
        left, right = pl.ds(0, cut), pl.ds(cut, width - cut)
        steps = []
        for s in range(chain):
            k = lax.rem(z_at + s, chain)
            step = {
                "left": left,
                "right": right,
                "mine": mine.at[s],
                "sibling": sibling.at[s],
                "in_a": in_a.at[s],
                "in_b": in_b.at[s],
                "in_x": in_x.at[s],
                "in_y": in_y.at[s],
                "here": mine.at[s, y_at, x_at],
                "to_x": mine.at[s, y_at, 1 - x_at],
                "to_y": mine.at[s, 1 - y_at, x_at],
                "local": pltpu.make_async_copy(part.at[k, :, :, core], mine.at[s], local.at[s]),
                "c": remote(
                    part.at[k, :, :, 1 - core], sibling.at[s], cs.at[s], cr.at[s], next_c
                ),
                "a": remote(
                    mine.at[s, 1 - y_at, 1 - x_at, :, left],
                    in_a.at[s],
                    a_s.at[s],
                    ar.at[s],
                    next_x,
                ),
                "b": remote(
                    mine.at[s, 1 - y_at, 1 - x_at, :, right],
                    in_b.at[s],
                    bs.at[s],
                    br.at[s],
                    next_y,
                ),
            }
            step["x"] = remote(step["to_x"], step["in_x"], xs.at[s], xr.at[s], next_x)
            step["y"] = remote(step["to_y"], step["in_y"], ys.at[s], yr.at[s], next_y)
            if s > 0:
                step["z"] = remote(
                    step["here"], in_z.at[s - 1], zs.at[s - 1], zr.at[s - 1], z_peers[s - 1]
                )
            steps.append(step)
        waves.append((steps, in_z, out))
    order = [s for s in range(1, chain)] + [0]
    flat = [waves[w][0][s] for w in range(2) for s in order]

    def halve(step):
        step["local"].wait()
        step["c"].wait_recv()
        for j in range(4):
            add_into(step["mine"].at[j // 2, j % 2], step["sibling"].at[j // 2, j % 2])
        step["a"].start()
        step["b"].start()

    def sideways(step):
        step["a"].wait_recv()
        add_into(step["to_y"].at[:, step["left"]], step["in_a"])
        step["y"].start()
        step["b"].wait_recv()
        add_into(step["to_x"].at[:, step["right"]], step["in_b"])
        step["x"].start()

    def finish(step):
        step["x"].wait_recv()
        step["y"].wait_recv()
        add_into(step["here"], step["in_x"], step["in_y"])
        if "z" in step:
            step["z"].start()

    for step in flat:
        step["local"].start()
        step["c"].start()
    for i in range(len(flat) + 2):
        if i < len(flat):
            halve(flat[i])
        if 1 <= i <= len(flat):
            sideways(flat[i - 1])
        if i >= 2:
            finish(flat[i - 2])
    for steps, in_z, out in waves:
        for step in steps[1:]:
            step["z"].wait_recv()
        rows = out.shape[0]

        @pl.loop(0, rows // 16)
        def _(i):
            at = pl.ds(pl.multiple_of(i * 16, 16), 16)
            total = steps[0]["here"][at].astype(F32)
            for s in range(chain - 1):
                total = total + in_z[s, at].astype(F32)
            out[at] = total

    for step in flat:
        for name in "cabxyz":
            if name in step:
                step[name].wait_send()


def scatter_weights(part_a, part_b):
    count = lax.axis_size("fsdp")
    chain = count // PLANE
    dma = pltpu.SemaphoreType.DMA
    scratch, outs, parts = [], [], []
    for part in (part_a, part_b):
        rows, width = part.shape[0] // count, part.shape[1]
        cut = half_split(width)
        shapes = [
            (chain, 2, 2, rows, width),
            (chain, 2, 2, rows, width),
            (chain, rows, cut),
            (chain, rows, width - cut),
            (chain, rows, width),
            (chain, rows, width),
            (chain - 1, rows, width),
        ]
        scratch += [pltpu.VMEM(shape, BF16) for shape in shapes] + [dma((chain,))] * 13
        outs.append(jax.ShapeDtypeStruct((rows, width), F32))
        parts.append(part.reshape(chain, 2, 2, 2, rows, width))
    return pl.pallas_call(
        functools.partial(scatter_kernel, chain),
        out_shape=outs,
        in_specs=[pl.BlockSpec(memory_space=pl.ANY)] * 2,
        out_specs=[pl.BlockSpec(memory_space=pltpu.VMEM)] * 2,
        scratch_shapes=scratch,
        compiler_params=pltpu.CompilerParams(
            collective_id=1, has_side_effects=True, vmem_limit_bytes=56 * 2**20
        ),
        name="scatter_weights",
    )(*parts)


TOKEN_BITS = (2, 4, 16)


def token_gather_kernel(own, out, local, ss, rs):
    me = lax.axis_index("fsdp")
    next_x, next_y, next_z = (flipped(me, bit) for bit in TOKEN_BITS)
    greet([next_x, next_y, next_z])
    half = own.shape[0] // 2
    top, low = pl.ds(0, half), pl.ds(half, half)
    keep = pltpu.make_async_copy(own, out.at[0], local)
    copies = [
        remote(own, out.at[4], ss.at[0], rs.at[0], next_z),
        remote(own, out.at[1], ss.at[1], rs.at[1], next_x),
        remote(own, out.at[2], ss.at[2], rs.at[2], next_y),
        remote(out.at[1, top], out.at[3, top], ss.at[3], rs.at[3], next_y),
        remote(out.at[2, low], out.at[3, low], ss.at[4], rs.at[4], next_x),
        remote(out.at[4], out.at[5], ss.at[5], rs.at[5], next_x),
        remote(out.at[4], out.at[6], ss.at[6], rs.at[6], next_y),
        remote(out.at[5, top], out.at[7, top], ss.at[7], rs.at[7], next_y),
        remote(out.at[6, low], out.at[7, low], ss.at[8], rs.at[8], next_x),
    ]
    keep.start()
    for i, after in enumerate((None, None, None, 1, 2, 0, None, 5, 6)):
        if after is not None:
            copies[after].wait_recv()
        copies[i].start()
    for i in (3, 4, 7, 8):
        copies[i].wait_recv()
    for copy in copies:
        copy.wait_send()
    keep.wait()


def gather_tokens(own, collective_id):
    dma = pltpu.SemaphoreType.DMA
    return pl.pallas_call(
        token_gather_kernel,
        out_shape=jax.ShapeDtypeStruct((8,) + own.shape, own.dtype),
        in_specs=[pl.BlockSpec(memory_space=pl.ANY)],
        out_specs=pl.BlockSpec(memory_space=pl.ANY),
        scratch_shapes=[dma, dma((9,)), dma((9,))],
        compiler_params=pltpu.CompilerParams(collective_id=collective_id, has_side_effects=True),
        name="gather_tokens",
    )(own).reshape(8 * own.shape[0], own.shape[1])


def token_scatter_kernel(part, out, mine, in_half, in_x, in_y, in_z, local, ss, rs):
    me = lax.axis_index("fsdp")
    next_x, next_y, next_z = (flipped(me, bit) for bit in TOKEN_BITS)
    greet([next_x, next_y, next_z])
    half = out.shape[0] // 2
    top, low = pl.ds(0, half), pl.ds(half, half)
    loads = [pltpu.make_async_copy(part.at[j], mine.at[j], local.at[j]) for j in range(8)]
    order = (7, 5, 6, 4, 3, 1, 2, 0)
    for j in order:
        loads[j].start()
    waves = []
    for w, base in enumerate((4, 0)):
        waves.append(
            {
                "a": remote(
                    mine.at[base + 3, top], in_half.at[w, 0], ss.at[w, 0], rs.at[w, 0], next_x
                ),
                "b": remote(
                    mine.at[base + 3, low], in_half.at[w, 1], ss.at[w, 1], rs.at[w, 1], next_y
                ),
                "x": remote(mine.at[base + 1], in_x.at[w], ss.at[w, 2], rs.at[w, 2], next_x),
                "y": remote(mine.at[base + 2], in_y.at[w], ss.at[w, 3], rs.at[w, 3], next_y),
            }
        )
    across = remote(mine.at[4], in_z, ss.at[0, 4], rs.at[0, 4], next_z)
    for w, base in enumerate((4, 0)):
        loads[base + 3].wait()
        waves[w]["a"].start()
        waves[w]["b"].start()
    for w, base in enumerate((4, 0)):
        loads[base + 2].wait()
        waves[w]["a"].wait_recv()
        add_into(mine.at[base + 2, top], in_half.at[w, 0])
        waves[w]["y"].start()
        loads[base + 1].wait()
        waves[w]["b"].wait_recv()
        add_into(mine.at[base + 1, low], in_half.at[w, 1])
        waves[w]["x"].start()
        loads[base].wait()
        if w == 0:
            continue
        waves[0]["x"].wait_recv()
        waves[0]["y"].wait_recv()
        add_into(mine.at[4], in_x.at[0], in_y.at[0])
        across.start()
    waves[1]["x"].wait_recv()
    waves[1]["y"].wait_recv()
    across.wait_recv()

    @pl.loop(0, out.shape[0] // 16)
    def _(i):
        at = pl.ds(pl.multiple_of(i * 16, 16), 16)
        out[at] = (
            mine[0, at].astype(F32)
            + in_x[1, at].astype(F32)
            + in_y[1, at].astype(F32)
            + in_z[at].astype(F32)
        )

    for wave in waves:
        for copy in wave.values():
            copy.wait_send()
    across.wait_send()


def scatter_tokens(part, collective_id):
    rows, width = part.shape[0] // 8, part.shape[1]
    dma = pltpu.SemaphoreType.DMA
    return pl.pallas_call(
        token_scatter_kernel,
        out_shape=jax.ShapeDtypeStruct((rows, width), F32),
        in_specs=[pl.BlockSpec(memory_space=pl.ANY)],
        out_specs=pl.BlockSpec(memory_space=pltpu.VMEM),
        scratch_shapes=[
            pltpu.VMEM((8, rows, width), BF16),
            pltpu.VMEM((2, 2, rows // 2, width), BF16),
            pltpu.VMEM((2, rows, width), BF16),
            pltpu.VMEM((2, rows, width), BF16),
            pltpu.VMEM((rows, width), BF16),
            dma((8,)),
            dma((2, 5)),
            dma((2, 5)),
        ],
        compiler_params=pltpu.CompilerParams(
            collective_id=collective_id, has_side_effects=True, vmem_limit_bytes=40 * 2**20
        ),
        name="scatter_tokens",
    )(part.reshape(8, rows, width))


def passed_along(block, axis, distance):
    devices = range(lax.axis_size(axis))
    route = [(i - distance, i) for i in devices if i - distance in devices]
    return lax.ppermute(block, axis, route)


def inv_rms(field):
    return lax.rsqrt(jnp.mean(field * field, axis=-1, keepdims=True) + EPSILON)


def gelu_tanh(field):
    return jax.nn.gelu(field, approximate=True)


def layout(seq_lengths, seq_order, token_index):
    slot_ids = jnp.arange(seq_lengths.shape[0], dtype=jnp.int32)
    packed = jnp.sum(
        jnp.where(seq_order[:, None] == slot_ids[None, :], seq_lengths[None, :], 0), axis=1
    )
    starts = jnp.sum(jnp.where(slot_ids[None, :] < slot_ids[:, None], packed[None, :], 0), axis=1)
    segment = jnp.sum((token_index[:, None] >= starts[None, :]).astype(jnp.int32), axis=1) - 1
    offset = jnp.max(jnp.where(starts[None, :] <= token_index[:, None], starts[None, :], 0), axis=1)
    return (segment, token_index - offset)


def angles(position):
    half_width = HD // 2
    freq = ROPE_BASE ** (-2.0 * jnp.arange(half_width, dtype=jnp.float32) / HD)
    phase = position.astype(jnp.float32)[:, None] * freq[None, :]
    phase = jnp.concatenate([phase, phase], axis=-1)
    return (jnp.cos(phase)[:, None, :], jnp.sin(phase)[:, None, :])


def rotate(field, cosine, sine):
    half_width = field.shape[-1] // 2
    turned = jnp.concatenate([-field[..., half_width:], field[..., :half_width]], axis=-1)
    return field * cosine + turned * sine


def rotate_back(grad_in, cosine, sine):
    half_width = grad_in.shape[-1] // 2
    shifted = grad_in * sine
    return grad_in * cosine + jnp.concatenate(
        [shifted[..., half_width:], -shifted[..., :half_width]], axis=-1
    )


def norm_back(grad_out, field, scale_inv, gain):
    weighted = grad_out * gain
    return scale_inv * weighted - field * scale_inv**3 * jnp.mean(
        weighted * field, axis=-1, keepdims=True
    )


def contract_rows(left_op, right_op):
    return lax.dot_general(
        left_op, right_op, (((0,), (0,)), ((), ())), preferred_element_type=jnp.float32
    )


def contract_cols(left_op, right_op):
    return lax.dot_general(
        left_op, right_op, (((1,), (1,)), ((), ())), preferred_element_type=jnp.float32
    )


def split_gains(gain_all):
    gain_f = gain_all.astype(jnp.float32)
    return (gain_f[:D], gain_f[D : 2 * D], gain_f[2 * D : 2 * D + HD], gain_f[2 * D + HD :])


def soft_weights(query_four, key_rows, allowed, score_scale):
    scores = (
        jnp.einsum("qkgd,nkd->kgqn", query_four, key_rows, preferred_element_type=jnp.float32)
        * score_scale
    )
    scores = jnp.where(allowed[None, None], scores, NEGATIVE)
    highest = jnp.max(scores, axis=-1, keepdims=True)
    exponent = jnp.exp(scores - highest)
    return exponent / jnp.sum(exponent, axis=-1, keepdims=True)


def local(
    tokens,
    per_layer,
    cotangent,
    seq_lengths,
    seq_order,
    qkv_weight,
    out_weight,
    ffn_weights,
    side_weights,
    norm_gains,
):
    tok_rows = tokens.shape[0]
    my_index = lax.axis_index("fsdp")
    token_index = my_index * tok_rows + jnp.arange(tok_rows, dtype=jnp.int32)
    segment, position = layout(seq_lengths, seq_order, token_index)
    cosine, sine = angles(position)
    reach = (WINDOW + tok_rows - 2) // tok_rows
    key_index = jnp.concatenate(
        [token_index - distance * tok_rows for distance in range(reach, 0, -1)] + [token_index]
    )
    key_segment, unused_pos = layout(seq_lengths, seq_order, key_index)
    key_gap = token_index[:, None] - key_index[None, :]
    allowed = (segment[:, None] == key_segment[None, :]) & (key_gap >= 0) & (key_gap < WINDOW)
    score_scale = HD ** (-0.5)
    split_at = PL + RANK
    group_size = HQ // KVH
    query_width = HQ * HD
    kv_width = KVH * HD
    count = lax.axis_size("fsdp")
    bits = weight_bits(count)
    held = ffn_weights.transpose(1, 0, 2)
    for bit in bits:
        held = jnp.concatenate([held, swapped(held, bit)], axis=1)
    gate_w, up_w, down_w = held[0], held[1], held[2]
    weight_rows = qkv_weight.shape[0]
    gain_block = jnp.pad(norm_gains, (0, weight_rows * LANES - norm_gains.shape[0]))
    qkv_gathered, out_gathered = gather_weights(
        jnp.concatenate([qkv_weight, gain_block.reshape(weight_rows, LANES)], axis=1),
        jnp.concatenate([out_weight, side_weights], axis=1),
    )
    qkv_all = qkv_gathered[:, : qkv_weight.shape[1]]
    out_all, side_all = out_gathered[:, :D], out_gathered[:, D:]
    gain_all = (
        qkv_gathered[:, qkv_weight.shape[1] :]
        .reshape(count, weight_rows * LANES)[:, : norm_gains.shape[0]]
        .reshape(-1)
    )
    attn_gain, ffn_gain, query_gain, key_gain = split_gains(gain_all)
    tokens_f = tokens.astype(jnp.float32)
    rms_one = inv_rms(tokens_f)
    normed_b = (tokens_f * rms_one * attn_gain).astype(jnp.bfloat16)
    projected = jnp.dot(normed_b, qkv_all, preferred_element_type=jnp.float32)
    query = projected[:, :query_width].reshape(tok_rows, HQ, HD)
    key_raw = projected[:, query_width : query_width + kv_width].reshape(tok_rows, KVH, HD)
    value_raw = projected[:, query_width + kv_width :].reshape(tok_rows, KVH, HD)
    rms_query = inv_rms(query)
    rms_key = inv_rms(key_raw)
    query_b = rotate(query * rms_query * query_gain, cosine, sine).astype(jnp.bfloat16)
    key_b = rotate(key_raw * rms_key * key_gain, cosine, sine).astype(jnp.bfloat16)
    value_b = value_raw.astype(jnp.bfloat16)
    key_parts = []
    value_parts = []
    for distance in range(reach, 0, -1):
        moved_keys, moved_values = passed_along((key_b, value_b), "fsdp", distance)
        key_parts.append(moved_keys)
        value_parts.append(moved_values)
    key_rows = jnp.concatenate(key_parts + [key_b], axis=0)
    value_rows = jnp.concatenate(value_parts + [value_b], axis=0)
    query_four = query_b.reshape(tok_rows, KVH, group_size, HD)
    probs = soft_weights(query_four, key_rows, allowed, score_scale)
    probs_b = probs.astype(jnp.bfloat16)
    mixed = jnp.einsum("kgqn,nkd->qkgd", probs_b, value_rows, preferred_element_type=jnp.float32)
    mixed_b = mixed.reshape(tok_rows, query_width).astype(jnp.bfloat16)
    first_sum = tokens_f + jnp.dot(mixed_b, out_all, preferred_element_type=jnp.float32)
    rms_two = inv_rms(first_sum)
    normed_two = (first_sum * rms_two * ffn_gain).astype(jnp.bfloat16)
    normed_all = gather_tokens(normed_two, 2)
    gate_out = contract_cols(normed_all, gate_w)
    up_out = contract_cols(normed_all, up_w)
    gelu_gate, pull_gate = jax.vjp(gelu_tanh, gate_out)
    act_b = (gelu_gate * up_out).astype(jnp.bfloat16)
    ffn_part = jnp.dot(act_b, down_w, preferred_element_type=jnp.float32).astype(jnp.bfloat16)
    ffn_out = scatter_tokens(ffn_part, 3)
    second_sum = first_sum + ffn_out
    second_b = second_sum.astype(jnp.bfloat16)
    side_in = jnp.dot(second_b, side_all[:, :split_at], preferred_element_type=jnp.float32)
    per_f = per_layer.astype(jnp.float32)
    gelu_per, pull_per = jax.vjp(gelu_tanh, side_in[:, :PL])
    combined = jnp.concatenate(
        [(gelu_per * per_f).astype(jnp.bfloat16), side_in[:, PL:].astype(jnp.bfloat16)], axis=1
    )
    output = (second_sum + contract_cols(combined, side_all[:, split_at:])).astype(jnp.bfloat16)
    back_qkv, back_out, back_side = qkv_all, out_all, side_all
    grad_y = cotangent.astype(jnp.float32)
    grad_comb = jnp.dot(cotangent, back_side[:, split_at:], preferred_element_type=jnp.float32)
    side_out_grad = contract_rows(cotangent, combined)
    per_layer_grad = (grad_comb[:, :PL] * gelu_per).astype(jnp.bfloat16)
    grad_per = pull_per(grad_comb[:, :PL] * per_f)[0]
    grad_side = jnp.concatenate([grad_per, grad_comb[:, PL:]], axis=1).astype(jnp.bfloat16)
    side_in_grad = contract_rows(second_b, grad_side)
    side_grad_full = jnp.concatenate([side_in_grad, side_out_grad], axis=1)
    grad_two = grad_y + contract_cols(grad_side, back_side[:, :split_at])
    grad_two_b = grad_two.astype(jnp.bfloat16)
    grad_two_all = gather_tokens(grad_two_b, 4)
    grad_act_b = contract_cols(grad_two_all, down_w).astype(jnp.bfloat16)
    grad_gate_b = pull_gate(grad_act_b * up_out)[0].astype(jnp.bfloat16)
    grad_up_b = (grad_act_b * gelu_gate).astype(jnp.bfloat16)
    grad_h2 = jnp.dot(grad_gate_b, gate_w, preferred_element_type=jnp.float32)
    grad_h2 = grad_h2 + jnp.dot(grad_up_b, up_w, preferred_element_type=jnp.float32)
    grad_h2 = scatter_tokens(grad_h2.astype(BF16), 5)
    ffn_parts = []
    for left, right in (
        (grad_gate_b, normed_all),
        (grad_up_b, normed_all),
        (act_b, grad_two_all),
    ):
        part = contract_rows(left, right).astype(BF16)
        for bit in reversed(bits):
            half = part.shape[0] // 2
            part = (part[:half].astype(F32) + swapped(part[half:], bit).astype(F32)).astype(
                F32 if bit == bits[0] else BF16
            )
        ffn_parts.append(part)
    ffn_grad = jnp.stack(ffn_parts, axis=1)
    ffn_gain_grad = jnp.sum(grad_h2 * first_sum * rms_two, axis=0)
    grad_one = grad_two + norm_back(grad_h2, first_sum, rms_two, ffn_gain)
    grad_one_b = grad_one.astype(jnp.bfloat16)
    out_grad_full = contract_rows(mixed_b, grad_one_b)
    grad_mixed_b = contract_cols(grad_one_b, back_out).astype(jnp.bfloat16)
    grad_mixed_four = grad_mixed_b.reshape(tok_rows, KVH, group_size, HD)
    probs_again = soft_weights(query_four, key_rows, allowed, score_scale)
    probs_again_b = probs_again.astype(jnp.bfloat16)
    grad_probs = jnp.einsum(
        "qkgd,nkd->kgqn", grad_mixed_four, value_rows, preferred_element_type=jnp.float32
    )
    row_delta = jnp.sum(probs_again * grad_probs, axis=-1, keepdims=True)
    grad_scores_b = (probs_again * (grad_probs - row_delta)).astype(jnp.bfloat16)
    grad_query_rot = (
        jnp.einsum("kgqn,nkd->qkgd", grad_scores_b, key_rows, preferred_element_type=jnp.float32)
        * score_scale
    )
    grad_keys = (
        jnp.einsum("kgqn,qkgd->nkd", grad_scores_b, query_four, preferred_element_type=jnp.float32)
        * score_scale
    )
    grad_values = jnp.einsum(
        "kgqn,qkgd->nkd", probs_again_b, grad_mixed_four, preferred_element_type=jnp.float32
    )
    local_keys = grad_keys[reach * tok_rows :]
    local_values = grad_values[reach * tok_rows :]
    for distance in range(1, reach + 1):
        first_row = (reach - distance) * tok_rows
        back_keys, back_values = (
            passed_along(
                grad_keys[first_row : first_row + tok_rows].astype(jnp.bfloat16), "fsdp", -distance
            ).astype(jnp.float32),
            passed_along(
                grad_values[first_row : first_row + tok_rows].astype(jnp.bfloat16),
                "fsdp",
                -distance,
            ).astype(jnp.float32),
        )
        local_keys = local_keys + back_keys
        local_values = local_values + back_values
    grad_query_norm = rotate_back(grad_query_rot.reshape(tok_rows, HQ, HD), cosine, sine)
    query_gain_grad = jnp.sum(grad_query_norm * query * rms_query, axis=(0, 1))
    grad_query = norm_back(grad_query_norm, query, rms_query, query_gain)
    grad_key_norm = rotate_back(local_keys, cosine, sine)
    key_gain_grad = jnp.sum(grad_key_norm * key_raw * rms_key, axis=(0, 1))
    grad_key = norm_back(grad_key_norm, key_raw, rms_key, key_gain)
    grad_projected = jnp.concatenate(
        [
            grad_query.reshape(tok_rows, query_width),
            grad_key.reshape(tok_rows, kv_width),
            local_values.reshape(tok_rows, kv_width),
        ],
        axis=1,
    ).astype(jnp.bfloat16)
    qkv_grad_full = contract_rows(normed_b, grad_projected)
    grad_normed = contract_cols(grad_projected, back_qkv)
    attn_gain_grad = jnp.sum(grad_normed * tokens_f * rms_one, axis=0)
    input_grad = (grad_one + norm_back(grad_normed, tokens_f, rms_one, attn_gain)).astype(
        jnp.bfloat16
    )
    gains_grad_full = jnp.concatenate(
        [attn_gain_grad, ffn_gain_grad, query_gain_grad, key_gain_grad]
    )
    gain_rows = jnp.pad(
        gains_grad_full.astype(BF16).reshape(count, -1),
        ((0, 0), (0, weight_rows * LANES - norm_gains.shape[0])),
    ).reshape(count * weight_rows, LANES)
    qkv_sum, out_sum = scatter_weights(
        jnp.concatenate([qkv_grad_full.astype(BF16), gain_rows], axis=1),
        jnp.concatenate([out_grad_full.astype(BF16), side_grad_full.astype(BF16)], axis=1),
    )
    qkv_grad = qkv_sum[:, : qkv_weight.shape[1]]
    gains_grad = qkv_sum[:, qkv_weight.shape[1] :].reshape(-1)[: norm_gains.shape[0]]
    out_grad, side_grad = out_sum[:, :D], out_sum[:, D:]
    return (output, input_grad, per_layer_grad, qkv_grad, out_grad, ffn_grad, side_grad, gains_grad)


def solution(mesh):
    return jax.shard_map(
        local,
        mesh=mesh,
        in_specs=(
            P("fsdp", None),
            P("fsdp", None),
            P("fsdp", None),
            P(),
            P(),
            P("fsdp", None),
            P("fsdp", None),
            P("fsdp", None, None),
            P("fsdp", None),
            P("fsdp"),
        ),
        out_specs=(
            P("fsdp", None),
            P("fsdp", None),
            P("fsdp", None),
            P("fsdp", None),
            P("fsdp", None),
            P("fsdp", None, None),
            P("fsdp", None),
            P("fsdp"),
        ),
        check_vma=False,
    )
```

```python
import functools

import jax
import jax.numpy as jnp
from jax import lax
from jax.experimental import pallas as pl
from jax.experimental.pallas import tpu as pltpu
from jax.sharding import PartitionSpec as P

D = 2048
HQ = 8
KVH = 2
HD = 256
PL = 256
RANK = 64
WINDOW = 512


EPSILON = 1e-06
NEGATIVE = -1e30
ROPE_BASE = 10000.0


PLANE = 8
LANES = 128
MESH = pl.DeviceIdType.MESH
BF16 = jnp.bfloat16
F32 = jnp.float32


def flipped(index, bit):
    return index + bit - 2 * bit * lax.rem(lax.div(index, bit), 2)


def swapped(block, bit):
    route = [(i, i ^ bit) for i in range(lax.axis_size("fsdp"))]
    return lax.ppermute(block, "fsdp", route)


def weight_bits(count):
    return [8] + [1 << i for i in range(5, count.bit_length() - 1)] + [1]


def greet(partners):
    barrier = pltpu.get_barrier_semaphore()
    for partner in partners:
        pl.semaphore_signal(barrier, inc=1, device_id=(partner,), device_id_type=MESH)
    pl.semaphore_wait(barrier, len(partners))


def remote(src, dst, send, recv, device):
    return pltpu.make_async_remote_copy(
        src_ref=src,
        dst_ref=dst,
        send_sem=send,
        recv_sem=recv,
        device_id=(device,),
        device_id_type=MESH,
    )


def half_split(width):
    return (width // LANES + 1) // 2 * LANES


def gather_kernel(chain, own_a, own_b, out_a, out_b, *sems):
    me = lax.axis_index("fsdp")
    core, x_at, y_at = lax.rem(me, 2), lax.rem(lax.div(me, 2), 2), lax.rem(lax.div(me, 4), 2)
    z_at = lax.div(me, PLANE)
    next_x, next_y, next_c = flipped(me, 2), flipped(me, 4), flipped(me, 1)
    z_peers = [me + (lax.rem(z_at + s, chain) - z_at) * PLANE for s in range(1, chain)]
    greet([next_x, next_y, next_c] + z_peers)
    waves = []
    for own, out, (local, zs, zr, xs, xr, ys, yr, a_s, ar, bs, br, cs, cr) in (
        (own_a, out_a, sems[:13]),
        (own_b, out_b, sems[13:]),
    ):
        cut = half_split(own.shape[-1])
        ops = {"own": pltpu.make_async_copy(own, out.at[z_at, y_at, x_at, core], local)}
        ops["z"] = [
            remote(own, out.at[z_at, y_at, x_at, core], zs.at[s], zr.at[s], z_peers[s - 1])
            for s in range(1, chain)
        ]
        steps = []
        for s in range(chain):
            k = lax.rem(z_at + chain - s, chain)
            here = out.at[k, y_at, x_at, core]
            src = own if s == 0 else here
            from_x = out.at[k, y_at, 1 - x_at, core]
            from_y = out.at[k, 1 - y_at, x_at, core]
            left, right = pl.ds(0, cut), pl.ds(cut, own.shape[-1] - cut)
            steps.append(
                {
                    "x": remote(src, here, xs.at[s], xr.at[s], next_x),
                    "y": remote(src, here, ys.at[s], yr.at[s], next_y),
                    "a": remote(
                        from_x.at[:, left], from_x.at[:, left], a_s.at[s], ar.at[s], next_y
                    ),
                    "b": remote(
                        from_y.at[:, right], from_y.at[:, right], bs.at[s], br.at[s], next_x
                    ),
                    "c": remote(
                        out.at[k, :, :, core], out.at[k, :, :, core], cs.at[s], cr.at[s], next_c
                    ),
                }
            )
        ops["steps"] = steps
        waves.append(ops)
    flat = [(w, s) for w in range(2) for s in range(chain)]

    def spread(w, s):
        ops = waves[w]
        if s == 0:
            for copy in [ops["own"]] + ops["z"]:
                copy.start()
        else:
            ops["z"][s - 1].wait_recv()
        ops["steps"][s]["x"].start()
        ops["steps"][s]["y"].start()

    def pass_on(w, s):
        step = waves[w]["steps"][s]
        step["x"].wait_recv()
        step["a"].start()
        step["y"].wait_recv()
        step["b"].start()

    def across(w, s):
        step = waves[w]["steps"][s]
        step["a"].wait_recv()
        step["b"].wait_recv()
        if s == 0:
            waves[w]["own"].wait()
        step["c"].start()

    for i in range(len(flat) + 2):
        if i < len(flat):
            spread(*flat[i])
        if 1 <= i <= len(flat):
            pass_on(*flat[i - 1])
        if i >= 2:
            across(*flat[i - 2])
    for ops in waves:
        for copy in ops["z"]:
            copy.wait_send()
        for step in ops["steps"]:
            for name in "xyab":
                step[name].wait_send()
            step["c"].wait()


def gather_weights(own_a, own_b):
    count = lax.axis_size("fsdp")
    chain = count // PLANE
    dma = pltpu.SemaphoreType.DMA
    sems = [dma] + [dma((chain,))] * 12
    outs = [
        jax.ShapeDtypeStruct((chain, 2, 2, 2) + own.shape, own.dtype) for own in (own_a, own_b)
    ]
    moved = sum(o.size * 2 for o in outs)
    full_a, full_b = pl.pallas_call(
        functools.partial(gather_kernel, chain),
        out_shape=outs,
        in_specs=[pl.BlockSpec(memory_space=pl.ANY)] * 2,
        out_specs=[pl.BlockSpec(memory_space=pl.ANY)] * 2,
        scratch_shapes=sems * 2,
        compiler_params=pltpu.CompilerParams(collective_id=0, has_side_effects=True),
        cost_estimate=pl.CostEstimate(flops=0, bytes_accessed=moved * 16, transcendentals=0),
        name="gather_weights",
    )(own_a, own_b)
    return (full_a.reshape(-1, own_a.shape[1]), full_b.reshape(-1, own_b.shape[1]))


def add_into(target, *terms):
    rows = target.shape[0]
    tile = 16

    @pl.loop(0, rows // tile)
    def _(i):
        at = pl.ds(pl.multiple_of(i * tile, tile), tile)
        total = target[at].astype(F32)
        for term in terms:
            total = total + term[at].astype(F32)
        target[at] = total.astype(target.dtype)


def scatter_kernel(chain, part_a, part_b, out_a, out_b, *scratch):
    me = lax.axis_index("fsdp")
    core, x_at, y_at = lax.rem(me, 2), lax.rem(lax.div(me, 2), 2), lax.rem(lax.div(me, 4), 2)
    z_at = lax.div(me, PLANE)
    next_x, next_y, next_c = flipped(me, 2), flipped(me, 4), flipped(me, 1)
    z_peers = [me + (lax.rem(z_at + s, chain) - z_at) * PLANE for s in range(1, chain)]
    greet([next_x, next_y, next_c] + z_peers)
    waves = []
    half = len(scratch) // 2
    for part, out, held in ((part_a, out_a, scratch[:half]), (part_b, out_b, scratch[half:])):
        mine, sibling, in_a, in_b, in_x, in_y, in_z = held[:7]
        local, cs, cr, a_s, ar, bs, br, xs, xr, ys, yr, zs, zr = held[7:]
        width = out.shape[-1]
        cut = half_split(width)
        left, right = pl.ds(0, cut), pl.ds(cut, width - cut)
        steps = []
        for s in range(chain):
            k = lax.rem(z_at + s, chain)
            step = {
                "left": left,
                "right": right,
                "mine": mine.at[s],
                "sibling": sibling.at[s],
                "in_a": in_a.at[s],
                "in_b": in_b.at[s],
                "in_x": in_x.at[s],
                "in_y": in_y.at[s],
                "here": mine.at[s, y_at, x_at],
                "to_x": mine.at[s, y_at, 1 - x_at],
                "to_y": mine.at[s, 1 - y_at, x_at],
                "local": pltpu.make_async_copy(part.at[k, :, :, core], mine.at[s], local.at[s]),
                "c": remote(
                    part.at[k, :, :, 1 - core], sibling.at[s], cs.at[s], cr.at[s], next_c
                ),
                "a": remote(
                    mine.at[s, 1 - y_at, 1 - x_at, :, left],
                    in_a.at[s],
                    a_s.at[s],
                    ar.at[s],
                    next_x,
                ),
                "b": remote(
                    mine.at[s, 1 - y_at, 1 - x_at, :, right],
                    in_b.at[s],
                    bs.at[s],
                    br.at[s],
                    next_y,
                ),
            }
            step["x"] = remote(step["to_x"], step["in_x"], xs.at[s], xr.at[s], next_x)
            step["y"] = remote(step["to_y"], step["in_y"], ys.at[s], yr.at[s], next_y)
            if s > 0:
                step["z"] = remote(
                    step["here"], in_z.at[s - 1], zs.at[s - 1], zr.at[s - 1], z_peers[s - 1]
                )
            steps.append(step)
        waves.append((steps, in_z, out))
    order = [s for s in range(1, chain)] + [0]
    flat = [waves[w][0][s] for w in range(2) for s in order]

    def halve(step):
        step["local"].wait()
        step["c"].wait_recv()
        for j in range(4):
            add_into(step["mine"].at[j // 2, j % 2], step["sibling"].at[j // 2, j % 2])
        step["a"].start()
        step["b"].start()

    def sideways(step):
        step["a"].wait_recv()
        add_into(step["to_y"].at[:, step["left"]], step["in_a"])
        step["y"].start()
        step["b"].wait_recv()
        add_into(step["to_x"].at[:, step["right"]], step["in_b"])
        step["x"].start()

    def finish(step):
        step["x"].wait_recv()
        step["y"].wait_recv()
        add_into(step["here"], step["in_x"], step["in_y"])
        if "z" in step:
            step["z"].start()

    for step in flat:
        step["local"].start()
        step["c"].start()
    for i in range(len(flat) + 2):
        if i < len(flat):
            halve(flat[i])
        if 1 <= i <= len(flat):
            sideways(flat[i - 1])
        if i >= 2:
            finish(flat[i - 2])
    for steps, in_z, out in waves:
        for step in steps[1:]:
            step["z"].wait_recv()
        rows = out.shape[0]

        @pl.loop(0, rows // 16)
        def _(i):
            at = pl.ds(pl.multiple_of(i * 16, 16), 16)
            total = steps[0]["here"][at].astype(F32)
            for s in range(chain - 1):
                total = total + in_z[s, at].astype(F32)
            out[at] = total

    for step in flat:
        for name in "cabxyz":
            if name in step:
                step[name].wait_send()


def scatter_weights(part_a, part_b):
    count = lax.axis_size("fsdp")
    chain = count // PLANE
    dma = pltpu.SemaphoreType.DMA
    scratch, outs, parts = [], [], []
    for part in (part_a, part_b):
        rows, width = part.shape[0] // count, part.shape[1]
        cut = half_split(width)
        shapes = [
            (chain, 2, 2, rows, width),
            (chain, 2, 2, rows, width),
            (chain, rows, cut),
            (chain, rows, width - cut),
            (chain, rows, width),
            (chain, rows, width),
            (chain - 1, rows, width),
        ]
        scratch += [pltpu.VMEM(shape, BF16) for shape in shapes] + [dma((chain,))] * 13
        outs.append(jax.ShapeDtypeStruct((rows, width), F32))
        parts.append(part.reshape(chain, 2, 2, 2, rows, width))
    return pl.pallas_call(
        functools.partial(scatter_kernel, chain),
        out_shape=outs,
        in_specs=[pl.BlockSpec(memory_space=pl.ANY)] * 2,
        out_specs=[pl.BlockSpec(memory_space=pltpu.VMEM)] * 2,
        scratch_shapes=scratch,
        compiler_params=pltpu.CompilerParams(
            collective_id=1, has_side_effects=True, vmem_limit_bytes=56 * 2**20
        ),
        name="scatter_weights",
    )(*parts)


class TokenCube:
    def __init__(self, own, held, part, in_half, in_x, in_y, in_z, gs, gr, ss, sr):
        me = lax.axis_index("fsdp")
        next_x, next_y, next_z = (flipped(me, bit) for bit in TOKEN_BITS)
        self.partners = [next_x, next_y, next_z]
        half = own.shape[0] // 2
        top, low = pl.ds(0, half), pl.ds(half, half)
        self.top, self.low = top, low
        plan = {
            "zt": (own.at[top], held.at[4, top], next_z),
            "zl": (own.at[low], held.at[4, low], next_z),
            "x": (own, held.at[1], next_x),
            "y": (own, held.at[2], next_y),
            "dt": (held.at[1, top], held.at[3, top], next_y),
            "dl": (held.at[2, low], held.at[3, low], next_x),
            "xt": (held.at[4, top], held.at[5, top], next_x),
            "yt": (held.at[4, top], held.at[6, top], next_y),
            "xl": (held.at[4, low], held.at[5, low], next_x),
            "yl": (held.at[4, low], held.at[6, low], next_y),
            "et": (held.at[5, top], held.at[7, top], next_y),
            "el": (held.at[6, low], held.at[7, low], next_x),
        }
        self.gather = {
            name: remote(src, dst, gs.at[i], gr.at[i], device)
            for i, (name, (src, dst, device)) in enumerate(plan.items())
        }
        self.part, self.in_half, self.in_x, self.in_y, self.in_z = part, in_half, in_x, in_y, in_z
        self.waves = []
        for w, base in enumerate((4, 0)):
            self.waves.append(
                {
                    "a": remote(
                        part.at[base + 3, top], in_half.at[w, 0], ss.at[w, 0], sr.at[w, 0], next_x
                    ),
                    "b": remote(
                        part.at[base + 3, low], in_half.at[w, 1], ss.at[w, 1], sr.at[w, 1], next_y
                    ),
                    "x": remote(part.at[base + 1], in_x.at[w], ss.at[w, 2], sr.at[w, 2], next_x),
                    "y": remote(part.at[base + 2], in_y.at[w], ss.at[w, 3], sr.at[w, 3], next_y),
                }
            )
        self.waves[0]["z"] = remote(part.at[4], in_z, ss.at[0, 4], sr.at[0, 4], next_z)

    def start(self, *names):
        for name in names:
            self.gather[name].start()

    def arrive(self, *names):
        for name in names:
            self.gather[name].wait_recv()

    def corners(self, w):
        self.waves[w]["a"].start()
        self.waves[w]["b"].start()

    def sideways(self, w):
        base, wave = 4 - 4 * w, self.waves[w]
        wave["a"].wait_recv()
        add_into(self.part.at[base + 2, self.top], self.in_half.at[w, 0])
        wave["y"].start()
        wave["b"].wait_recv()
        add_into(self.part.at[base + 1, self.low], self.in_half.at[w, 1])
        wave["x"].start()

    def across(self):
        self.waves[0]["x"].wait_recv()
        self.waves[0]["y"].wait_recv()
        add_into(self.part.at[4], self.in_x.at[0], self.in_y.at[0])
        self.waves[0]["z"].start()

    def finish(self, out):
        self.waves[1]["x"].wait_recv()
        self.waves[1]["y"].wait_recv()
        self.waves[0]["z"].wait_recv()

        @pl.loop(0, out.shape[0] // 16)
        def _(i):
            at = pl.ds(pl.multiple_of(i * 16, 16), 16)
            out[at] = (
                self.part[0, at].astype(F32)
                + self.in_x[1, at].astype(F32)
                + self.in_y[1, at].astype(F32)
                + self.in_z[at].astype(F32)
            )

        for copy in self.gather.values():
            copy.wait_send()
        for wave in self.waves:
            for copy in wave.values():
                copy.wait_send()


TOKEN_BITS = (2, 4, 16)
ORDER = (0, 1, 2, 4, 5, 6, 7, 3)


def cube_scratch(rows, width):
    dma = pltpu.SemaphoreType.DMA
    return [
        pltpu.VMEM((8, rows, width), BF16),
        pltpu.VMEM((8, rows, width), BF16),
        pltpu.VMEM((2, 2, rows // 2, width), BF16),
        pltpu.VMEM((2, rows, width), BF16),
        pltpu.VMEM((2, rows, width), BF16),
        pltpu.VMEM((rows, width), BF16),
        dma((12,)),
        dma((12,)),
        dma((2, 5)),
        dma((2, 5)),
        dma,
    ]


def load_weights(blocks, held, sems):
    rows = blocks[0].shape[1]
    loads = []
    for m in (2, 0, 1):
        loads.append(
            [
                pltpu.make_async_copy(
                    block.at[m], held.at[m, pl.ds(i * rows, rows)], sems.at[m, i]
                )
                for i, block in enumerate(blocks)
            ]
        )
        for load in loads[-1]:
            load.start()
    return loads[1:] + loads[:1]


GELU_A = 0.7978845608028654
GELU_B = 0.044715


def tanh_inner(gate):
    return jnp.tanh(GELU_A * (gate + GELU_B * gate * gate * gate))


def dot_nt(left, right):
    return lax.dot_general(left, right, (((1,), (1,)), ((), ())), preferred_element_type=F32)


def dot_tn(left, right):
    return lax.dot_general(left, right, (((0,), (0,)), ((), ())), preferred_element_type=F32)


HIDDEN_TILE = 512
WIDTH_TILE = 1024


def ffn_forward_kernel(n_blocks, own, *refs):
    blocks = refs[:n_blocks]
    out, held_out, gate_out, up_out, weights, gate_st, up_st, act = refs[n_blocks : n_blocks + 8]
    load_sem, save_sem, keep_sem = refs[n_blocks + 8 : n_blocks + 11]
    held, part, in_half, in_x, in_y, in_z, gs, gr, ss, sr, own_sem = refs[n_blocks + 11 :]
    cube = TokenCube(own, held, part, in_half, in_x, in_y, in_z, gs, gr, ss, sr)
    greet(cube.partners)
    cube.start("zt", "zl", "x", "y")
    keep = pltpu.make_async_copy(own, held.at[0], own_sem)
    keep.start()
    loads = load_weights(blocks, weights, load_sem)
    hidden, width = weights.shape[1], weights.shape[2]
    saves = []

    def compute(step):
        j, slot = ORDER[step], step % 2
        if step >= 2:
            for save in saves[step - 2]:
                save.wait()

        @pl.loop(0, hidden // HIDDEN_TILE)
        def _(n):
            at = pl.ds(pl.multiple_of(n * HIDDEN_TILE, HIDDEN_TILE), HIDDEN_TILE)
            gate = dot_nt(held[j], weights[0, at])
            up = dot_nt(held[j], weights[1, at])
            gate_st[slot, :, at] = gate
            up_st[slot, :, at] = up
            act[:, at] = (0.5 * gate * (1.0 + tanh_inner(gate)) * up).astype(BF16)

        saves.append(
            [
                pltpu.make_async_copy(gate_st.at[slot], gate_out.at[j], save_sem.at[0, slot]),
                pltpu.make_async_copy(up_st.at[slot], up_out.at[j], save_sem.at[1, slot]),
            ]
        )
        for save in saves[step]:
            save.start()
        if step == 0:
            for load in loads[2]:
                load.wait()

        @pl.loop(0, width // WIDTH_TILE)
        def _(n):
            at = pl.ds(pl.multiple_of(n * WIDTH_TILE, WIDTH_TILE), WIDTH_TILE)
            part[j, :, at] = jnp.dot(
                act[...], weights[2, :, at], preferred_element_type=F32
            ).astype(BF16)

    keep.wait()
    for load in loads[0] + loads[1]:
        load.wait()
    compute(0)
    cube.arrive("x", "y", "zt")
    cube.start("xt", "yt")
    compute(1)
    compute(2)
    cube.arrive("zl")
    cube.start("xl", "yl")
    cube.arrive("xt")
    cube.start("et")
    compute(3)
    cube.arrive("xl", "yt", "yl")
    cube.start("el", "dt", "dl")
    compute(4)
    compute(5)
    cube.arrive("et", "el")
    compute(6)
    cube.corners(0)
    cube.arrive("dt", "dl")
    whole = pltpu.make_async_copy(held, held_out, keep_sem)
    whole.start()
    compute(7)
    cube.sideways(0)
    cube.corners(1)
    cube.sideways(1)
    cube.across()
    cube.finish(out)
    for save in saves[6] + saves[7]:
        save.wait()
    whole.wait()


def ffn_forward(own, blocks):
    rows, width = own.shape
    hidden = blocks[0].shape[1] * len(blocks)
    dma = pltpu.SemaphoreType.DMA
    anywhere = pl.BlockSpec(memory_space=pl.ANY)
    return pl.pallas_call(
        functools.partial(ffn_forward_kernel, len(blocks)),
        out_shape=[
            jax.ShapeDtypeStruct((rows, width), F32),
            jax.ShapeDtypeStruct((8, rows, width), BF16),
            jax.ShapeDtypeStruct((8, rows, hidden), F32),
            jax.ShapeDtypeStruct((8, rows, hidden), F32),
        ],
        in_specs=[anywhere] * (1 + len(blocks)),
        out_specs=[pl.BlockSpec(memory_space=pltpu.VMEM)] + [anywhere] * 3,
        scratch_shapes=[
            pltpu.VMEM((3, hidden, width), BF16),
            pltpu.VMEM((2, rows, hidden), F32),
            pltpu.VMEM((2, rows, hidden), F32),
            pltpu.VMEM((rows, hidden), BF16),
            dma((3, len(blocks))),
            dma((2, 2)),
            dma,
        ]
        + cube_scratch(rows, width),
        compiler_params=pltpu.CompilerParams(
            collective_id=2, has_side_effects=True, vmem_limit_bytes=58 * 2**20
        ),
        cost_estimate=pl.CostEstimate(
            flops=48 * rows * width * hidden, bytes_accessed=300 * 2**20, transcendentals=0
        ),
        name="ffn_forward",
    )(own, *blocks)


def ffn_backward_kernel(n_blocks, own, normed, gate_in, up_in, *refs):
    blocks = refs[:n_blocks]
    out, mine, theirs, weights, gate_st, up_st, grads, stage = refs[n_blocks : n_blocks + 8]
    load_sem, read_sem, write_sem, normed_sem = refs[n_blocks + 8 : n_blocks + 12]
    held, part, in_half, in_x, in_y, in_z, gs, gr, ss, sr, own_sem = refs[n_blocks + 12 :]
    cube = TokenCube(own, held, part, in_half, in_x, in_y, in_z, gs, gr, ss, sr)
    greet(cube.partners)
    cube.start("zt", "zl", "x", "y")
    keep = pltpu.make_async_copy(own, held.at[0], own_sem)
    keep.start()
    hidden, width = weights.shape[1], weights.shape[2]
    rows = own.shape[0]
    reads = []
    for step, j in enumerate(ORDER):
        slot = step % 2
        reads.append(
            [
                pltpu.make_async_copy(gate_in.at[j], gate_st.at[slot], read_sem.at[0, slot]),
                pltpu.make_async_copy(up_in.at[j], up_st.at[slot], read_sem.at[1, slot]),
            ]
        )
    for read in reads[0]:
        read.start()
    loads = load_weights(blocks, weights, load_sem)

    def compute(step):
        j, slot = ORDER[step], step % 2
        if step < 7:
            for read in reads[step + 1]:
                read.start()
        for read in reads[step]:
            read.wait()

        @pl.loop(0, hidden // HIDDEN_TILE)
        def _(n):
            at = pl.ds(pl.multiple_of(n * HIDDEN_TILE, HIDDEN_TILE), HIDDEN_TILE)
            grad_act = dot_nt(held[j], weights[2, at]).astype(BF16).astype(F32)
            gate, up = gate_st[slot, :, at], up_st[slot, :, at]
            inner = tanh_inner(gate)
            gelu = 0.5 * gate * (1.0 + inner)
            slope = 0.5 * (1.0 + inner) + 0.5 * gate * (1.0 - inner * inner) * GELU_A * (
                1.0 + 3.0 * GELU_B * gate * gate
            )
            token = pl.ds(j * rows, rows)
            grads[2, token, at] = (gelu * up).astype(BF16)
            grads[0, token, at] = (grad_act * up * slope).astype(BF16)
            grads[1, token, at] = (grad_act * gelu).astype(BF16)

        if step == 0:
            for load in loads[0] + loads[1]:
                load.wait()
        token = pl.ds(j * rows, rows)

        @pl.loop(0, width // WIDTH_TILE)
        def _(n):
            at = pl.ds(pl.multiple_of(n * WIDTH_TILE, WIDTH_TILE), WIDTH_TILE)
            part[j, :, at] = (
                jnp.dot(grads[0, token], weights[0, :, at], preferred_element_type=F32)
                + jnp.dot(grads[1, token], weights[1, :, at], preferred_element_type=F32)
            ).astype(BF16)

    keep.wait()
    for load in loads[2]:
        load.wait()
    compute(0)
    cube.arrive("x", "y", "zt")
    cube.start("xt", "yt")
    compute(1)
    compute(2)
    cube.arrive("zl")
    cube.start("xl", "yl")
    cube.arrive("xt")
    cube.start("et")
    compute(3)
    cube.arrive("xl", "yt", "yl")
    cube.start("el", "dt", "dl")
    compute(4)
    compute(5)
    cube.arrive("et", "el")
    compute(6)
    cube.corners(0)
    cube.arrive("dt", "dl")
    compute(7)
    cube.corners(1)
    tokens = 8 * rows
    refill = pltpu.make_async_copy(
        normed, weights.at[pl.ds(0, tokens // hidden)], normed_sem
    )
    refill.start()
    tile = stage.shape[1]
    half = hidden // 2
    jobs = [(m, i) for m in (2, 0, 1) for i in range(hidden // tile)]
    writes = []

    def weight_grad(count):
        for _ in range(count):
            index = len(writes)
            m, i = jobs[index]
            slot = index % 2
            if index >= 2:
                writes[index - 2].wait()
            if m == 0 and i == 0:
                refill.wait()
            first = (i * tile + half) % hidden

            @pl.loop(0, width // WIDTH_TILE)
            def _(n):
                at = pl.ds(pl.multiple_of(n * WIDTH_TILE, WIDTH_TILE), WIDTH_TILE)
                if m == 2:
                    right = held[:, :, at].reshape(tokens, WIDTH_TILE)
                else:
                    right = weights[: tokens // hidden, :, at].reshape(tokens, WIDTH_TILE)
                stage[slot, :, at] = dot_tn(
                    grads[m, :, pl.ds(first, tile)], right
                ).astype(BF16)

            target = theirs if first >= half else mine
            write = pltpu.make_async_copy(
                stage.at[slot], target.at[m, pl.ds(first % half, tile)], write_sem.at[slot]
            )
            write.start()
            writes.append(write)

    weight_grad(1)
    cube.sideways(0)
    weight_grad(1)
    cube.sideways(1)
    weight_grad(4)
    cube.across()
    weight_grad(len(jobs) - 6)
    cube.finish(out)
    writes[-2].wait()
    writes[-1].wait()


def ffn_backward(own, normed, gate, up, blocks):
    rows, width = own.shape
    hidden = blocks[0].shape[1] * len(blocks)
    dma = pltpu.SemaphoreType.DMA
    anywhere = pl.BlockSpec(memory_space=pl.ANY)
    grad = jax.ShapeDtypeStruct((3, hidden // 2, width), BF16)
    return pl.pallas_call(
        functools.partial(ffn_backward_kernel, len(blocks)),
        out_shape=[jax.ShapeDtypeStruct((rows, width), F32), grad, grad],
        in_specs=[anywhere] * (4 + len(blocks)),
        out_specs=[pl.BlockSpec(memory_space=pltpu.VMEM), anywhere, anywhere],
        scratch_shapes=[
            pltpu.VMEM((3, hidden, width), BF16),
            pltpu.VMEM((2, rows, hidden), F32),
            pltpu.VMEM((2, rows, hidden), F32),
            pltpu.VMEM((3, 8 * rows, hidden), BF16),
            pltpu.VMEM((2, 256, width), BF16),
            dma((3, len(blocks))),
            dma((2, 2)),
            dma((2,)),
            dma,
        ]
        + cube_scratch(rows, width),
        compiler_params=pltpu.CompilerParams(
            collective_id=3, has_side_effects=True, vmem_limit_bytes=62 * 2**20
        ),
        cost_estimate=pl.CostEstimate(
            flops=96 * rows * width * hidden, bytes_accessed=400 * 2**20, transcendentals=0
        ),
        name="ffn_backward",
    )(own, normed.reshape(8 * rows // hidden, hidden, width), gate, up, *blocks)


def passed_along(block, axis, distance):
    devices = range(lax.axis_size(axis))
    route = [(i - distance, i) for i in devices if i - distance in devices]
    return lax.ppermute(block, axis, route)


def inv_rms(field):
    return lax.rsqrt(jnp.mean(field * field, axis=-1, keepdims=True) + EPSILON)


def gelu_tanh(field):
    return jax.nn.gelu(field, approximate=True)


def layout(seq_lengths, seq_order, token_index):
    slot_ids = jnp.arange(seq_lengths.shape[0], dtype=jnp.int32)
    packed = jnp.sum(
        jnp.where(seq_order[:, None] == slot_ids[None, :], seq_lengths[None, :], 0), axis=1
    )
    starts = jnp.sum(jnp.where(slot_ids[None, :] < slot_ids[:, None], packed[None, :], 0), axis=1)
    segment = jnp.sum((token_index[:, None] >= starts[None, :]).astype(jnp.int32), axis=1) - 1
    offset = jnp.max(jnp.where(starts[None, :] <= token_index[:, None], starts[None, :], 0), axis=1)
    return (segment, token_index - offset)


def angles(position):
    half_width = HD // 2
    freq = ROPE_BASE ** (-2.0 * jnp.arange(half_width, dtype=jnp.float32) / HD)
    phase = position.astype(jnp.float32)[:, None] * freq[None, :]
    phase = jnp.concatenate([phase, phase], axis=-1)
    return (jnp.cos(phase)[:, None, :], jnp.sin(phase)[:, None, :])


def rotate(field, cosine, sine):
    half_width = field.shape[-1] // 2
    turned = jnp.concatenate([-field[..., half_width:], field[..., :half_width]], axis=-1)
    return field * cosine + turned * sine


def rotate_back(grad_in, cosine, sine):
    half_width = grad_in.shape[-1] // 2
    shifted = grad_in * sine
    return grad_in * cosine + jnp.concatenate(
        [shifted[..., half_width:], -shifted[..., :half_width]], axis=-1
    )


def norm_back(grad_out, field, scale_inv, gain):
    weighted = grad_out * gain
    return scale_inv * weighted - field * scale_inv**3 * jnp.mean(
        weighted * field, axis=-1, keepdims=True
    )


def contract_rows(left_op, right_op):
    return lax.dot_general(
        left_op, right_op, (((0,), (0,)), ((), ())), preferred_element_type=jnp.float32
    )


def contract_cols(left_op, right_op):
    return lax.dot_general(
        left_op, right_op, (((1,), (1,)), ((), ())), preferred_element_type=jnp.float32
    )


def split_gains(gain_all):
    gain_f = gain_all.astype(jnp.float32)
    return (gain_f[:D], gain_f[D : 2 * D], gain_f[2 * D : 2 * D + HD], gain_f[2 * D + HD :])


def soft_weights(query_four, key_rows, allowed, score_scale):
    scores = (
        jnp.einsum("qkgd,nkd->kgqn", query_four, key_rows, preferred_element_type=jnp.float32)
        * score_scale
    )
    scores = jnp.where(allowed[None, None], scores, NEGATIVE)
    highest = jnp.max(scores, axis=-1, keepdims=True)
    exponent = jnp.exp(scores - highest)
    return exponent / jnp.sum(exponent, axis=-1, keepdims=True)


def local(
    tokens,
    per_layer,
    cotangent,
    seq_lengths,
    seq_order,
    qkv_weight,
    out_weight,
    ffn_weights,
    side_weights,
    norm_gains,
):
    tok_rows = tokens.shape[0]
    my_index = lax.axis_index("fsdp")
    token_index = my_index * tok_rows + jnp.arange(tok_rows, dtype=jnp.int32)
    segment, position = layout(seq_lengths, seq_order, token_index)
    cosine, sine = angles(position)
    reach = (WINDOW + tok_rows - 2) // tok_rows
    key_index = jnp.concatenate(
        [token_index - distance * tok_rows for distance in range(reach, 0, -1)] + [token_index]
    )
    key_segment, unused_pos = layout(seq_lengths, seq_order, key_index)
    key_gap = token_index[:, None] - key_index[None, :]
    allowed = (segment[:, None] == key_segment[None, :]) & (key_gap >= 0) & (key_gap < WINDOW)
    score_scale = HD ** (-0.5)
    split_at = PL + RANK
    group_size = HQ // KVH
    query_width = HQ * HD
    kv_width = KVH * HD
    count = lax.axis_size("fsdp")
    bits = weight_bits(count)
    weight_rows = qkv_weight.shape[0]
    gain_block = jnp.pad(norm_gains, (0, weight_rows * LANES - norm_gains.shape[0]))
    qkv_gathered, out_gathered = gather_weights(
        jnp.concatenate([qkv_weight, gain_block.reshape(weight_rows, LANES)], axis=1),
        jnp.concatenate([out_weight, side_weights], axis=1),
    )
    ffn_own, qkv_gathered = lax.optimization_barrier((ffn_weights, qkv_gathered))
    ffn_blocks = [ffn_own.transpose(1, 0, 2)]
    for bit in bits:
        ffn_blocks += [swapped(block, bit) for block in ffn_blocks]
    qkv_all = qkv_gathered[:, : qkv_weight.shape[1]]
    out_all, side_all = out_gathered[:, :D], out_gathered[:, D:]
    gain_all = (
        qkv_gathered[:, qkv_weight.shape[1] :]
        .reshape(count, weight_rows * LANES)[:, : norm_gains.shape[0]]
        .reshape(-1)
    )
    attn_gain, ffn_gain, query_gain, key_gain = split_gains(gain_all)
    tokens_f = tokens.astype(jnp.float32)
    rms_one = inv_rms(tokens_f)
    normed_b = (tokens_f * rms_one * attn_gain).astype(jnp.bfloat16)
    projected = jnp.dot(normed_b, qkv_all, preferred_element_type=jnp.float32)
    query = projected[:, :query_width].reshape(tok_rows, HQ, HD)
    key_raw = projected[:, query_width : query_width + kv_width].reshape(tok_rows, KVH, HD)
    value_raw = projected[:, query_width + kv_width :].reshape(tok_rows, KVH, HD)
    rms_query = inv_rms(query)
    rms_key = inv_rms(key_raw)
    query_b = rotate(query * rms_query * query_gain, cosine, sine).astype(jnp.bfloat16)
    key_b = rotate(key_raw * rms_key * key_gain, cosine, sine).astype(jnp.bfloat16)
    value_b = value_raw.astype(jnp.bfloat16)
    key_parts = []
    value_parts = []
    for distance in range(reach, 0, -1):
        moved_keys, moved_values = passed_along((key_b, value_b), "fsdp", distance)
        key_parts.append(moved_keys)
        value_parts.append(moved_values)
    key_rows = jnp.concatenate(key_parts + [key_b], axis=0)
    value_rows = jnp.concatenate(value_parts + [value_b], axis=0)
    query_four = query_b.reshape(tok_rows, KVH, group_size, HD)
    probs = soft_weights(query_four, key_rows, allowed, score_scale)
    probs_b = probs.astype(jnp.bfloat16)
    mixed = jnp.einsum("kgqn,nkd->qkgd", probs_b, value_rows, preferred_element_type=jnp.float32)
    mixed_b = mixed.reshape(tok_rows, query_width).astype(jnp.bfloat16)
    first_sum = tokens_f + jnp.dot(mixed_b, out_all, preferred_element_type=jnp.float32)
    rms_two = inv_rms(first_sum)
    normed_two = (first_sum * rms_two * ffn_gain).astype(jnp.bfloat16)
    ffn_out, normed_all, gate_kept, up_kept = ffn_forward(normed_two, ffn_blocks)
    second_sum = first_sum + ffn_out
    second_b = second_sum.astype(jnp.bfloat16)
    side_in = jnp.dot(second_b, side_all[:, :split_at], preferred_element_type=jnp.float32)
    per_f = per_layer.astype(jnp.float32)
    gelu_per, pull_per = jax.vjp(gelu_tanh, side_in[:, :PL])
    combined = jnp.concatenate(
        [(gelu_per * per_f).astype(jnp.bfloat16), side_in[:, PL:].astype(jnp.bfloat16)], axis=1
    )
    output = (second_sum + contract_cols(combined, side_all[:, split_at:])).astype(jnp.bfloat16)
    back_qkv, back_out, back_side = qkv_all, out_all, side_all
    grad_y = cotangent.astype(jnp.float32)
    grad_comb = jnp.dot(cotangent, back_side[:, split_at:], preferred_element_type=jnp.float32)
    side_out_grad = contract_rows(cotangent, combined)
    per_layer_grad = (grad_comb[:, :PL] * gelu_per).astype(jnp.bfloat16)
    grad_per = pull_per(grad_comb[:, :PL] * per_f)[0]
    grad_side = jnp.concatenate([grad_per, grad_comb[:, PL:]], axis=1).astype(jnp.bfloat16)
    side_in_grad = contract_rows(second_b, grad_side)
    side_grad_full = jnp.concatenate([side_in_grad, side_out_grad], axis=1)
    grad_two = grad_y + contract_cols(grad_side, back_side[:, :split_at])
    grad_two_b = grad_two.astype(jnp.bfloat16)
    grad_h2, ffn_part, ffn_sent = ffn_backward(
        grad_two_b, normed_all, gate_kept, up_kept, ffn_blocks
    )
    for bit in reversed(bits):
        ffn_part = ffn_part.astype(F32) + swapped(ffn_sent, bit).astype(F32)
        if bit != bits[0]:
            half = ffn_part.shape[1] // 2
            ffn_sent = ffn_part[:, half:].astype(BF16)
            ffn_part = ffn_part[:, :half]
    ffn_grad = ffn_part.transpose(1, 0, 2)
    ffn_gain_grad = jnp.sum(grad_h2 * first_sum * rms_two, axis=0)
    grad_one = grad_two + norm_back(grad_h2, first_sum, rms_two, ffn_gain)
    grad_one_b = grad_one.astype(jnp.bfloat16)
    out_grad_full = contract_rows(mixed_b, grad_one_b)
    grad_mixed_b = contract_cols(grad_one_b, back_out).astype(jnp.bfloat16)
    grad_mixed_four = grad_mixed_b.reshape(tok_rows, KVH, group_size, HD)
    probs_again = soft_weights(query_four, key_rows, allowed, score_scale)
    probs_again_b = probs_again.astype(jnp.bfloat16)
    grad_probs = jnp.einsum(
        "qkgd,nkd->kgqn", grad_mixed_four, value_rows, preferred_element_type=jnp.float32
    )
    row_delta = jnp.sum(probs_again * grad_probs, axis=-1, keepdims=True)
    grad_scores_b = (probs_again * (grad_probs - row_delta)).astype(jnp.bfloat16)
    grad_query_rot = (
        jnp.einsum("kgqn,nkd->qkgd", grad_scores_b, key_rows, preferred_element_type=jnp.float32)
        * score_scale
    )
    grad_keys = (
        jnp.einsum("kgqn,qkgd->nkd", grad_scores_b, query_four, preferred_element_type=jnp.float32)
        * score_scale
    )
    grad_values = jnp.einsum(
        "kgqn,qkgd->nkd", probs_again_b, grad_mixed_four, preferred_element_type=jnp.float32
    )
    local_keys = grad_keys[reach * tok_rows :]
    local_values = grad_values[reach * tok_rows :]
    for distance in range(1, reach + 1):
        first_row = (reach - distance) * tok_rows
        back_keys, back_values = (
            passed_along(
                grad_keys[first_row : first_row + tok_rows].astype(jnp.bfloat16), "fsdp", -distance
            ).astype(jnp.float32),
            passed_along(
                grad_values[first_row : first_row + tok_rows].astype(jnp.bfloat16),
                "fsdp",
                -distance,
            ).astype(jnp.float32),
        )
        local_keys = local_keys + back_keys
        local_values = local_values + back_values
    grad_query_norm = rotate_back(grad_query_rot.reshape(tok_rows, HQ, HD), cosine, sine)
    query_gain_grad = jnp.sum(grad_query_norm * query * rms_query, axis=(0, 1))
    grad_query = norm_back(grad_query_norm, query, rms_query, query_gain)
    grad_key_norm = rotate_back(local_keys, cosine, sine)
    key_gain_grad = jnp.sum(grad_key_norm * key_raw * rms_key, axis=(0, 1))
    grad_key = norm_back(grad_key_norm, key_raw, rms_key, key_gain)
    grad_projected = jnp.concatenate(
        [
            grad_query.reshape(tok_rows, query_width),
            grad_key.reshape(tok_rows, kv_width),
            local_values.reshape(tok_rows, kv_width),
        ],
        axis=1,
    ).astype(jnp.bfloat16)
    qkv_grad_full = contract_rows(normed_b, grad_projected)
    grad_normed = contract_cols(grad_projected, back_qkv)
    attn_gain_grad = jnp.sum(grad_normed * tokens_f * rms_one, axis=0)
    input_grad = (grad_one + norm_back(grad_normed, tokens_f, rms_one, attn_gain)).astype(
        jnp.bfloat16
    )
    gains_grad_full = jnp.concatenate(
        [attn_gain_grad, ffn_gain_grad, query_gain_grad, key_gain_grad]
    )
    gain_rows = jnp.pad(
        gains_grad_full.astype(BF16).reshape(count, -1),
        ((0, 0), (0, weight_rows * LANES - norm_gains.shape[0])),
    ).reshape(count * weight_rows, LANES)
    qkv_sum, out_sum = scatter_weights(
        jnp.concatenate([qkv_grad_full.astype(BF16), gain_rows], axis=1),
        jnp.concatenate([out_grad_full.astype(BF16), side_grad_full.astype(BF16)], axis=1),
    )
    qkv_grad = qkv_sum[:, : qkv_weight.shape[1]]
    gains_grad = qkv_sum[:, qkv_weight.shape[1] :].reshape(-1)[: norm_gains.shape[0]]
    out_grad, side_grad = out_sum[:, :D], out_sum[:, D:]
    return (output, input_grad, per_layer_grad, qkv_grad, out_grad, ffn_grad, side_grad, gains_grad)


def solution(mesh):
    return jax.shard_map(
        local,
        mesh=mesh,
        in_specs=(
            P("fsdp", None),
            P("fsdp", None),
            P("fsdp", None),
            P(),
            P(),
            P("fsdp", None),
            P("fsdp", None),
            P("fsdp", None, None),
            P("fsdp", None),
            P("fsdp"),
        ),
        out_specs=(
            P("fsdp", None),
            P("fsdp", None),
            P("fsdp", None),
            P("fsdp", None),
            P("fsdp", None),
            P("fsdp", None, None),
            P("fsdp", None),
            P("fsdp"),
        ),
        check_vma=False,
    )
```

```python
import functools

import jax
import jax.numpy as jnp
from jax import lax
from jax.experimental import pallas as pl
from jax.experimental.pallas import tpu as pltpu
from jax.sharding import PartitionSpec as P

D = 2048
HQ = 8
KVH = 2
HD = 256
PL = 256
RANK = 64
WINDOW = 512


EPSILON = 1e-06
NEGATIVE = -1e30
ROPE_BASE = 10000.0


PLANE = 8
LANES = 128
MESH = pl.DeviceIdType.MESH
BF16 = jnp.bfloat16
F32 = jnp.float32


def flipped(index, bit):
    return index + bit - 2 * bit * lax.rem(lax.div(index, bit), 2)


def swapped(block, bit):
    route = [(i, i ^ bit) for i in range(lax.axis_size("fsdp"))]
    return lax.ppermute(block, "fsdp", route)


def weight_bits(count):
    return [8] + [1 << i for i in range(5, count.bit_length() - 1)] + [1]


def greet(partners):
    barrier = pltpu.get_barrier_semaphore()
    for partner in partners:
        pl.semaphore_signal(barrier, inc=1, device_id=(partner,), device_id_type=MESH)
    pl.semaphore_wait(barrier, len(partners))


def remote(src, dst, send, recv, device):
    return pltpu.make_async_remote_copy(
        src_ref=src,
        dst_ref=dst,
        send_sem=send,
        recv_sem=recv,
        device_id=(device,),
        device_id_type=MESH,
    )


def half_split(width):
    return (width // LANES + 1) // 2 * LANES


def head_norm(field):
    return lax.rsqrt(jnp.mean(field * field, axis=-1, keepdims=True) + EPSILON)


def turn(field, cosine, sine):
    half = field.shape[1] // 2
    low, high = field[:, :half], field[:, half:]
    return jnp.concatenate([low * cosine - high * sine, high * cosine + low * sine], axis=1)


def gain_spans(count, total):
    per = total // count
    spans = []
    for d in range(count):
        first = per * d // LANES
        last = (per * (d + 1) - 1) // LANES
        spans.append((first, last - first + 1))
    return spans


def placed_gains(norm_gains, rows):
    per = norm_gains.shape[0]
    offset = lax.rem(per * lax.axis_index("fsdp"), LANES)
    return lax.dynamic_update_slice(
        jnp.zeros((rows * LANES,), norm_gains.dtype), norm_gains, (offset,)
    ).reshape(rows, LANES)


def soft_rows(query, keys, reach, gap):
    scores = dot_nt(query, keys) * HD ** (-0.5)
    scores = jnp.where((gap >= 0) & (gap <= reach), scores, NEGATIVE)
    exponent = jnp.exp(scores - jnp.max(scores, axis=-1, keepdims=True))
    return exponent / jnp.sum(exponent, axis=-1, keepdims=True)


class WeightGather:
    def __init__(self, chain, pairs):
        me = lax.axis_index("fsdp")
        core, x_at, y_at = lax.rem(me, 2), lax.rem(lax.div(me, 2), 2), lax.rem(lax.div(me, 4), 2)
        z_at = lax.div(me, PLANE)
        next_x, next_y, next_c = flipped(me, 2), flipped(me, 4), flipped(me, 1)
        z_peers = [me + (lax.rem(z_at + s, chain) - z_at) * PLANE for s in range(1, chain)]
        self.partners = [next_x, next_y, next_c] + z_peers
        self.waves = []
        for own, out, (local, zs, zr, xs, xr, ys, yr, a_s, ar, bs, br, cs, cr) in pairs:
            cut = half_split(own.shape[-1])
            left, right = pl.ds(0, cut), pl.ds(cut, own.shape[-1] - cut)
            ops = {"own": pltpu.make_async_copy(own, out.at[z_at, y_at, x_at, core], local)}
            ops["z"] = [
                remote(own, out.at[z_at, y_at, x_at, core], zs.at[s], zr.at[s], z_peers[s - 1])
                for s in range(1, chain)
            ]
            steps = []
            for s in range(chain):
                k = lax.rem(z_at + chain - s, chain)
                here = out.at[k, y_at, x_at, core]
                src = own if s == 0 else here
                from_x = out.at[k, y_at, 1 - x_at, core]
                from_y = out.at[k, 1 - y_at, x_at, core]
                column = out.at[k, :, :, core]
                steps.append(
                    {
                        "x": remote(src, here, xs.at[s], xr.at[s], next_x),
                        "y": remote(src, here, ys.at[s], yr.at[s], next_y),
                        "a": remote(
                            from_x.at[:, left], from_x.at[:, left], a_s.at[s], ar.at[s], next_y
                        ),
                        "b": remote(
                            from_y.at[:, right], from_y.at[:, right], bs.at[s], br.at[s], next_x
                        ),
                        "c": remote(column, column, cs.at[s], cr.at[s], next_c),
                    }
                )
            ops["steps"] = steps
            self.waves.append(ops)

    def spread(self, w, s):
        ops = self.waves[w]
        if s == 0:
            for copy in [ops["own"]] + ops["z"]:
                copy.start()
        else:
            ops["z"][s - 1].wait_recv()
        ops["steps"][s]["x"].start()
        ops["steps"][s]["y"].start()

    def pass_on(self, w, s):
        step = self.waves[w]["steps"][s]
        step["x"].wait_recv()
        step["a"].start()
        step["y"].wait_recv()
        step["b"].start()

    def across(self, w, s):
        step = self.waves[w]["steps"][s]
        step["a"].wait_recv()
        step["b"].wait_recv()
        if s == 0:
            self.waves[w]["own"].wait()
        step["c"].start()

    def complete(self, w):
        for step in self.waves[w]["steps"]:
            step["c"].wait_recv()

    def drain(self):
        for ops in self.waves:
            for copy in ops["z"]:
                copy.wait_send()
            for step in ops["steps"]:
                for name in "xyabc":
                    step[name].wait_send()


def attention_forward_kernel(
    count,
    own_a,
    own_b,
    own_ffn,
    tokens,
    cosine,
    sine,
    position,
    full_a,
    full_b,
    full_ffn,
    gains,
    normed,
    projected,
    query,
    key_rows,
    value_rows,
    mixed,
    first_sum,
    normed_two,
    wa,
    wb,
    *sems,
):
    me = lax.axis_index("fsdp")
    chain = count // PLANE
    bits = weight_bits(count)
    gather = WeightGather(chain, ((own_a, wa, sems[:13]), (own_b, wb, sems[13:26])))
    ffn_local, ffn_s, ffn_r, halo_s, halo_r, save = sems[26:]
    ahead = [lax.rem(me + d, count) for d in (1, 2)]
    behind = [lax.rem(me + count - d, count) for d in (1, 2)]
    greet(gather.partners + [flipped(me, bit) for bit in bits[:-1]] + ahead + behind)
    ffn_own = pltpu.make_async_copy(own_ffn, full_ffn.at[0], ffn_local)
    ffn_copies = []
    for i, bit in enumerate(bits):
        size = 1 << i
        src = own_ffn if i == 0 else full_ffn.at[pl.ds(0, size)]
        dst = full_ffn.at[1] if i == 0 else full_ffn.at[pl.ds(size, size)]
        ffn_copies.append(remote(src, dst, ffn_s.at[i], ffn_r.at[i], flipped(me, bit)))
    halo = []
    for d in (1, 2):
        for j, rows in enumerate((key_rows, value_rows)):
            at = 2 * (d - 1) + j
            halo.append(
                remote(rows.at[2], rows.at[2 - d], halo_s.at[at], halo_r.at[at], ahead[d - 1])
            )
    for s in range(chain):
        gather.spread(0, s)
        if s >= 1:
            gather.pass_on(0, s - 1)
        if s >= 2:
            gather.across(0, s - 2)
    gather.spread(1, 0)
    ffn_own.start()
    gather.pass_on(0, chain - 1)
    gather.across(0, chain - 2)
    gather.across(0, chain - 1)
    gather.complete(0)
    keep_a = pltpu.make_async_copy(wa, full_a, save.at[0])
    keep_a.start()

    width_a, per = QKV_WIDTH, gains.shape[1] // count
    spans = gain_spans(count, gains.shape[1])
    pieces = {}
    for d, (first, n_rows) in enumerate(spans):
        block = wa[
            d // PLANE, d // 4 % 2, d // 2 % 2, d % 2, 0:16, width_a : width_a + LANES
        ].astype(F32)
        for r in range(n_rows):
            pieces.setdefault(first + r, []).append(block[r : r + 1])
    for t, terms in pieces.items():
        total = terms[0]
        for term in terms[1:]:
            total = total + term
        gains[:, t * LANES : (t + 1) * LANES] = total

    rows, depth = tokens.shape

    @pl.loop(0, rows // 32)
    def _(i):
        at = pl.ds(pl.multiple_of(i * 32, 32), 32)
        field = tokens[at].astype(F32)
        normed[at] = (field * head_norm(field) * gains[:, :depth]).astype(BF16)

    def project(n):
        at = pl.ds(pl.multiple_of(n * 512, 512), 512)
        weight = wa[:, :, :, :, :, at].reshape(depth, 512)
        projected[:, at] = jnp.dot(normed[...], weight, preferred_element_type=F32)

    query_width = HQ * HD
    kv_width = KVH * HD

    @pl.loop(query_width // 512, (query_width + 2 * kv_width) // 512)
    def _(n):
        project(n)

    for g in range(KVH):
        at = slice(query_width + g * HD, query_width + (g + 1) * HD)
        field = projected[:, at]
        key_gain = gains[:, 2 * depth + HD :]
        key_rows[2, :, g * HD : (g + 1) * HD] = turn(
            field * head_norm(field) * key_gain, cosine[...], sine[...]
        ).astype(BF16)
    value_rows[2] = projected[:, query_width + kv_width :].astype(BF16)
    for copy in halo:
        copy.start()
    gather.pass_on(1, 0)
    gather.spread(1, 1)
    ffn_copies[0].start()

    @pl.loop(0, query_width // 512)
    def _(n):
        project(n)

    @pl.loop(0, HQ)
    def _(h):
        at = pl.ds(pl.multiple_of(h * HD, HD), HD)
        field = projected[:, at]
        query_gain = gains[:, 2 * depth : 2 * depth + HD]
        query[:, at] = turn(
            field * head_norm(field) * query_gain, cosine[...], sine[...]
        ).astype(BF16)

    gather.pass_on(1, 1)
    gather.spread(1, 2)
    gather.across(1, 0)
    for copy in halo:
        copy.wait_recv()
    n_keys = 3 * rows
    gap = (
        lax.broadcasted_iota(jnp.int32, (rows, n_keys), 0)
        - lax.broadcasted_iota(jnp.int32, (rows, n_keys), 1)
        + 2 * rows
    )
    reach = jnp.minimum(position[...], WINDOW - 1)

    def heads(first, last):
        @pl.loop(first, last)
        def _(h):
            at = pl.ds(pl.multiple_of(h * HD, HD), HD)
            group = pl.ds(pl.multiple_of(lax.div(h, HQ // KVH) * HD, HD), HD)
            keys = key_rows[:, :, group].reshape(n_keys, HD)
            values = value_rows[:, :, group].reshape(n_keys, HD)
            probs = soft_rows(query[:, at], keys, reach, gap).astype(BF16)
            mixed[:, at] = jnp.dot(probs, values, preferred_element_type=F32).astype(BF16)

    heads(0, 2)
    for s in range(3, chain):
        gather.pass_on(1, s - 1)
        gather.spread(1, s)
        gather.across(1, s - 2)
    heads(2, 5)
    gather.pass_on(1, chain - 1)
    gather.across(1, chain - 2)
    heads(5, 8)
    gather.across(1, chain - 1)
    gather.complete(1)
    keep_b = pltpu.make_async_copy(wb, full_b, save.at[1])
    keep_b.start()

    @pl.loop(0, depth // 512)
    def _(n):
        at = pl.ds(pl.multiple_of(n * 512, 512), 512)
        weight = wb[:, :, :, :, :, at].reshape(depth, 512)
        first_sum[:, at] = tokens[:, at].astype(F32) + jnp.dot(
            mixed[...], weight, preferred_element_type=F32
        )

    @pl.loop(0, rows // 32)
    def _(i):
        at = pl.ds(pl.multiple_of(i * 32, 32), 32)
        field = first_sum[at]
        normed_two[at] = (field * head_norm(field) * gains[:, depth : 2 * depth]).astype(BF16)

    ffn_own.wait()
    for i, copy in enumerate(ffn_copies):
        if i > 0:
            copy.start()
        copy.wait_recv()
    for copy in ffn_copies + halo:
        copy.wait_send()
    gather.drain()
    keep_a.wait()
    keep_b.wait()


QKV_WIDTH = (HQ + 2 * KVH) * HD


def attention_forward(own_a, own_b, own_ffn, tokens, cosine, sine, position):
    count = lax.axis_size("fsdp")
    chain = count // PLANE
    rows, depth = tokens.shape
    n_blocks = 1 << len(weight_bits(count))
    dma = pltpu.SemaphoreType.DMA
    anywhere, vmem = pl.BlockSpec(memory_space=pl.ANY), pl.BlockSpec(memory_space=pltpu.VMEM)
    shape_a, shape_b = ((chain, 2, 2, 2) + own.shape for own in (own_a, own_b))
    full_a, full_b, *rest = pl.pallas_call(
        functools.partial(attention_forward_kernel, count),
        out_shape=[
            jax.ShapeDtypeStruct(shape_a, BF16),
            jax.ShapeDtypeStruct(shape_b, BF16),
            jax.ShapeDtypeStruct((n_blocks,) + own_ffn.shape, BF16),
            jax.ShapeDtypeStruct((1, 2 * depth + 2 * HD), F32),
            jax.ShapeDtypeStruct((rows, depth), BF16),
            jax.ShapeDtypeStruct((rows, QKV_WIDTH), F32),
            jax.ShapeDtypeStruct((rows, HQ * HD), BF16),
            jax.ShapeDtypeStruct((3, rows, KVH * HD), BF16),
            jax.ShapeDtypeStruct((3, rows, KVH * HD), BF16),
            jax.ShapeDtypeStruct((rows, HQ * HD), BF16),
            jax.ShapeDtypeStruct((rows, depth), F32),
            jax.ShapeDtypeStruct((rows, depth), BF16),
        ],
        in_specs=[anywhere] * 3 + [vmem] * 4,
        out_specs=[anywhere] * 3 + [vmem] * 9,
        scratch_shapes=[pltpu.VMEM(shape_a, BF16), pltpu.VMEM(shape_b, BF16)]
        + ([dma] + [dma((chain,))] * 12) * 2
        + [dma, dma((len(weight_bits(count)),)), dma((len(weight_bits(count)),))]
        + [dma((4,)), dma((4,)), dma((2,))],
        compiler_params=pltpu.CompilerParams(
            collective_id=0, has_side_effects=True, vmem_limit_bytes=58 * 2**20
        ),
        name="attention_forward",
    )(own_a, own_b, own_ffn, tokens, cosine, sine, position)
    return (full_a.reshape(-1, own_a.shape[1]), full_b.reshape(-1, own_b.shape[1]), *rest)


def add_into(target, *terms):
    rows = target.shape[0]
    tile = 16

    @pl.loop(0, rows // tile)
    def _(i):
        at = pl.ds(pl.multiple_of(i * tile, tile), tile)
        if len(terms) == 1:
            target[at] = target[at] + terms[0][at]
        else:
            total = target[at].astype(F32)
            for term in terms:
                total = total + term[at].astype(F32)
            target[at] = total.astype(target.dtype)


class WeightScatter:
    def __init__(self, chain, part, out, sibling, in_a, in_b, in_x, in_y, in_z, *sems):
        cs, cr, a_s, ar, bs, br, xs, xr, ys, yr, zs, zr = sems
        me = lax.axis_index("fsdp")
        core, x_at, y_at = lax.rem(me, 2), lax.rem(lax.div(me, 2), 2), lax.rem(lax.div(me, 4), 2)
        z_at = lax.div(me, PLANE)
        next_x, next_y, next_c = flipped(me, 2), flipped(me, 4), flipped(me, 1)
        z_peers = [me + (lax.rem(z_at + s, chain) - z_at) * PLANE for s in range(1, chain)]
        self.partners = [next_x, next_y, next_c] + z_peers
        self.chain, self.out, self.in_z = chain, out, in_z
        cut = half_split(out.shape[-1])
        left, right = pl.ds(0, cut), pl.ds(cut, out.shape[-1] - cut)
        self.left, self.right = left, right
        self.order = list(range(1, chain)) + [0]
        self.blocks = [lax.rem(z_at + s, chain) for s in range(chain)]
        self.steps = []
        for s in range(chain):
            mine = part.at[s, :, :, core]
            step = {
                "mine": [part.at[s, j // 2, j % 2, core] for j in range(4)],
                "sibling": [sibling.at[s, j // 2, j % 2] for j in range(4)],
                "in": (in_a.at[s], in_b.at[s], in_x.at[s], in_y.at[s]),
                "here": part.at[s, y_at, x_at, core],
                "to_x": part.at[s, y_at, 1 - x_at, core],
                "to_y": part.at[s, 1 - y_at, x_at, core],
                "c": remote(
                    part.at[s, :, :, 1 - core], sibling.at[s], cs.at[s], cr.at[s], next_c
                ),
            }
            corner = part.at[s, 1 - y_at, 1 - x_at, core]
            step["a"] = remote(corner.at[:, left], in_a.at[s], a_s.at[s], ar.at[s], next_x)
            step["b"] = remote(corner.at[:, right], in_b.at[s], bs.at[s], br.at[s], next_y)
            step["x"] = remote(step["to_x"], in_x.at[s], xs.at[s], xr.at[s], next_x)
            step["y"] = remote(step["to_y"], in_y.at[s], ys.at[s], yr.at[s], next_y)
            if s > 0:
                step["z"] = remote(
                    step["here"], in_z.at[s - 1], zs.at[s - 1], zr.at[s - 1], z_peers[s - 1]
                )
            self.steps.append(step)

    def cross(self, i):
        self.steps[self.order[i]]["c"].start()

    def halve(self, i):
        step = self.steps[self.order[i]]
        step["c"].wait_recv()
        for mine, sibling in zip(step["mine"], step["sibling"]):
            add_into(mine, sibling)
        step["a"].start()
        step["b"].start()

    def sideways(self, i):
        step = self.steps[self.order[i]]
        in_a, in_b, _, _ = step["in"]
        step["a"].wait_recv()
        add_into(step["to_y"].at[:, self.left], in_a)
        step["y"].start()
        step["b"].wait_recv()
        add_into(step["to_x"].at[:, self.right], in_b)
        step["x"].start()

    def finish(self, i):
        step = self.steps[self.order[i]]
        step["x"].wait_recv()
        step["y"].wait_recv()
        add_into(step["here"], *step["in"][2:])
        if "z" in step:
            step["z"].start()

    def total(self):
        for step in self.steps[1:]:
            step["z"].wait_recv()

        @pl.loop(0, self.out.shape[0] // 16)
        def _(i):
            at = pl.ds(pl.multiple_of(i * 16, 16), 16)
            total = self.steps[0]["here"][at].astype(F32)
            for s in range(self.chain - 1):
                total = total + self.in_z[s, at].astype(F32)
            self.out[at] = total

        for step in self.steps:
            for name in "cabxyz":
                if name in step:
                    step[name].wait_send()


def scatter_scratch(chain, rows, width):
    cut = half_split(width)
    shapes = [
        (chain, 2, 2, 2, rows, width),
        (chain, 2, 2, rows, width),
        (chain, rows, cut),
        (chain, rows, width - cut),
        (chain, rows, width),
        (chain, rows, width),
        (chain - 1, rows, width),
    ]
    return [pltpu.VMEM(shape, BF16) for shape in shapes] + [
        pltpu.SemaphoreType.DMA((chain,))
    ] * 12


def turn_back(grad, cosine, sine):
    half = grad.shape[1] // 2
    low, high = grad[:, :half], grad[:, half:]
    return jnp.concatenate([low * cosine + high * sine, high * cosine - low * sine], axis=1)


def head_back(grad_rot, field, gain, cosine, sine):
    grad = turn_back(grad_rot, cosine, sine)
    scale = head_norm(field)
    weighted = grad * gain
    back = scale * weighted - field * (
        scale * scale * scale * jnp.mean(weighted * field, axis=-1, keepdims=True)
    )
    return back, jnp.sum(grad * field * scale, axis=0, keepdims=True)


def attention_backward_kernel(
    count,
    full_a,
    full_b,
    side_part,
    grad_one_b,
    grad_one,
    tokens,
    mixed,
    query,
    key_rows,
    value_rows,
    projected,
    gains,
    cosine,
    sine,
    position,
    out_sum,
    grad_projected,
    input_grad,
    attn_gain_grad,
    head_gain_grad,
    weight,
    grad_mixed,
    grad_normed,
    grad_keys,
    grad_values,
    halo_out,
    halo_in,
    weight_sem,
    side_sem,
    halo_s,
    halo_r,
    part,
    *scratch,
):
    me = lax.axis_index("fsdp")
    chain = count // PLANE
    scatter = WeightScatter(chain, part, out_sum, *scratch)
    ahead = [lax.rem(me + d, count) for d in (1, 2)]
    behind = [lax.rem(me + count - d, count) for d in (1, 2)]
    greet(scatter.partners + ahead + behind)
    rows, depth = tokens.shape
    query_width, kv_width = HQ * HD, KVH * HD
    out_width = depth
    load_out = pltpu.make_async_copy(
        full_b.at[:, :, :, :, :, pl.ds(0, out_width)],
        weight.at[:, :, :, :, :, pl.ds(0, out_width)],
        weight_sem,
    )
    load_out.start()
    sides = []
    for s in range(chain):
        sides.append(
            pltpu.make_async_copy(
                side_part.at[scatter.blocks[s]],
                part.at[s, :, :, :, :, pl.ds(out_width, part.shape[-1] - out_width)],
                side_sem.at[s],
            )
        )
        sides[-1].start()
    tile = depth // chain
    block_shape = part.shape[1:5]
    for i, s in enumerate(scatter.order):
        left = mixed[:, pl.ds(pl.multiple_of(scatter.blocks[s] * tile, tile), tile)]

        @pl.loop(0, out_width // 512)
        def _(n):
            at = pl.ds(pl.multiple_of(n * 512, 512), 512)
            part[s, :, :, :, :, at] = (
                dot_tn(left, grad_one_b[:, at]).astype(BF16).reshape(block_shape + (512,))
            )

        sides[s].wait()
        scatter.cross(i)
    load_out.wait()

    @pl.loop(0, chain)
    def _(k):
        at = pl.ds(pl.multiple_of(k * tile, tile), tile)
        grad_mixed[:, at] = dot_nt(
            grad_one_b[...], weight[k, :, :, :, :, 0:out_width].reshape(tile, out_width)
        ).astype(BF16)

    load_qkv = pltpu.make_async_copy(
        full_a.at[:, :, :, :, :, pl.ds(0, QKV_WIDTH)], weight, weight_sem
    )
    load_qkv.start()
    grad_keys[...] = jnp.zeros_like(grad_keys)
    grad_values[...] = jnp.zeros_like(grad_values)
    head_gain_grad[...] = jnp.zeros_like(head_gain_grad)
    n_keys = 3 * rows
    gap = (
        lax.broadcasted_iota(jnp.int32, (rows, n_keys), 0)
        - lax.broadcasted_iota(jnp.int32, (rows, n_keys), 1)
        + 2 * rows
    )
    reach = jnp.minimum(position[...], WINDOW - 1)
    query_gain = gains[:, 2 * depth : 2 * depth + HD]
    key_gain = gains[:, 2 * depth + HD :]
    scale = HD ** (-0.5)

    def heads(first, last):
        @pl.loop(first, last)
        def _(h):
            at = pl.ds(pl.multiple_of(h * HD, HD), HD)
            group = pl.ds(pl.multiple_of(lax.div(h, HQ // KVH) * HD, HD), HD)
            keys = key_rows[:, :, group].reshape(n_keys, HD)
            values = value_rows[:, :, group].reshape(n_keys, HD)
            probs = soft_rows(query[:, at], keys, reach, gap)
            grad_probs = dot_nt(grad_mixed[:, at], values)
            delta = jnp.sum(probs * grad_probs, axis=-1, keepdims=True)
            grad_scores = (probs * (grad_probs - delta)).astype(BF16)
            grad_rot = jnp.dot(grad_scores, keys, preferred_element_type=F32) * scale
            grad_keys[:, :, group] += (dot_tn(grad_scores, query[:, at]) * scale).reshape(
                3, rows, HD
            )
            grad_values[:, :, group] += dot_tn(probs.astype(BF16), grad_mixed[:, at]).reshape(
                3, rows, HD
            )
            back, gain_grad = head_back(
                grad_rot, projected[:, at], query_gain, cosine[...], sine[...]
            )
            grad_projected[:, at] = back.astype(BF16)
            head_gain_grad[:, 0:HD] += gain_grad

    last = chain - 1
    for i in range(chain - 2):
        scatter.halve(i)
        if i >= 2:
            scatter.sideways(i - 2)
        if i >= 4:
            scatter.finish(i - 4)
    if chain > 5:
        scatter.finish(last - 5)
    heads(0, 1)
    scatter.sideways(last - 3)
    scatter.halve(last - 1)
    heads(1, 2)
    if chain > 4:
        scatter.finish(last - 4)
    scatter.sideways(last - 2)
    scatter.halve(last)
    heads(2, 3)
    scatter.finish(last - 3)
    scatter.sideways(last - 1)
    heads(3, 5)
    scatter.finish(last - 2)
    scatter.sideways(last)
    heads(5, 7)
    scatter.finish(last - 1)
    heads(7, 8)
    halo = []
    for d in (1, 2):
        for j, grad in enumerate((grad_keys, grad_values)):
            at = 2 * (d - 1) + j
            halo_out[at] = grad[2 - d].astype(BF16)
            halo.append(
                remote(
                    halo_out.at[at],
                    halo_in.at[at],
                    halo_s.at[at],
                    halo_r.at[at],
                    behind[d - 1],
                )
            )
            halo[-1].start()
    load_qkv.wait()

    @pl.loop(0, chain)
    def _(k):
        at = pl.ds(pl.multiple_of(k * tile, tile), tile)
        grad_normed[:, at] = dot_nt(
            grad_projected[:, 0:query_width],
            weight[k, :, :, :, :, 0:query_width].reshape(tile, query_width),
        )

    scatter.finish(last)
    for copy in halo:
        copy.wait_recv()
    for g in range(KVH):
        at = slice(g * HD, (g + 1) * HD)
        place = slice(query_width + g * HD, query_width + (g + 1) * HD)
        grad_rot = (
            grad_keys[2, :, at] + halo_in[0, :, at].astype(F32) + halo_in[2, :, at].astype(F32)
        )
        back, gain_grad = head_back(
            grad_rot, projected[:, place], key_gain, cosine[...], sine[...]
        )
        grad_projected[:, place] = back.astype(BF16)
        head_gain_grad[:, HD : 2 * HD] += gain_grad
    grad_projected[:, query_width + kv_width :] = (
        grad_values[2] + halo_in[1].astype(F32) + halo_in[3].astype(F32)
    ).astype(BF16)

    @pl.loop(0, chain)
    def _(k):
        at = pl.ds(pl.multiple_of(k * tile, tile), tile)
        grad_normed[:, at] += dot_nt(
            grad_projected[:, query_width:],
            weight[k, :, :, :, :, query_width:].reshape(tile, 2 * kv_width),
        )

    attn_gain_grad[...] = jnp.zeros_like(attn_gain_grad)
    attn_gain = gains[:, :depth]

    @pl.loop(0, rows // 16)
    def _(i):
        at = pl.ds(pl.multiple_of(i * 16, 16), 16)
        field = tokens[at].astype(F32)
        rms = head_norm(field)
        grad = grad_normed[at]
        weighted = grad * attn_gain
        back = rms * weighted - field * (
            rms * rms * rms * jnp.mean(weighted * field, axis=-1, keepdims=True)
        )
        input_grad[at] = (grad_one[at] + back).astype(BF16)
        attn_gain_grad[...] += jnp.sum(grad * field * rms, axis=0, keepdims=True)

    scatter.total()
    for copy in halo:
        copy.wait_send()


def attention_backward(
    full_a,
    full_b,
    side_part,
    grad_one_b,
    grad_one,
    tokens,
    mixed,
    query,
    key_rows,
    value_rows,
    projected,
    gains,
    cosine,
    sine,
    position,
):
    count = lax.axis_size("fsdp")
    chain = count // PLANE
    rows, depth = tokens.shape
    weight_rows, out_width = full_b.shape[0] // count, full_b.shape[1]
    dma = pltpu.SemaphoreType.DMA
    anywhere, vmem = pl.BlockSpec(memory_space=pl.ANY), pl.BlockSpec(memory_space=pltpu.VMEM)
    blocked = [
        array.reshape(chain, 2, 2, 2, weight_rows, array.shape[1])
        for array in (full_a, full_b, side_part)
    ]
    kv_width = KVH * HD
    return pl.pallas_call(
        functools.partial(attention_backward_kernel, count),
        out_shape=[
            jax.ShapeDtypeStruct((weight_rows, out_width), F32),
            jax.ShapeDtypeStruct((rows, QKV_WIDTH), BF16),
            jax.ShapeDtypeStruct((rows, depth), BF16),
            jax.ShapeDtypeStruct((1, depth), F32),
            jax.ShapeDtypeStruct((1, 2 * HD), F32),
        ],
        in_specs=[anywhere] * 3 + [vmem] * 12,
        out_specs=[vmem] * 5,
        scratch_shapes=[
            pltpu.VMEM((chain, 2, 2, 2, weight_rows, QKV_WIDTH), BF16),
            pltpu.VMEM((rows, HQ * HD), BF16),
            pltpu.VMEM((rows, depth), F32),
            pltpu.VMEM((3, rows, kv_width), F32),
            pltpu.VMEM((3, rows, kv_width), F32),
            pltpu.VMEM((4, rows, kv_width), BF16),
            pltpu.VMEM((4, rows, kv_width), BF16),
            dma,
            dma((chain,)),
            dma((4,)),
            dma((4,)),
        ]
        + scatter_scratch(chain, weight_rows, out_width),
        compiler_params=pltpu.CompilerParams(
            collective_id=1, has_side_effects=True, vmem_limit_bytes=62 * 2**20
        ),
        cost_estimate=pl.CostEstimate(
            flops=40 * 10**9, bytes_accessed=180 * 2**20, transcendentals=0
        ),
        name="attention_backward",
    )(
        *blocked,
        grad_one_b,
        grad_one,
        tokens,
        mixed,
        query,
        key_rows,
        value_rows,
        projected,
        gains,
        cosine,
        sine,
        position,
    )


def qkv_scatter_kernel(count, gain_part, normed, grad_projected, out_sum, gain_sem, part, *scratch):
    chain = count // PLANE
    scatter = WeightScatter(chain, part, out_sum, *scratch)
    greet(scatter.partners)
    width = grad_projected.shape[1]
    places = []
    for s in range(chain):
        places.append(
            pltpu.make_async_copy(
                gain_part.at[scatter.blocks[s]],
                part.at[s, :, :, :, :, pl.ds(width, LANES)],
                gain_sem.at[s],
            )
        )
        places[-1].start()
    tile = normed.shape[1] // chain
    block_shape = part.shape[1:5]
    for i in range(chain + 3):
        if i < chain:
            s = scatter.order[i]
            left = normed[:, pl.ds(pl.multiple_of(scatter.blocks[s] * tile, tile), tile)]

            @pl.loop(0, width // 512)
            def _(n):
                at = pl.ds(pl.multiple_of(n * 512, 512), 512)
                part[s, :, :, :, :, at] = (
                    dot_tn(left, grad_projected[:, at]).astype(BF16).reshape(block_shape + (512,))
                )

            places[s].wait()
            scatter.cross(i)
        if 1 <= i <= chain:
            scatter.halve(i - 1)
        if 2 <= i <= chain + 1:
            scatter.sideways(i - 2)
        if i >= 3:
            scatter.finish(i - 3)
    scatter.total()


def qkv_scatter(gain_part, normed, grad_projected):
    count = lax.axis_size("fsdp")
    chain = count // PLANE
    weight_rows, width = normed.shape[1] // count, grad_projected.shape[1] + LANES
    vmem = pl.BlockSpec(memory_space=pltpu.VMEM)
    return pl.pallas_call(
        functools.partial(qkv_scatter_kernel, count),
        out_shape=jax.ShapeDtypeStruct((weight_rows, width), F32),
        in_specs=[pl.BlockSpec(memory_space=pl.ANY)] + [vmem] * 2,
        out_specs=vmem,
        scratch_shapes=[pltpu.SemaphoreType.DMA((chain,))]
        + scatter_scratch(chain, weight_rows, width),
        compiler_params=pltpu.CompilerParams(
            collective_id=4, has_side_effects=True, vmem_limit_bytes=48 * 2**20
        ),
        cost_estimate=pl.CostEstimate(
            flops=40 * 10**9, bytes_accessed=180 * 2**20, transcendentals=0
        ),
        name="qkv_scatter",
    )(gain_part.reshape(chain, 2, 2, 2, weight_rows, LANES), normed, grad_projected)


class TokenCube:
    def __init__(self, own, held, part, in_half, in_x, in_y, in_z, gs, gr, ss, sr):
        me = lax.axis_index("fsdp")
        next_x, next_y, next_z = (flipped(me, bit) for bit in TOKEN_BITS)
        self.partners = [next_x, next_y, next_z]
        half = own.shape[0] // 2
        top, low = pl.ds(0, half), pl.ds(half, half)
        self.top, self.low = top, low
        plan = {
            "zt": (own.at[top], held.at[4, top], next_z),
            "zl": (own.at[low], held.at[4, low], next_z),
            "x": (own, held.at[1], next_x),
            "y": (own, held.at[2], next_y),
            "dt": (held.at[1, top], held.at[3, top], next_y),
            "dl": (held.at[2, low], held.at[3, low], next_x),
            "xt": (held.at[4, top], held.at[5, top], next_x),
            "yt": (held.at[4, top], held.at[6, top], next_y),
            "xl": (held.at[4, low], held.at[5, low], next_x),
            "yl": (held.at[4, low], held.at[6, low], next_y),
            "et": (held.at[5, top], held.at[7, top], next_y),
            "el": (held.at[6, low], held.at[7, low], next_x),
        }
        self.gather = {
            name: remote(src, dst, gs.at[i], gr.at[i], device)
            for i, (name, (src, dst, device)) in enumerate(plan.items())
        }
        self.part, self.in_half, self.in_x, self.in_y, self.in_z = part, in_half, in_x, in_y, in_z
        self.waves = []
        for w, base in enumerate((4, 0)):
            self.waves.append(
                {
                    "a": remote(
                        part.at[base + 3, top], in_half.at[w, 0], ss.at[w, 0], sr.at[w, 0], next_x
                    ),
                    "b": remote(
                        part.at[base + 3, low], in_half.at[w, 1], ss.at[w, 1], sr.at[w, 1], next_y
                    ),
                    "x": remote(part.at[base + 1], in_x.at[w], ss.at[w, 2], sr.at[w, 2], next_x),
                    "y": remote(part.at[base + 2], in_y.at[w], ss.at[w, 3], sr.at[w, 3], next_y),
                }
            )
        self.waves[0]["z"] = remote(part.at[4], in_z, ss.at[0, 4], sr.at[0, 4], next_z)

    def start(self, *names):
        for name in names:
            self.gather[name].start()

    def arrive(self, *names):
        for name in names:
            self.gather[name].wait_recv()

    def corners(self, w):
        self.waves[w]["a"].start()
        self.waves[w]["b"].start()

    def sideways(self, w):
        base, wave = 4 - 4 * w, self.waves[w]
        wave["a"].wait_recv()
        add_into(self.part.at[base + 2, self.top], self.in_half.at[w, 0])
        wave["y"].start()
        wave["b"].wait_recv()
        add_into(self.part.at[base + 1, self.low], self.in_half.at[w, 1])
        wave["x"].start()

    def across(self):
        self.waves[0]["x"].wait_recv()
        self.waves[0]["y"].wait_recv()
        add_into(self.part.at[4], self.in_x.at[0], self.in_y.at[0])
        self.waves[0]["z"].start()

    def finish(self, out):
        self.waves[1]["x"].wait_recv()
        self.waves[1]["y"].wait_recv()
        self.waves[0]["z"].wait_recv()

        @pl.loop(0, out.shape[0] // 16)
        def _(i):
            at = pl.ds(pl.multiple_of(i * 16, 16), 16)
            out[at] = (
                self.part[0, at].astype(F32)
                + self.in_x[1, at].astype(F32)
                + self.in_y[1, at].astype(F32)
                + self.in_z[at].astype(F32)
            )

        for copy in self.gather.values():
            copy.wait_send()
        for wave in self.waves:
            for copy in wave.values():
                copy.wait_send()


TOKEN_BITS = (2, 4, 16)
ORDER = (0, 1, 2, 4, 5, 6, 7, 3)


def cube_scratch(rows, width):
    dma = pltpu.SemaphoreType.DMA
    return [
        pltpu.VMEM((8, rows, width), BF16),
        pltpu.VMEM((8, rows, width), BF16),
        pltpu.VMEM((2, 2, rows // 2, width), BF16),
        pltpu.VMEM((2, rows, width), BF16),
        pltpu.VMEM((2, rows, width), BF16),
        pltpu.VMEM((rows, width), BF16),
        dma((12,)),
        dma((12,)),
        dma((2, 5)),
        dma((2, 5)),
        dma,
    ]


def load_weights(blocks, held, sems):
    rows = blocks.shape[2]
    loads = []
    for m in (2, 0, 1):
        loads.append(
            [
                pltpu.make_async_copy(
                    blocks.at[i, m], held.at[m, pl.ds(i * rows, rows)], sems.at[m, i]
                )
                for i in range(blocks.shape[0])
            ]
        )
        for load in loads[-1]:
            load.start()
    return loads[1:] + loads[:1]


GELU_A = 0.7978845608028654
GELU_B = 0.044715


def tanh_inner(gate):
    return jnp.tanh(GELU_A * (gate + GELU_B * gate * gate * gate))


def dot_nt(left, right):
    return lax.dot_general(left, right, (((1,), (1,)), ((), ())), preferred_element_type=F32)


def dot_tn(left, right):
    return lax.dot_general(left, right, (((0,), (0,)), ((), ())), preferred_element_type=F32)


HIDDEN_TILE = 512
WIDTH_TILE = 1024


def ffn_forward_kernel(own, blocks, *refs):
    out, held_out, gate_out, up_out, weights, gate_st, up_st, act = refs[:8]
    load_sem, save_sem, keep_sem = refs[8:11]
    held, part, in_half, in_x, in_y, in_z, gs, gr, ss, sr, own_sem = refs[11:]
    cube = TokenCube(own, held, part, in_half, in_x, in_y, in_z, gs, gr, ss, sr)
    greet(cube.partners)
    cube.start("zt", "zl", "x", "y")
    keep = pltpu.make_async_copy(own, held.at[0], own_sem)
    keep.start()
    loads = load_weights(blocks, weights, load_sem)
    hidden, width = weights.shape[1], weights.shape[2]
    saves = []

    def compute(step):
        j, slot = ORDER[step], step % 2
        if step >= 2:
            for save in saves[step - 2]:
                save.wait()

        @pl.loop(0, hidden // HIDDEN_TILE)
        def _(n):
            at = pl.ds(pl.multiple_of(n * HIDDEN_TILE, HIDDEN_TILE), HIDDEN_TILE)
            gate = dot_nt(held[j], weights[0, at])
            up = dot_nt(held[j], weights[1, at])
            gate_st[slot, :, at] = gate
            up_st[slot, :, at] = up
            act[:, at] = (0.5 * gate * (1.0 + tanh_inner(gate)) * up).astype(BF16)

        saves.append(
            [
                pltpu.make_async_copy(gate_st.at[slot], gate_out.at[j], save_sem.at[0, slot]),
                pltpu.make_async_copy(up_st.at[slot], up_out.at[j], save_sem.at[1, slot]),
            ]
        )
        for save in saves[step]:
            save.start()
        if step == 0:
            for load in loads[2]:
                load.wait()

        @pl.loop(0, width // WIDTH_TILE)
        def _(n):
            at = pl.ds(pl.multiple_of(n * WIDTH_TILE, WIDTH_TILE), WIDTH_TILE)
            part[j, :, at] = jnp.dot(
                act[...], weights[2, :, at], preferred_element_type=F32
            ).astype(BF16)

    keep.wait()
    for load in loads[0] + loads[1]:
        load.wait()
    compute(0)
    cube.arrive("x", "y", "zt")
    cube.start("xt", "yt")
    compute(1)
    compute(2)
    cube.arrive("zl")
    cube.start("xl", "yl")
    cube.arrive("xt")
    cube.start("et")
    compute(3)
    cube.arrive("xl", "yt", "yl")
    cube.start("el", "dt", "dl")
    compute(4)
    compute(5)
    cube.arrive("et", "el")
    compute(6)
    cube.corners(0)
    cube.arrive("dt", "dl")
    whole = pltpu.make_async_copy(held, held_out, keep_sem)
    whole.start()
    compute(7)
    cube.sideways(0)
    cube.corners(1)
    cube.sideways(1)
    cube.across()
    cube.finish(out)
    for save in saves[6] + saves[7]:
        save.wait()
    whole.wait()


def ffn_forward(own, blocks):
    rows, width = own.shape
    hidden = blocks.shape[0] * blocks.shape[2]
    dma = pltpu.SemaphoreType.DMA
    anywhere = pl.BlockSpec(memory_space=pl.ANY)
    return pl.pallas_call(
        ffn_forward_kernel,
        out_shape=[
            jax.ShapeDtypeStruct((rows, width), F32),
            jax.ShapeDtypeStruct((8, rows, width), BF16),
            jax.ShapeDtypeStruct((8, rows, hidden), F32),
            jax.ShapeDtypeStruct((8, rows, hidden), F32),
        ],
        in_specs=[anywhere] * 2,
        out_specs=[pl.BlockSpec(memory_space=pltpu.VMEM)] + [anywhere] * 3,
        scratch_shapes=[
            pltpu.VMEM((3, hidden, width), BF16),
            pltpu.VMEM((2, rows, hidden), F32),
            pltpu.VMEM((2, rows, hidden), F32),
            pltpu.VMEM((rows, hidden), BF16),
            dma((3, blocks.shape[0])),
            dma((2, 2)),
            dma,
        ]
        + cube_scratch(rows, width),
        compiler_params=pltpu.CompilerParams(
            collective_id=2, has_side_effects=True, vmem_limit_bytes=58 * 2**20
        ),
        cost_estimate=pl.CostEstimate(
            flops=48 * rows * width * hidden, bytes_accessed=300 * 2**20, transcendentals=0
        ),
        name="ffn_forward",
    )(own, blocks)


def ffn_backward_kernel(own, normed, gate_in, up_in, blocks, *refs):
    out, mine, theirs, weights, gate_st, up_st, grads, stage = refs[:8]
    load_sem, read_sem, write_sem, normed_sem = refs[8:12]
    held, part, in_half, in_x, in_y, in_z, gs, gr, ss, sr, own_sem = refs[12:]
    cube = TokenCube(own, held, part, in_half, in_x, in_y, in_z, gs, gr, ss, sr)
    greet(cube.partners)
    cube.start("zt", "zl", "x", "y")
    keep = pltpu.make_async_copy(own, held.at[0], own_sem)
    keep.start()
    hidden, width = weights.shape[1], weights.shape[2]
    rows = own.shape[0]
    reads = []
    for step, j in enumerate(ORDER):
        slot = step % 2
        reads.append(
            [
                pltpu.make_async_copy(gate_in.at[j], gate_st.at[slot], read_sem.at[0, slot]),
                pltpu.make_async_copy(up_in.at[j], up_st.at[slot], read_sem.at[1, slot]),
            ]
        )
    for read in reads[0]:
        read.start()
    loads = load_weights(blocks, weights, load_sem)

    def compute(step):
        j, slot = ORDER[step], step % 2
        if step < 7:
            for read in reads[step + 1]:
                read.start()
        for read in reads[step]:
            read.wait()

        @pl.loop(0, hidden // HIDDEN_TILE)
        def _(n):
            at = pl.ds(pl.multiple_of(n * HIDDEN_TILE, HIDDEN_TILE), HIDDEN_TILE)
            grad_act = dot_nt(held[j], weights[2, at]).astype(BF16).astype(F32)
            gate, up = gate_st[slot, :, at], up_st[slot, :, at]
            inner = tanh_inner(gate)
            gelu = 0.5 * gate * (1.0 + inner)
            slope = 0.5 * (1.0 + inner) + 0.5 * gate * (1.0 - inner * inner) * GELU_A * (
                1.0 + 3.0 * GELU_B * gate * gate
            )
            token = pl.ds(j * rows, rows)
            grads[2, token, at] = (gelu * up).astype(BF16)
            grads[0, token, at] = (grad_act * up * slope).astype(BF16)
            grads[1, token, at] = (grad_act * gelu).astype(BF16)

        if step == 0:
            for load in loads[0] + loads[1]:
                load.wait()
        token = pl.ds(j * rows, rows)

        @pl.loop(0, width // WIDTH_TILE)
        def _(n):
            at = pl.ds(pl.multiple_of(n * WIDTH_TILE, WIDTH_TILE), WIDTH_TILE)
            part[j, :, at] = (
                jnp.dot(grads[0, token], weights[0, :, at], preferred_element_type=F32)
                + jnp.dot(grads[1, token], weights[1, :, at], preferred_element_type=F32)
            ).astype(BF16)

    keep.wait()
    for load in loads[2]:
        load.wait()
    compute(0)
    cube.arrive("x", "y", "zt")
    cube.start("xt", "yt")
    compute(1)
    compute(2)
    cube.arrive("zl")
    cube.start("xl", "yl")
    cube.arrive("xt")
    cube.start("et")
    compute(3)
    cube.arrive("xl", "yt", "yl")
    cube.start("el", "dt", "dl")
    compute(4)
    compute(5)
    cube.arrive("et", "el")
    compute(6)
    cube.corners(0)
    cube.arrive("dt", "dl")
    compute(7)
    cube.corners(1)
    tokens = 8 * rows
    refill = pltpu.make_async_copy(
        normed, weights.at[pl.ds(0, tokens // hidden)], normed_sem
    )
    refill.start()
    tile = stage.shape[1]
    half = hidden // 2
    jobs = [(m, i) for m in (2, 0, 1) for i in range(hidden // tile)]
    writes = []

    def weight_grad(count):
        for _ in range(count):
            index = len(writes)
            m, i = jobs[index]
            slot = index % 2
            if index >= 2:
                writes[index - 2].wait()
            if m == 0 and i == 0:
                refill.wait()
            first = (i * tile + half) % hidden

            @pl.loop(0, width // WIDTH_TILE)
            def _(n):
                at = pl.ds(pl.multiple_of(n * WIDTH_TILE, WIDTH_TILE), WIDTH_TILE)
                if m == 2:
                    right = held[:, :, at].reshape(tokens, WIDTH_TILE)
                else:
                    right = weights[: tokens // hidden, :, at].reshape(tokens, WIDTH_TILE)
                stage[slot, :, at] = dot_tn(
                    grads[m, :, pl.ds(first, tile)], right
                ).astype(BF16)

            target = theirs if first >= half else mine
            write = pltpu.make_async_copy(
                stage.at[slot], target.at[m, pl.ds(first % half, tile)], write_sem.at[slot]
            )
            write.start()
            writes.append(write)

    weight_grad(1)
    cube.sideways(0)
    weight_grad(1)
    cube.sideways(1)
    weight_grad(4)
    cube.across()
    weight_grad(len(jobs) - 6)
    cube.finish(out)
    writes[-2].wait()
    writes[-1].wait()


def ffn_backward(own, normed, gate, up, blocks):
    rows, width = own.shape
    hidden = blocks.shape[0] * blocks.shape[2]
    dma = pltpu.SemaphoreType.DMA
    anywhere = pl.BlockSpec(memory_space=pl.ANY)
    grad = jax.ShapeDtypeStruct((3, hidden // 2, width), BF16)
    return pl.pallas_call(
        ffn_backward_kernel,
        out_shape=[jax.ShapeDtypeStruct((rows, width), F32), grad, grad],
        in_specs=[anywhere] * 5,
        out_specs=[pl.BlockSpec(memory_space=pltpu.VMEM), anywhere, anywhere],
        scratch_shapes=[
            pltpu.VMEM((3, hidden, width), BF16),
            pltpu.VMEM((2, rows, hidden), F32),
            pltpu.VMEM((2, rows, hidden), F32),
            pltpu.VMEM((3, 8 * rows, hidden), BF16),
            pltpu.VMEM((2, 256, width), BF16),
            dma((3, blocks.shape[0])),
            dma((2, 2)),
            dma((2,)),
            dma,
        ]
        + cube_scratch(rows, width),
        compiler_params=pltpu.CompilerParams(
            collective_id=3, has_side_effects=True, vmem_limit_bytes=62 * 2**20
        ),
        cost_estimate=pl.CostEstimate(
            flops=96 * rows * width * hidden, bytes_accessed=400 * 2**20, transcendentals=0
        ),
        name="ffn_backward",
    )(own, normed.reshape(8 * rows // hidden, hidden, width), gate, up, blocks)


def passed_along(block, axis, distance):
    devices = range(lax.axis_size(axis))
    route = [(i - distance, i) for i in devices if i - distance in devices]
    return lax.ppermute(block, axis, route)


def inv_rms(field):
    return lax.rsqrt(jnp.mean(field * field, axis=-1, keepdims=True) + EPSILON)


def gelu_tanh(field):
    return jax.nn.gelu(field, approximate=True)


def layout(seq_lengths, seq_order, token_index):
    slot_ids = jnp.arange(seq_lengths.shape[0], dtype=jnp.int32)
    packed = jnp.sum(
        jnp.where(seq_order[:, None] == slot_ids[None, :], seq_lengths[None, :], 0), axis=1
    )
    starts = jnp.sum(jnp.where(slot_ids[None, :] < slot_ids[:, None], packed[None, :], 0), axis=1)
    segment = jnp.sum((token_index[:, None] >= starts[None, :]).astype(jnp.int32), axis=1) - 1
    offset = jnp.max(jnp.where(starts[None, :] <= token_index[:, None], starts[None, :], 0), axis=1)
    return (segment, token_index - offset)


def angles(position):
    half_width = HD // 2
    freq = ROPE_BASE ** (-2.0 * jnp.arange(half_width, dtype=jnp.float32) / HD)
    phase = position.astype(jnp.float32)[:, None] * freq[None, :]
    phase = jnp.concatenate([phase, phase], axis=-1)
    return (jnp.cos(phase)[:, None, :], jnp.sin(phase)[:, None, :])


def rotate(field, cosine, sine):
    half_width = field.shape[-1] // 2
    turned = jnp.concatenate([-field[..., half_width:], field[..., :half_width]], axis=-1)
    return field * cosine + turned * sine


def rotate_back(grad_in, cosine, sine):
    half_width = grad_in.shape[-1] // 2
    shifted = grad_in * sine
    return grad_in * cosine + jnp.concatenate(
        [shifted[..., half_width:], -shifted[..., :half_width]], axis=-1
    )


def norm_back(grad_out, field, scale_inv, gain):
    weighted = grad_out * gain
    return scale_inv * weighted - field * scale_inv**3 * jnp.mean(
        weighted * field, axis=-1, keepdims=True
    )


def contract_rows(left_op, right_op):
    return lax.dot_general(
        left_op, right_op, (((0,), (0,)), ((), ())), preferred_element_type=jnp.float32
    )


def contract_cols(left_op, right_op):
    return lax.dot_general(
        left_op, right_op, (((1,), (1,)), ((), ())), preferred_element_type=jnp.float32
    )


def local(
    tokens,
    per_layer,
    cotangent,
    seq_lengths,
    seq_order,
    qkv_weight,
    out_weight,
    ffn_weights,
    side_weights,
    norm_gains,
):
    tok_rows = tokens.shape[0]
    my_index = lax.axis_index("fsdp")
    token_index = my_index * tok_rows + jnp.arange(tok_rows, dtype=jnp.int32)
    segment, position = layout(seq_lengths, seq_order, token_index)
    cosine, sine = angles(position)
    reach = (WINDOW + tok_rows - 2) // tok_rows
    assert reach == 2
    key_index = jnp.concatenate(
        [token_index - distance * tok_rows for distance in range(reach, 0, -1)] + [token_index]
    )
    key_segment, unused_pos = layout(seq_lengths, seq_order, key_index)
    key_gap = token_index[:, None] - key_index[None, :]
    allowed = (segment[:, None] == key_segment[None, :]) & (key_gap >= 0) & (key_gap < WINDOW)
    score_scale = HD ** (-0.5)
    split_at = PL + RANK
    group_size = HQ // KVH
    query_width = HQ * HD
    kv_width = KVH * HD
    count = lax.axis_size("fsdp")
    bits = weight_bits(count)
    weight_rows = qkv_weight.shape[0]
    (
        qkv_gathered,
        out_gathered,
        ffn_blocks,
        gain_all,
        normed_b,
        projected,
        query_b,
        key_blocks,
        value_blocks,
        mixed_b,
        first_sum,
        normed_two,
    ) = attention_forward(
        jnp.concatenate([qkv_weight, placed_gains(norm_gains, weight_rows)], axis=1),
        jnp.concatenate([out_weight, side_weights], axis=1),
        ffn_weights.transpose(1, 0, 2),
        tokens,
        cosine[:, 0, : HD // 2],
        sine[:, 0, : HD // 2],
        position[:, None],
    )
    qkv_all = qkv_gathered[:, : qkv_weight.shape[1]]
    out_all, side_all = out_gathered[:, :D], out_gathered[:, D:]
    ffn_gain = gain_all[0, D : 2 * D]
    rms_two = inv_rms(first_sum)
    ffn_out, normed_all, gate_kept, up_kept = ffn_forward(normed_two, ffn_blocks)
    second_sum = first_sum + ffn_out
    second_b = second_sum.astype(jnp.bfloat16)
    side_in = jnp.dot(second_b, side_all[:, :split_at], preferred_element_type=jnp.float32)
    per_f = per_layer.astype(jnp.float32)
    gelu_per, pull_per = jax.vjp(gelu_tanh, side_in[:, :PL])
    combined = jnp.concatenate(
        [(gelu_per * per_f).astype(jnp.bfloat16), side_in[:, PL:].astype(jnp.bfloat16)], axis=1
    )
    output = (second_sum + contract_cols(combined, side_all[:, split_at:])).astype(jnp.bfloat16)
    back_qkv, back_out, back_side = qkv_all, out_all, side_all
    grad_y = cotangent.astype(jnp.float32)
    grad_comb = jnp.dot(cotangent, back_side[:, split_at:], preferred_element_type=jnp.float32)
    side_out_grad = contract_rows(cotangent, combined)
    per_layer_grad = (grad_comb[:, :PL] * gelu_per).astype(jnp.bfloat16)
    grad_per = pull_per(grad_comb[:, :PL] * per_f)[0]
    grad_side = jnp.concatenate([grad_per, grad_comb[:, PL:]], axis=1).astype(jnp.bfloat16)
    side_in_grad = contract_rows(second_b, grad_side)
    side_grad_full = jnp.concatenate([side_in_grad, side_out_grad], axis=1).astype(BF16)
    grad_two = grad_y + contract_cols(grad_side, back_side[:, :split_at])
    grad_two_b = grad_two.astype(jnp.bfloat16)
    grad_h2, ffn_part, ffn_sent = ffn_backward(
        grad_two_b, normed_all, gate_kept, up_kept, ffn_blocks
    )
    for bit in reversed(bits):
        ffn_part = ffn_part.astype(F32) + swapped(ffn_sent, bit).astype(F32)
        if bit != bits[0]:
            half = ffn_part.shape[1] // 2
            ffn_sent = ffn_part[:, half:].astype(BF16)
            ffn_part = ffn_part[:, :half]
    ffn_grad = ffn_part.transpose(1, 0, 2)
    ffn_gain_grad = jnp.sum(grad_h2 * first_sum * rms_two, axis=0)
    grad_one = grad_two + norm_back(grad_h2, first_sum, rms_two, ffn_gain)
    grad_one_b = grad_one.astype(jnp.bfloat16)
    out_sum, grad_projected, input_grad, attn_gain_grad, head_gain_grad = attention_backward(
        qkv_gathered,
        out_gathered,
        side_grad_full,
        grad_one_b,
        grad_one,
        tokens,
        mixed_b,
        query_b,
        key_blocks,
        value_blocks,
        projected,
        gain_all,
        cosine[:, 0, : HD // 2],
        sine[:, 0, : HD // 2],
        position[:, None],
    )
    gains_grad_full = jnp.concatenate([attn_gain_grad[0], ffn_gain_grad, head_gain_grad[0]])
    gain_rows = jnp.pad(
        gains_grad_full.astype(BF16).reshape(count, -1),
        ((0, 0), (0, weight_rows * LANES - norm_gains.shape[0])),
    ).reshape(count * weight_rows, LANES)
    qkv_sum = qkv_scatter(gain_rows, normed_b, grad_projected)
    qkv_grad = qkv_sum[:, : qkv_weight.shape[1]]
    gains_grad = qkv_sum[:, qkv_weight.shape[1] :].reshape(-1)[: norm_gains.shape[0]]
    out_grad, side_grad = out_sum[:, :D], out_sum[:, D:]
    return (output, input_grad, per_layer_grad, qkv_grad, out_grad, ffn_grad, side_grad, gains_grad)


def solution(mesh):
    return jax.shard_map(
        local,
        mesh=mesh,
        in_specs=(
            P("fsdp", None),
            P("fsdp", None),
            P("fsdp", None),
            P(),
            P(),
            P("fsdp", None),
            P("fsdp", None),
            P("fsdp", None, None),
            P("fsdp", None),
            P("fsdp"),
        ),
        out_specs=(
            P("fsdp", None),
            P("fsdp", None),
            P("fsdp", None),
            P("fsdp", None),
            P("fsdp", None),
            P("fsdp", None, None),
            P("fsdp", None),
            P("fsdp"),
        ),
        check_vma=False,
    )
```

```python
import functools

import jax
import jax.numpy as jnp
from jax import lax
from jax.experimental import pallas as pl
from jax.experimental.pallas import tpu as pltpu
from jax.sharding import PartitionSpec as P

D = 2048
HQ = 8
KVH = 2
HD = 256
PL = 256
RANK = 64
WINDOW = 512


EPSILON = 1e-06
NEGATIVE = -1e30
ROPE_BASE = 10000.0


PLANE = 8
LANES = 128
MESH = pl.DeviceIdType.MESH
BF16 = jnp.bfloat16
F32 = jnp.float32


def flipped(index, bit):
    return index + bit - 2 * bit * lax.rem(lax.div(index, bit), 2)


def swapped(block, bit):
    route = [(i, i ^ bit) for i in range(lax.axis_size("fsdp"))]
    return lax.ppermute(block, "fsdp", route)


def weight_bits(count):
    return [8] + [1 << i for i in range(5, count.bit_length() - 1)] + [1]


def greet(partners):
    barrier = pltpu.get_barrier_semaphore()
    for partner in partners:
        pl.semaphore_signal(barrier, inc=1, device_id=(partner,), device_id_type=MESH)
    pl.semaphore_wait(barrier, len(partners))


def remote(src, dst, send, recv, device):
    return pltpu.make_async_remote_copy(
        src_ref=src,
        dst_ref=dst,
        send_sem=send,
        recv_sem=recv,
        device_id=(device,),
        device_id_type=MESH,
    )


def half_split(width):
    return (width // LANES + 1) // 2 * LANES


def head_norm(field):
    return lax.rsqrt(jnp.mean(field * field, axis=-1, keepdims=True) + EPSILON)


def turn(field, cosine, sine):
    half = field.shape[1] // 2
    low, high = field[:, :half], field[:, half:]
    return jnp.concatenate([low * cosine - high * sine, high * cosine + low * sine], axis=1)


def gain_spans(count, total):
    per = total // count
    spans = []
    for d in range(count):
        first = per * d // LANES
        last = (per * (d + 1) - 1) // LANES
        spans.append((first, last - first + 1))
    return spans


def placed_gains(norm_gains, rows):
    per = norm_gains.shape[0]
    offset = lax.rem(per * lax.axis_index("fsdp"), LANES)
    return lax.dynamic_update_slice(
        jnp.zeros((rows * LANES,), norm_gains.dtype), norm_gains, (offset,)
    ).reshape(rows, LANES)


def soft_rows(query, keys, reach, gap):
    scores = dot_nt(query, keys) * HD ** (-0.5)
    scores = jnp.where((gap >= 0) & (gap <= reach), scores, NEGATIVE)
    exponent = jnp.exp(scores - jnp.max(scores, axis=-1, keepdims=True))
    return exponent / jnp.sum(exponent, axis=-1, keepdims=True)


class WeightGather:
    def __init__(self, chain, pairs):
        me = lax.axis_index("fsdp")
        core, x_at, y_at = lax.rem(me, 2), lax.rem(lax.div(me, 2), 2), lax.rem(lax.div(me, 4), 2)
        z_at = lax.div(me, PLANE)
        next_x, next_y, next_c = flipped(me, 2), flipped(me, 4), flipped(me, 1)
        z_peers = [me + (lax.rem(z_at + s, chain) - z_at) * PLANE for s in range(1, chain)]
        self.partners = [next_x, next_y, next_c] + z_peers
        self.order = sorted(range(chain), key=lambda s: (min(s, chain - s), s))
        self.waves = []
        for own, out, (local, zs, zr, xs, xr, ys, yr, a_s, ar, bs, br, cs, cr) in pairs:
            cut = half_split(own.shape[-1])
            left, right = pl.ds(0, cut), pl.ds(cut, own.shape[-1] - cut)
            ops = {"own": pltpu.make_async_copy(own, out.at[z_at, y_at, x_at, core], local)}
            ops["z"] = [None] + [
                remote(own, out.at[z_at, y_at, x_at, core], zs.at[s], zr.at[s], z_peers[s - 1])
                for s in self.order[1:]
            ]
            steps = []
            for s in self.order:
                k = lax.rem(z_at + chain - s, chain)
                here = out.at[k, y_at, x_at, core]
                src = own if s == 0 else here
                from_x = out.at[k, y_at, 1 - x_at, core]
                from_y = out.at[k, 1 - y_at, x_at, core]
                column = out.at[k, :, :, core]
                steps.append(
                    {
                        "x": remote(src, here, xs.at[s], xr.at[s], next_x),
                        "y": remote(src, here, ys.at[s], yr.at[s], next_y),
                        "a": remote(
                            from_x.at[:, left], from_x.at[:, left], a_s.at[s], ar.at[s], next_y
                        ),
                        "b": remote(
                            from_y.at[:, right], from_y.at[:, right], bs.at[s], br.at[s], next_x
                        ),
                        "c": remote(column, column, cs.at[s], cr.at[s], next_c),
                    }
                )
            ops["steps"] = steps
            self.waves.append(ops)

    def spread(self, w, s):
        ops = self.waves[w]
        if s == 0:
            ops["own"].start()
        else:
            ops["z"][s].wait_recv()
        if w == 0 and s + 1 < len(ops["z"]):
            ops["z"][s + 1].start()
        if w > 0 and s == 0:
            for copy in ops["z"][1:]:
                copy.start()
        ops["steps"][s]["x"].start()
        ops["steps"][s]["y"].start()

    def pass_on(self, w, s):
        step = self.waves[w]["steps"][s]
        step["x"].wait_recv()
        step["a"].start()
        step["y"].wait_recv()
        step["b"].start()

    def across(self, w, s):
        step = self.waves[w]["steps"][s]
        step["a"].wait_recv()
        step["b"].wait_recv()
        if s == 0:
            self.waves[w]["own"].wait()
        step["c"].start()

    def complete(self, w):
        for step in self.waves[w]["steps"]:
            step["c"].wait_recv()

    def drain(self):
        for ops in self.waves:
            for copy in ops["z"][1:]:
                copy.wait_send()
            for step in ops["steps"]:
                for name in "xyabc":
                    step[name].wait_send()


def attention_forward_kernel(
    count,
    own_a,
    own_b,
    own_ffn,
    tokens,
    cosine,
    sine,
    position,
    full_a,
    full_b,
    full_ffn,
    gains,
    normed,
    projected,
    query,
    key_rows,
    value_rows,
    mixed,
    first_sum,
    normed_two,
    wa,
    wb,
    *sems,
):
    me = lax.axis_index("fsdp")
    chain = count // PLANE
    bits = weight_bits(count)
    gather = WeightGather(chain, ((own_a, wa, sems[:13]), (own_b, wb, sems[13:26])))
    first_s, first_r, ffn_s, ffn_r, rest_s, rest_r, halo_s, halo_r, save = sems[26:]
    ahead = [lax.rem(me + d, count) for d in (1, 2)]
    behind = [lax.rem(me + count - d, count) for d in (1, 2)]
    greet(gather.partners + [flipped(me, bit) for bit in bits[:-1]] + ahead + behind)
    ffn_first, ffn_copies, ffn_rest = [], [], []
    piece = own_ffn.shape[1] // FFN_PIECES
    for j in range(2 * FFN_PIECES):
        at = pl.ds(j % FFN_PIECES * piece, piece)
        m = j // FFN_PIECES
        ffn_first.append(
            remote(
                own_ffn.at[m, at],
                full_ffn.at[1, m, at],
                first_s.at[j],
                first_r.at[j],
                flipped(me, bits[0]),
            )
        )
    for i, bit in enumerate(bits[1:]):
        size, partner = 2 << i, flipped(me, bit)
        ffn_copies.append(remote(own_ffn, full_ffn.at[size], ffn_s.at[i], ffn_r.at[i], partner))
        ffn_rest.append(
            remote(
                full_ffn.at[pl.ds(1, size - 1)],
                full_ffn.at[pl.ds(size + 1, size - 1)],
                rest_s.at[i],
                rest_r.at[i],
                partner,
            )
        )
    halo = []
    for d in (1, 2):
        for j, rows in enumerate((key_rows, value_rows)):
            at = 2 * (d - 1) + j
            halo.append(
                remote(rows.at[2], rows.at[2 - d], halo_s.at[at], halo_r.at[at], ahead[d - 1])
            )
    for s in range(chain):
        gather.spread(0, s)
        if s >= 1:
            gather.pass_on(0, s - 1)
        if s >= 2:
            gather.across(0, s - 2)
    gather.spread(1, 0)
    for copy in ffn_first + ffn_copies:
        copy.start()
    gather.pass_on(0, chain - 1)
    gather.across(0, chain - 2)
    gather.across(0, chain - 1)
    gather.complete(0)
    for s in range(1, chain):
        gather.spread(1, s)
    keep_a = pltpu.make_async_copy(wa, full_a, save.at[0])
    keep_a.start()

    width_a, per = QKV_WIDTH, gains.shape[1] // count
    spans = gain_spans(count, gains.shape[1])
    pieces = {}
    for d, (first, n_rows) in enumerate(spans):
        block = wa[
            d // PLANE, d // 4 % 2, d // 2 % 2, d % 2, 0:16, width_a : width_a + LANES
        ].astype(F32)
        for r in range(n_rows):
            pieces.setdefault(first + r, []).append(block[r : r + 1])
    for t, terms in pieces.items():
        total = terms[0]
        for term in terms[1:]:
            total = total + term
        gains[:, t * LANES : (t + 1) * LANES] = total

    rows, depth = tokens.shape

    @pl.loop(0, rows // 32)
    def _(i):
        at = pl.ds(pl.multiple_of(i * 32, 32), 32)
        field = tokens[at].astype(F32)
        normed[at] = (field * head_norm(field) * gains[:, :depth]).astype(BF16)

    def project(n):
        at = pl.ds(pl.multiple_of(n * 512, 512), 512)
        weight = wa[:, :, :, :, :, at].reshape(depth, 512)
        projected[:, at] = jnp.dot(normed[...], weight, preferred_element_type=F32)

    query_width = HQ * HD
    kv_width = KVH * HD

    @pl.loop(query_width // 512, (query_width + 2 * kv_width) // 512)
    def _(n):
        project(n)

    for g in range(KVH):
        at = slice(query_width + g * HD, query_width + (g + 1) * HD)
        field = projected[:, at]
        key_gain = gains[:, 2 * depth + HD :]
        key_rows[2, :, g * HD : (g + 1) * HD] = turn(
            field * head_norm(field) * key_gain, cosine[...], sine[...]
        ).astype(BF16)
    value_rows[2] = projected[:, query_width + kv_width :].astype(BF16)
    for copy in halo:
        copy.start()
    for s in range(chain - 3):
        gather.pass_on(1, s)

    @pl.loop(0, query_width // 512)
    def _(n):
        project(n)

    gather.pass_on(1, chain - 3)
    for s in range(chain - 3):
        gather.across(1, s)

    @pl.loop(0, HQ)
    def _(h):
        at = pl.ds(pl.multiple_of(h * HD, HD), HD)
        field = projected[:, at]
        query_gain = gains[:, 2 * depth : 2 * depth + HD]
        query[:, at] = turn(
            field * head_norm(field) * query_gain, cosine[...], sine[...]
        ).astype(BF16)

    gather.pass_on(1, chain - 2)
    gather.across(1, chain - 3)
    for copy in halo:
        copy.wait_recv()
    n_keys = 3 * rows
    gap = (
        lax.broadcasted_iota(jnp.int32, (rows, n_keys), 0)
        - lax.broadcasted_iota(jnp.int32, (rows, n_keys), 1)
        + 2 * rows
    )
    reach = jnp.minimum(position[...], WINDOW - 1)

    def heads(first, last):
        @pl.loop(first, last)
        def _(h):
            at = pl.ds(pl.multiple_of(h * HD, HD), HD)
            group = pl.ds(pl.multiple_of(lax.div(h, HQ // KVH) * HD, HD), HD)
            keys = key_rows[:, :, group].reshape(n_keys, HD)
            values = value_rows[:, :, group].reshape(n_keys, HD)
            probs = soft_rows(query[:, at], keys, reach, gap).astype(BF16)
            mixed[:, at] = jnp.dot(probs, values, preferred_element_type=F32).astype(BF16)

    heads(0, 1)
    gather.pass_on(1, chain - 1)
    heads(1, 2)
    gather.across(1, chain - 2)
    heads(2, 4)
    gather.across(1, chain - 1)
    heads(4, 8)
    gather.complete(1)
    keep_b = pltpu.make_async_copy(wb, full_b, save.at[1])
    keep_b.start()

    @pl.loop(0, depth // 512)
    def _(n):
        at = pl.ds(pl.multiple_of(n * 512, 512), 512)
        weight = wb[:, :, :, :, :, at].reshape(depth, 512)
        first_sum[:, at] = tokens[:, at].astype(F32) + jnp.dot(
            mixed[...], weight, preferred_element_type=F32
        )

    @pl.loop(0, rows // 32)
    def _(i):
        at = pl.ds(pl.multiple_of(i * 32, 32), 32)
        field = first_sum[at]
        normed_two[at] = (field * head_norm(field) * gains[:, depth : 2 * depth]).astype(BF16)

    for copy in ffn_first:
        copy.wait_recv()
    for copy, rest in zip(ffn_copies, ffn_rest):
        rest.start()
        copy.wait_recv()
        rest.wait_recv()
    for copy in ffn_first + ffn_copies + ffn_rest + halo:
        copy.wait_send()
    gather.drain()
    keep_a.wait()
    keep_b.wait()


FFN_PIECES = 2
QKV_WIDTH = (HQ + 2 * KVH) * HD


def attention_forward(own_a, own_b, own_ffn, tokens, cosine, sine, position):
    count = lax.axis_size("fsdp")
    chain = count // PLANE
    rows, depth = tokens.shape
    n_blocks = 1 << len(weight_bits(count))
    dma = pltpu.SemaphoreType.DMA
    anywhere, vmem = pl.BlockSpec(memory_space=pl.ANY), pl.BlockSpec(memory_space=pltpu.VMEM)
    shape_a, shape_b = ((chain, 2, 2, 2) + own.shape for own in (own_a, own_b))
    full_a, full_b, *rest = pl.pallas_call(
        functools.partial(attention_forward_kernel, count),
        out_shape=[
            jax.ShapeDtypeStruct(shape_a, BF16),
            jax.ShapeDtypeStruct(shape_b, BF16),
            jax.ShapeDtypeStruct((n_blocks,) + own_ffn.shape, BF16),
            jax.ShapeDtypeStruct((1, 2 * depth + 2 * HD), F32),
            jax.ShapeDtypeStruct((rows, depth), BF16),
            jax.ShapeDtypeStruct((rows, QKV_WIDTH), F32),
            jax.ShapeDtypeStruct((rows, HQ * HD), BF16),
            jax.ShapeDtypeStruct((3, rows, KVH * HD), BF16),
            jax.ShapeDtypeStruct((3, rows, KVH * HD), BF16),
            jax.ShapeDtypeStruct((rows, HQ * HD), BF16),
            jax.ShapeDtypeStruct((rows, depth), F32),
            jax.ShapeDtypeStruct((rows, depth), BF16),
        ],
        in_specs=[anywhere] * 3 + [vmem] * 4,
        out_specs=[anywhere] * 3 + [vmem] * 9,
        scratch_shapes=[pltpu.VMEM(shape_a, BF16), pltpu.VMEM(shape_b, BF16)]
        + ([dma] + [dma((chain,))] * 12) * 2
        + [dma((2 * FFN_PIECES,))] * 2
        + [dma((len(weight_bits(count)) - 1,))] * 4
        + [dma((4,)), dma((4,)), dma((2,))],
        compiler_params=pltpu.CompilerParams(
            collective_id=0, has_side_effects=True, vmem_limit_bytes=58 * 2**20
        ),
        name="attention_forward",
    )(own_a, own_b, own_ffn, tokens, cosine, sine, position)
    return (full_a.reshape(-1, own_a.shape[1]), full_b.reshape(-1, own_b.shape[1]), *rest)


def add_into(target, *terms):
    rows = target.shape[0]
    tile = 16

    @pl.loop(0, rows // tile)
    def _(i):
        at = pl.ds(pl.multiple_of(i * tile, tile), tile)
        if len(terms) == 1:
            target[at] = target[at] + terms[0][at]
        else:
            total = target[at].astype(F32)
            for term in terms:
                total = total + term[at].astype(F32)
            target[at] = total.astype(target.dtype)


class WeightScatter:
    def __init__(self, chain, part, out, sibling, in_a, in_b, in_x, in_y, in_z, *sems):
        cs, cr, a_s, ar, bs, br, xs, xr, ys, yr, zs, zr = sems
        me = lax.axis_index("fsdp")
        core, x_at, y_at = lax.rem(me, 2), lax.rem(lax.div(me, 2), 2), lax.rem(lax.div(me, 4), 2)
        z_at = lax.div(me, PLANE)
        next_x, next_y, next_c = flipped(me, 2), flipped(me, 4), flipped(me, 1)
        z_peers = [me + (lax.rem(z_at + s, chain) - z_at) * PLANE for s in range(1, chain)]
        self.partners = [next_x, next_y, next_c] + z_peers
        self.chain, self.out, self.in_z = chain, out, in_z
        cut = half_split(out.shape[-1])
        left, right = pl.ds(0, cut), pl.ds(cut, out.shape[-1] - cut)
        self.left, self.right = left, right
        self.order = list(range(1, chain)) + [0]
        self.blocks = [lax.rem(z_at + s, chain) for s in range(chain)]
        self.steps = []
        for s in range(chain):
            mine = part.at[s, :, :, core]
            step = {
                "mine": [part.at[s, j // 2, j % 2, core] for j in range(4)],
                "sibling": [sibling.at[s, j // 2, j % 2] for j in range(4)],
                "in": (in_a.at[s], in_b.at[s], in_x.at[s], in_y.at[s]),
                "here": part.at[s, y_at, x_at, core],
                "to_x": part.at[s, y_at, 1 - x_at, core],
                "to_y": part.at[s, 1 - y_at, x_at, core],
                "c": remote(
                    part.at[s, :, :, 1 - core], sibling.at[s], cs.at[s], cr.at[s], next_c
                ),
            }
            corner = part.at[s, 1 - y_at, 1 - x_at, core]
            step["a"] = remote(corner.at[:, left], in_a.at[s], a_s.at[s], ar.at[s], next_x)
            step["b"] = remote(corner.at[:, right], in_b.at[s], bs.at[s], br.at[s], next_y)
            step["x"] = remote(step["to_x"], in_x.at[s], xs.at[s], xr.at[s], next_x)
            step["y"] = remote(step["to_y"], in_y.at[s], ys.at[s], yr.at[s], next_y)
            if s > 0:
                step["z"] = remote(
                    step["here"], in_z.at[s - 1], zs.at[s - 1], zr.at[s - 1], z_peers[s - 1]
                )
            self.steps.append(step)

    def cross(self, i):
        self.steps[self.order[i]]["c"].start()

    def halve(self, i):
        step = self.steps[self.order[i]]
        step["c"].wait_recv()
        for mine, sibling in zip(step["mine"], step["sibling"]):
            add_into(mine, sibling)
        step["a"].start()
        step["b"].start()

    def sideways(self, i):
        step = self.steps[self.order[i]]
        in_a, in_b, _, _ = step["in"]
        step["a"].wait_recv()
        add_into(step["to_y"].at[:, self.left], in_a)
        step["y"].start()
        step["b"].wait_recv()
        add_into(step["to_x"].at[:, self.right], in_b)
        step["x"].start()

    def finish(self, i):
        step = self.steps[self.order[i]]
        step["x"].wait_recv()
        step["y"].wait_recv()
        add_into(step["here"], *step["in"][2:])
        if "z" in step:
            step["z"].start()

    def total(self):
        for step in self.steps[1:]:
            step["z"].wait_recv()

        @pl.loop(0, self.out.shape[0] // 16)
        def _(i):
            at = pl.ds(pl.multiple_of(i * 16, 16), 16)
            total = self.steps[0]["here"][at].astype(F32)
            for s in range(self.chain - 1):
                total = total + self.in_z[s, at].astype(F32)
            self.out[at] = total

        for step in self.steps:
            for name in "cabxyz":
                if name in step:
                    step[name].wait_send()


def scatter_scratch(chain, rows, width):
    cut = half_split(width)
    shapes = [
        (chain, 2, 2, 2, rows, width),
        (chain, 2, 2, rows, width),
        (chain, rows, cut),
        (chain, rows, width - cut),
        (chain, rows, width),
        (chain, rows, width),
        (chain - 1, rows, width),
    ]
    return [pltpu.VMEM(shape, BF16) for shape in shapes] + [
        pltpu.SemaphoreType.DMA((chain,))
    ] * 12


def turn_back(grad, cosine, sine):
    half = grad.shape[1] // 2
    low, high = grad[:, :half], grad[:, half:]
    return jnp.concatenate([low * cosine + high * sine, high * cosine - low * sine], axis=1)


def head_back(grad_rot, field, gain, cosine, sine):
    grad = turn_back(grad_rot, cosine, sine)
    scale = head_norm(field)
    weighted = grad * gain
    back = scale * weighted - field * (
        scale * scale * scale * jnp.mean(weighted * field, axis=-1, keepdims=True)
    )
    return back, jnp.sum(grad * field * scale, axis=0, keepdims=True)


def attention_backward_kernel(
    count,
    full_a,
    full_b,
    grad_one_in,
    tokens_in,
    query_in,
    key_in,
    value_in,
    projected_in,
    grad_one_b,
    mixed,
    second,
    grad_side,
    cotangent,
    combined,
    gains,
    cosine,
    sine,
    position,
    out_sum,
    grad_projected,
    input_grad,
    attn_gain_grad,
    head_gain_grad,
    weight,
    grad_mixed,
    grad_normed,
    grad_keys,
    grad_values,
    halo_out,
    halo_in,
    grad_one,
    tokens,
    query,
    key_rows,
    value_rows,
    projected,
    weight_sem,
    fill_sem,
    halo_s,
    halo_r,
    part,
    *scratch,
):
    me = lax.axis_index("fsdp")
    chain = count // PLANE
    scatter = WeightScatter(chain, part, out_sum, *scratch)
    ahead = [lax.rem(me + d, count) for d in (1, 2)]
    behind = [lax.rem(me + count - d, count) for d in (1, 2)]
    greet(scatter.partners + ahead + behind)
    rows, depth = tokens.shape
    query_width, kv_width = HQ * HD, KVH * HD
    out_width = depth
    load_out = pltpu.make_async_copy(
        full_b.at[:, :, :, :, :, pl.ds(0, out_width)],
        weight.at[:, :, :, :, :, pl.ds(0, out_width)],
        weight_sem,
    )
    load_out.start()
    fills = [
        pltpu.make_async_copy(src, dst, fill_sem.at[i])
        for i, (src, dst) in enumerate(
            (
                (query_in, query),
                (key_in, key_rows),
                (value_in, value_rows),
                (projected_in, projected),
                (tokens_in, tokens),
                (grad_one_in, grad_one),
            )
        )
    ]
    for fill in fills:
        fill.start()
    tile = depth // chain
    block_shape = part.shape[1:5]
    for i, s in enumerate(scatter.order):
        columns = pl.ds(pl.multiple_of(scatter.blocks[s] * tile, tile), tile)
        left = mixed[:, columns]

        @pl.loop(0, out_width // 512)
        def _(n):
            at = pl.ds(pl.multiple_of(n * 512, 512), 512)
            part[s, :, :, :, :, at] = (
                dot_tn(left, grad_one_b[:, at]).astype(BF16).reshape(block_shape + (512,))
            )

        side = dot_tn(second[:, columns], grad_side[...])
        side = side + dot_tn(cotangent[:, columns], combined[...])
        part[s, :, :, :, :, out_width:] = side.astype(BF16).reshape(
            block_shape + (part.shape[-1] - out_width,)
        )
        scatter.cross(i)
        if i >= 1:
            scatter.halve(i - 1)
        if i >= 3:
            scatter.sideways(i - 3)
        if i >= 5:
            scatter.finish(i - 5)
    load_out.wait()

    @pl.loop(0, chain)
    def _(k):
        at = pl.ds(pl.multiple_of(k * tile, tile), tile)
        grad_mixed[:, at] = dot_nt(
            grad_one_b[...], weight[k, :, :, :, :, 0:out_width].reshape(tile, out_width)
        ).astype(BF16)

    load_qkv = pltpu.make_async_copy(
        full_a.at[:, :, :, :, :, pl.ds(0, QKV_WIDTH)], weight, weight_sem
    )
    load_qkv.start()
    grad_keys[...] = jnp.zeros_like(grad_keys)
    grad_values[...] = jnp.zeros_like(grad_values)
    head_gain_grad[...] = jnp.zeros_like(head_gain_grad)
    n_keys = 3 * rows
    gap = (
        lax.broadcasted_iota(jnp.int32, (rows, n_keys), 0)
        - lax.broadcasted_iota(jnp.int32, (rows, n_keys), 1)
        + 2 * rows
    )
    reach = jnp.minimum(position[...], WINDOW - 1)
    query_gain = gains[:, 2 * depth : 2 * depth + HD]
    key_gain = gains[:, 2 * depth + HD :]
    scale = HD ** (-0.5)

    def heads(first, last):
        @pl.loop(first, last)
        def _(h):
            at = pl.ds(pl.multiple_of(h * HD, HD), HD)
            group = pl.ds(pl.multiple_of(lax.div(h, HQ // KVH) * HD, HD), HD)
            keys = key_rows[:, :, group].reshape(n_keys, HD)
            values = value_rows[:, :, group].reshape(n_keys, HD)
            probs = soft_rows(query[:, at], keys, reach, gap)
            grad_probs = dot_nt(grad_mixed[:, at], values)
            delta = jnp.sum(probs * grad_probs, axis=-1, keepdims=True)
            grad_scores = (probs * (grad_probs - delta)).astype(BF16)
            grad_rot = jnp.dot(grad_scores, keys, preferred_element_type=F32) * scale
            grad_keys[:, :, group] += (dot_tn(grad_scores, query[:, at]) * scale).reshape(
                3, rows, HD
            )
            grad_values[:, :, group] += dot_tn(probs.astype(BF16), grad_mixed[:, at]).reshape(
                3, rows, HD
            )
            back, gain_grad = head_back(
                grad_rot, projected[:, at], query_gain, cosine[...], sine[...]
            )
            grad_projected[:, at] = back.astype(BF16)
            head_gain_grad[:, 0:HD] += gain_grad

    last = chain - 1
    scatter.sideways(last - 2)
    if chain > 4:
        scatter.finish(last - 4)
    scatter.halve(last)
    for fill in fills:
        fill.wait()
    heads(0, 1)
    scatter.sideways(last - 1)
    scatter.finish(last - 3)
    heads(1, 3)
    scatter.sideways(last)
    scatter.finish(last - 2)
    heads(3, 6)
    scatter.finish(last - 1)
    heads(6, 8)
    halo = []
    for d in (1, 2):
        for j, grad in enumerate((grad_keys, grad_values)):
            at = 2 * (d - 1) + j
            halo_out[at] = grad[2 - d].astype(BF16)
            halo.append(
                remote(
                    halo_out.at[at],
                    halo_in.at[at],
                    halo_s.at[at],
                    halo_r.at[at],
                    behind[d - 1],
                )
            )
            halo[-1].start()
    load_qkv.wait()

    @pl.loop(0, chain)
    def _(k):
        at = pl.ds(pl.multiple_of(k * tile, tile), tile)
        grad_normed[:, at] = dot_nt(
            grad_projected[:, 0:query_width],
            weight[k, :, :, :, :, 0:query_width].reshape(tile, query_width),
        )

    for copy in halo:
        copy.wait_recv()
    for g in range(KVH):
        at = slice(g * HD, (g + 1) * HD)
        place = slice(query_width + g * HD, query_width + (g + 1) * HD)
        grad_rot = (
            grad_keys[2, :, at] + halo_in[0, :, at].astype(F32) + halo_in[2, :, at].astype(F32)
        )
        back, gain_grad = head_back(
            grad_rot, projected[:, place], key_gain, cosine[...], sine[...]
        )
        grad_projected[:, place] = back.astype(BF16)
        head_gain_grad[:, HD : 2 * HD] += gain_grad
    grad_projected[:, query_width + kv_width :] = (
        grad_values[2] + halo_in[1].astype(F32) + halo_in[3].astype(F32)
    ).astype(BF16)

    @pl.loop(0, chain)
    def _(k):
        at = pl.ds(pl.multiple_of(k * tile, tile), tile)
        grad_normed[:, at] += dot_nt(
            grad_projected[:, query_width:],
            weight[k, :, :, :, :, query_width:].reshape(tile, 2 * kv_width),
        )

    attn_gain_grad[...] = jnp.zeros_like(attn_gain_grad)
    attn_gain = gains[:, :depth]

    @pl.loop(0, rows // 16)
    def _(i):
        at = pl.ds(pl.multiple_of(i * 16, 16), 16)
        field = tokens[at].astype(F32)
        rms = head_norm(field)
        grad = grad_normed[at]
        weighted = grad * attn_gain
        back = rms * weighted - field * (
            rms * rms * rms * jnp.mean(weighted * field, axis=-1, keepdims=True)
        )
        input_grad[at] = (grad_one[at] + back).astype(BF16)
        attn_gain_grad[...] += jnp.sum(grad * field * rms, axis=0, keepdims=True)

    scatter.finish(last)
    scatter.total()
    for copy in halo:
        copy.wait_send()


def attention_backward(
    full_a,
    full_b,
    grad_one_b,
    grad_one,
    tokens,
    mixed,
    second,
    grad_side,
    cotangent,
    combined,
    query,
    key_rows,
    value_rows,
    projected,
    gains,
    cosine,
    sine,
    position,
):
    count = lax.axis_size("fsdp")
    chain = count // PLANE
    rows, depth = tokens.shape
    weight_rows, out_width = full_b.shape[0] // count, full_b.shape[1]
    dma = pltpu.SemaphoreType.DMA
    anywhere, vmem = pl.BlockSpec(memory_space=pl.ANY), pl.BlockSpec(memory_space=pltpu.VMEM)
    blocked = [
        array.reshape(chain, 2, 2, 2, weight_rows, array.shape[1])
        for array in (full_a, full_b)
    ]
    kv_width = KVH * HD
    filled = (grad_one, tokens, query, key_rows, value_rows, projected)
    return pl.pallas_call(
        functools.partial(attention_backward_kernel, count),
        out_shape=[
            jax.ShapeDtypeStruct((weight_rows, out_width), F32),
            jax.ShapeDtypeStruct((rows, QKV_WIDTH), BF16),
            jax.ShapeDtypeStruct((rows, depth), BF16),
            jax.ShapeDtypeStruct((1, depth), F32),
            jax.ShapeDtypeStruct((1, 2 * HD), F32),
        ],
        in_specs=[anywhere] * 8 + [vmem] * 10,
        out_specs=[vmem] * 5,
        scratch_shapes=[
            pltpu.VMEM((chain, 2, 2, 2, weight_rows, QKV_WIDTH), BF16),
            pltpu.VMEM((rows, HQ * HD), BF16),
            pltpu.VMEM((rows, depth), F32),
            pltpu.VMEM((3, rows, kv_width), F32),
            pltpu.VMEM((3, rows, kv_width), F32),
            pltpu.VMEM((4, rows, kv_width), BF16),
            pltpu.VMEM((4, rows, kv_width), BF16),
            *(
                pltpu.VMEM(array.shape, array.dtype)
                for array in filled
            ),
            dma,
            dma((len(filled),)),
            dma((4,)),
            dma((4,)),
        ]
        + scatter_scratch(chain, weight_rows, out_width),
        compiler_params=pltpu.CompilerParams(
            collective_id=1, has_side_effects=True, vmem_limit_bytes=62 * 2**20
        ),
        cost_estimate=pl.CostEstimate(
            flops=40 * 10**9, bytes_accessed=180 * 2**20, transcendentals=0
        ),
        name="attention_backward",
    )(
        *blocked,
        grad_one,
        tokens,
        query,
        key_rows,
        value_rows,
        projected,
        grad_one_b,
        mixed,
        second,
        grad_side,
        cotangent,
        combined,
        gains,
        cosine,
        sine,
        position,
    )


def qkv_scatter_kernel(count, gain_part, normed, grad_projected, out_sum, gain_sem, part, *scratch):
    chain = count // PLANE
    scatter = WeightScatter(chain, part, out_sum, *scratch)
    greet(scatter.partners)
    width = grad_projected.shape[1]
    places = []
    for s in range(chain):
        places.append(
            pltpu.make_async_copy(
                gain_part.at[scatter.blocks[s]],
                part.at[s, :, :, :, :, pl.ds(width, LANES)],
                gain_sem.at[s],
            )
        )
        places[-1].start()
    tile = normed.shape[1] // chain
    block_shape = part.shape[1:5]
    for i in range(chain + 3):
        if i < chain:
            s = scatter.order[i]
            left = normed[:, pl.ds(pl.multiple_of(scatter.blocks[s] * tile, tile), tile)]

            @pl.loop(0, width // 512)
            def _(n):
                at = pl.ds(pl.multiple_of(n * 512, 512), 512)
                part[s, :, :, :, :, at] = (
                    dot_tn(left, grad_projected[:, at]).astype(BF16).reshape(block_shape + (512,))
                )

            places[s].wait()
            scatter.cross(i)
        if 1 <= i <= chain:
            scatter.halve(i - 1)
        if 2 <= i <= chain + 1:
            scatter.sideways(i - 2)
        if i >= 3:
            scatter.finish(i - 3)
    scatter.total()


def qkv_scatter(gain_part, normed, grad_projected):
    count = lax.axis_size("fsdp")
    chain = count // PLANE
    weight_rows, width = normed.shape[1] // count, grad_projected.shape[1] + LANES
    vmem = pl.BlockSpec(memory_space=pltpu.VMEM)
    return pl.pallas_call(
        functools.partial(qkv_scatter_kernel, count),
        out_shape=jax.ShapeDtypeStruct((weight_rows, width), F32),
        in_specs=[pl.BlockSpec(memory_space=pl.ANY)] + [vmem] * 2,
        out_specs=vmem,
        scratch_shapes=[pltpu.SemaphoreType.DMA((chain,))]
        + scatter_scratch(chain, weight_rows, width),
        compiler_params=pltpu.CompilerParams(
            collective_id=4, has_side_effects=True, vmem_limit_bytes=48 * 2**20
        ),
        cost_estimate=pl.CostEstimate(
            flops=40 * 10**9, bytes_accessed=180 * 2**20, transcendentals=0
        ),
        name="qkv_scatter",
    )(gain_part.reshape(chain, 2, 2, 2, weight_rows, LANES), normed, grad_projected)


class TokenCube:
    def __init__(self, own, held, part, in_half, in_x, in_y, in_z, gs, gr, ss, sr):
        me = lax.axis_index("fsdp")
        next_x, next_y, next_z = (flipped(me, bit) for bit in TOKEN_BITS)
        self.partners = [next_x, next_y, next_z]
        half = own.shape[0] // 2
        top, low = pl.ds(0, half), pl.ds(half, half)
        self.top, self.low = top, low
        plan = {
            "zt": (own.at[top], held.at[4, top], next_z),
            "zl": (own.at[low], held.at[4, low], next_z),
            "x": (own, held.at[1], next_x),
            "y": (own, held.at[2], next_y),
            "dt": (held.at[1, top], held.at[3, top], next_y),
            "dl": (held.at[2, low], held.at[3, low], next_x),
            "xt": (held.at[4, top], held.at[5, top], next_x),
            "yt": (held.at[4, top], held.at[6, top], next_y),
            "xl": (held.at[4, low], held.at[5, low], next_x),
            "yl": (held.at[4, low], held.at[6, low], next_y),
            "et": (held.at[5, top], held.at[7, top], next_y),
            "el": (held.at[6, low], held.at[7, low], next_x),
        }
        self.gather = {
            name: remote(src, dst, gs.at[i], gr.at[i], device)
            for i, (name, (src, dst, device)) in enumerate(plan.items())
        }
        self.part, self.in_half, self.in_x, self.in_y, self.in_z = part, in_half, in_x, in_y, in_z
        self.waves = []
        side = own.shape[1] // 2
        for w, (base, first) in enumerate(((4, 0), (4, side), (0, 0), (0, side))):
            at = pl.ds(first, side)
            corner = part.at[base + 3, :, at]
            to_x, to_y = part.at[base + 1, :, at], part.at[base + 2, :, at]
            here = part.at[base, :, at]
            wave = {
                "a": remote(corner.at[top], in_half.at[w, 0], ss.at[w, 0], sr.at[w, 0], next_x),
                "b": remote(corner.at[low], in_half.at[w, 1], ss.at[w, 1], sr.at[w, 1], next_y),
                "x": remote(to_x, in_x.at[w], ss.at[w, 2], sr.at[w, 2], next_x),
                "y": remote(to_y, in_y.at[w], ss.at[w, 3], sr.at[w, 3], next_y),
            }
            if base:
                wave["z"] = remote(here, in_z.at[w], ss.at[w, 4], sr.at[w, 4], next_z)
            self.waves.append((wave, at, to_x, to_y, here))

    def start(self, *names):
        for name in names:
            self.gather[name].start()

    def arrive(self, *names):
        for name in names:
            self.gather[name].wait_recv()

    def corners(self, w):
        wave = self.waves[w][0]
        wave["a"].start()
        wave["b"].start()

    def sideways(self, w):
        wave, _, to_x, to_y, _ = self.waves[w]
        wave["a"].wait_recv()
        add_into(to_y.at[self.top], self.in_half.at[w, 0])
        wave["y"].start()
        wave["b"].wait_recv()
        add_into(to_x.at[self.low], self.in_half.at[w, 1])
        wave["x"].start()

    def across(self, w):
        wave, _, _, _, here = self.waves[w]
        wave["x"].wait_recv()
        wave["y"].wait_recv()
        add_into(here, self.in_x.at[w], self.in_y.at[w])
        wave["z"].start()

    def finish(self, out):
        for w in (2, 3):
            wave, side = self.waves[w][:2]
            wave["x"].wait_recv()
            wave["y"].wait_recv()
            self.waves[w - 2][0]["z"].wait_recv()

            @pl.loop(0, out.shape[0] // 16)
            def _(i):
                at = pl.ds(pl.multiple_of(i * 16, 16), 16)
                out[at, side] = (
                    self.part[0, at, side].astype(F32)
                    + self.in_x[w, at].astype(F32)
                    + self.in_y[w, at].astype(F32)
                    + self.in_z[w - 2, at].astype(F32)
                )

        for copy in self.gather.values():
            copy.wait_send()
        for wave, *_ in self.waves:
            for copy in wave.values():
                copy.wait_send()


TOKEN_BITS = (2, 4, 16)
ORDER = (0, 1, 2, 4, 5, 6, 7, 3)


def cube_scratch(rows, width):
    dma = pltpu.SemaphoreType.DMA
    return [
        pltpu.VMEM((8, rows, width), BF16),
        pltpu.VMEM((8, rows, width), BF16),
        pltpu.VMEM((4, 2, rows // 2, width // 2), BF16),
        pltpu.VMEM((4, rows, width // 2), BF16),
        pltpu.VMEM((4, rows, width // 2), BF16),
        pltpu.VMEM((2, rows, width // 2), BF16),
        dma((12,)),
        dma((12,)),
        dma((4, 5)),
        dma((4, 5)),
        dma,
    ]


def load_weights(own, blocks, held, sems):
    rows = blocks.shape[2]
    loads = []
    for m in range(2):
        for i in range(blocks.shape[0]):
            loads.append(
                pltpu.make_async_copy(
                    own.at[m] if i == 0 else blocks.at[i, m],
                    held.at[m, pl.ds(i * rows, rows)],
                    sems.at[m, i],
                )
            )
            loads[-1].start()
    return loads


GELU_A = 0.7978845608028654
GELU_B = 0.044715


def tanh_inner(gate):
    return jnp.tanh(GELU_A * (gate + GELU_B * gate * gate * gate))


def dot_nt(left, right):
    return lax.dot_general(left, right, (((1,), (1,)), ((), ())), preferred_element_type=F32)


def dot_tn(left, right):
    return lax.dot_general(left, right, (((0,), (0,)), ((), ())), preferred_element_type=F32)


HIDDEN_TILE = 512
WIDTH_TILE = 1024


def ffn_forward_kernel(count, own, own_down, own_ffn, blocks, *refs):
    out, held_out, gate_out, up_out, down_out, weights, gate_st, up_st, act = refs[:9]
    load_sem, save_sem, keep_sem, down_local, down_s, down_r = refs[9:15]
    held, part, in_half, in_x, in_y, in_z, gs, gr, ss, sr, own_sem = refs[15:]
    me = lax.axis_index("fsdp")
    bits = weight_bits(count)
    cube = TokenCube(own, held, part, in_half, in_x, in_y, in_z, gs, gr, ss, sr)
    greet(cube.partners + [flipped(me, bit) for bit in bits])
    cube.start("zt", "zl", "x", "y")
    keep = pltpu.make_async_copy(own, held.at[0], own_sem)
    keep.start()
    block = own_down.shape[0]
    down_keep = pltpu.make_async_copy(own_down, weights.at[2, pl.ds(0, block)], down_local)
    down_keep.start()
    downs = []
    for i, bit in enumerate(bits):
        size = block << i
        src = own_down if i == 0 else weights.at[2, pl.ds(0, size)]
        downs.append(
            remote(
                src, weights.at[2, pl.ds(size, size)], down_s.at[i], down_r.at[i], flipped(me, bit)
            )
        )
    downs[0].start()
    loads = load_weights(own_ffn, blocks, weights, load_sem)
    hidden, width = weights.shape[1], weights.shape[2]
    saves = []

    def enter(step):
        j, slot, third = ORDER[step], step % 2, step % 3
        if step >= 2:
            for save in saves[step - 2]:
                save.wait()

        @pl.loop(0, hidden // HIDDEN_TILE)
        def _(n):
            at = pl.ds(pl.multiple_of(n * HIDDEN_TILE, HIDDEN_TILE), HIDDEN_TILE)
            gate = dot_nt(held[j], weights[0, at])
            up = dot_nt(held[j], weights[1, at])
            gate_st[slot, :, at] = gate
            up_st[slot, :, at] = up
            act[third, :, at] = (0.5 * gate * (1.0 + tanh_inner(gate)) * up).astype(BF16)

        saves.append(
            [
                pltpu.make_async_copy(gate_st.at[slot], gate_out.at[j], save_sem.at[0, slot]),
                pltpu.make_async_copy(up_st.at[slot], up_out.at[j], save_sem.at[1, slot]),
            ]
        )
        for save in saves[step]:
            save.start()

    def leave(step):
        j, third = ORDER[step], step % 3

        @pl.loop(0, width // WIDTH_TILE)
        def _(n):
            at = pl.ds(pl.multiple_of(n * WIDTH_TILE, WIDTH_TILE), WIDTH_TILE)
            part[j, :, at] = jnp.dot(
                act[third], weights[2, :, at], preferred_element_type=F32
            ).astype(BF16)

    keep.wait()
    for load in loads:
        load.wait()
    enter(0)
    cube.arrive("x", "y", "zt")
    cube.start("xt", "yt")
    enter(1)
    down_keep.wait()
    for i in range(1, len(downs)):
        downs[i - 1].wait_recv()
        downs[i].start()
    enter(2)
    cube.arrive("zl")
    cube.start("xl", "yl")
    cube.arrive("xt")
    cube.start("et")
    downs[-1].wait_recv()
    leave(0)
    leave(1)
    leave(2)
    save_down = pltpu.make_async_copy(weights.at[2], down_out, down_local)
    save_down.start()
    enter(3)
    cube.arrive("xl", "yt", "yl")
    cube.start("el", "dt", "dl")
    leave(3)
    for step in (4, 5):
        enter(step)
        leave(step)
    cube.arrive("et", "el")
    enter(6)
    leave(6)
    cube.corners(0)
    cube.corners(1)
    cube.arrive("dt", "dl")
    whole = pltpu.make_async_copy(held, held_out, keep_sem)
    whole.start()
    enter(7)
    leave(7)
    cube.sideways(0)
    cube.sideways(1)
    cube.corners(2)
    cube.corners(3)
    cube.across(0)
    cube.across(1)
    cube.sideways(2)
    cube.sideways(3)
    cube.finish(out)
    for save in saves[6] + saves[7] + [save_down, whole]:
        save.wait()
    for copy in downs:
        copy.wait_send()


def ffn_forward(own, own_down, own_ffn, blocks):
    count = lax.axis_size("fsdp")
    rows, width = own.shape
    hidden = blocks.shape[0] * blocks.shape[2]
    n_bits = len(weight_bits(count))
    dma = pltpu.SemaphoreType.DMA
    anywhere = pl.BlockSpec(memory_space=pl.ANY)
    return pl.pallas_call(
        functools.partial(ffn_forward_kernel, count),
        out_shape=[
            jax.ShapeDtypeStruct((rows, width), F32),
            jax.ShapeDtypeStruct((8, rows, width), BF16),
            jax.ShapeDtypeStruct((8, rows, hidden), F32),
            jax.ShapeDtypeStruct((8, rows, hidden), F32),
            jax.ShapeDtypeStruct((hidden, width), BF16),
        ],
        in_specs=[anywhere] * 4,
        out_specs=[pl.BlockSpec(memory_space=pltpu.VMEM)] + [anywhere] * 4,
        scratch_shapes=[
            pltpu.VMEM((3, hidden, width), BF16),
            pltpu.VMEM((2, rows, hidden), F32),
            pltpu.VMEM((2, rows, hidden), F32),
            pltpu.VMEM((3, rows, hidden), BF16),
            dma((2, blocks.shape[0])),
            dma((2, 2)),
            dma,
            dma,
            dma((n_bits,)),
            dma((n_bits,)),
        ]
        + cube_scratch(rows, width),
        compiler_params=pltpu.CompilerParams(
            collective_id=2, has_side_effects=True, vmem_limit_bytes=58 * 2**20
        ),
        cost_estimate=pl.CostEstimate(
            flops=48 * rows * width * hidden, bytes_accessed=300 * 2**20, transcendentals=0
        ),
        name="ffn_forward",
    )(own, own_down, own_ffn, blocks)


def ffn_backward_kernel(own, normed, gate_in, up_in, down, own_ffn, blocks, *refs):
    out, mine, further, landed, weights, gate_st, up_st, grads, stage, fetched = refs[:10]
    load_sem, down_sem, read_sem, write_sem, normed_sem, pair_s, pair_r, fetch_sem = refs[10:18]
    held, part, in_half, in_x, in_y, in_z, gs, gr, ss, sr, own_sem = refs[18:]
    sibling = flipped(lax.axis_index("fsdp"), 1)
    cube = TokenCube(own, held, part, in_half, in_x, in_y, in_z, gs, gr, ss, sr)
    greet(cube.partners + [sibling])
    cube.start("zt", "zl", "x", "y")
    keep = pltpu.make_async_copy(own, held.at[0], own_sem)
    keep.start()
    hidden, width = weights.shape[1], weights.shape[2]
    rows = own.shape[0]
    reads = []
    for step, j in enumerate(ORDER):
        slot = step % 2
        reads.append(
            [
                pltpu.make_async_copy(gate_in.at[j], gate_st.at[slot], read_sem.at[0, slot]),
                pltpu.make_async_copy(up_in.at[j], up_st.at[slot], read_sem.at[1, slot]),
            ]
        )
    for read in reads[0]:
        read.start()
    load_down = pltpu.make_async_copy(down, weights.at[2], down_sem)
    load_down.start()
    loads = load_weights(own_ffn, blocks, weights, load_sem)

    def compute(step):
        j, slot = ORDER[step], step % 2
        if step < 7:
            for read in reads[step + 1]:
                read.start()
        for read in reads[step]:
            read.wait()

        @pl.loop(0, hidden // HIDDEN_TILE)
        def _(n):
            at = pl.ds(pl.multiple_of(n * HIDDEN_TILE, HIDDEN_TILE), HIDDEN_TILE)
            grad_act = dot_nt(held[j], weights[2, at]).astype(BF16).astype(F32)
            gate, up = gate_st[slot, :, at], up_st[slot, :, at]
            inner = tanh_inner(gate)
            gelu = 0.5 * gate * (1.0 + inner)
            slope = 0.5 * (1.0 + inner) + 0.5 * gate * (1.0 - inner * inner) * GELU_A * (
                1.0 + 3.0 * GELU_B * gate * gate
            )
            token = pl.ds(j * rows, rows)
            grads[2, token, at] = (gelu * up).astype(BF16)
            grads[0, token, at] = (grad_act * up * slope).astype(BF16)
            grads[1, token, at] = (grad_act * gelu).astype(BF16)

        if step == 0:
            for load in loads:
                load.wait()
        token = pl.ds(j * rows, rows)

        @pl.loop(0, width // WIDTH_TILE)
        def _(n):
            at = pl.ds(pl.multiple_of(n * WIDTH_TILE, WIDTH_TILE), WIDTH_TILE)
            part[j, :, at] = (
                jnp.dot(grads[0, token], weights[0, :, at], preferred_element_type=F32)
                + jnp.dot(grads[1, token], weights[1, :, at], preferred_element_type=F32)
            ).astype(BF16)

    keep.wait()
    load_down.wait()
    compute(0)
    cube.arrive("x", "y", "zt")
    cube.start("xt", "yt")
    compute(1)
    compute(2)
    cube.arrive("zl")
    cube.start("xl", "yl")
    cube.arrive("xt")
    cube.start("et")
    compute(3)
    cube.arrive("xl", "yt", "yl")
    cube.start("el", "dt", "dl")
    compute(4)
    compute(5)
    cube.arrive("et", "el")
    compute(6)
    cube.corners(0)
    cube.corners(1)
    cube.arrive("dt", "dl")
    compute(7)
    tokens = 8 * rows
    refill = pltpu.make_async_copy(
        normed, weights.at[pl.ds(0, tokens // hidden)], normed_sem
    )
    refill.start()
    tile = stage.shape[1]
    half, quarter = hidden // 2, hidden // 4
    tiles = [(m, i * tile) for m in (2, 0, 1) for i in range(half // tile)]
    pairs, busy = [], [None, None]
    for n, (m, first) in enumerate(tiles):
        pairs.append(
            remote(
                stage.at[n % 2],
                landed.at[m, pl.ds(first, tile)],
                pair_s.at[n],
                pair_r.at[n],
                sibling,
            )
        )
    fetches = [
        pltpu.make_async_copy(
            landed.at[m, pl.ds(first, tile)], fetched.at[n % 2], fetch_sem.at[n % 2]
        )
        for n, (m, first) in enumerate(tiles)
    ]
    done = [0]

    def weight_grad(times):
        for _ in range(times):
            job = done[0]
            done[0] = job + 1
            n, for_sibling = job % len(tiles), job < len(tiles)
            m, first = tiles[n]
            slot = job % 2
            if job == len(tiles) // 3:
                refill.wait()
            if busy[slot] is not None:
                busy[slot]()
            if not for_sibling:
                pairs[n].wait_recv()
                fetches[n].start()
                fetches[n].wait()
            place = first + half if for_sibling else first

            @pl.loop(0, width // WIDTH_TILE)
            def _(k):
                at = pl.ds(pl.multiple_of(k * WIDTH_TILE, WIDTH_TILE), WIDTH_TILE)
                if m == 2:
                    right = held[:, :, at].reshape(tokens, WIDTH_TILE)
                else:
                    right = weights[: tokens // hidden, :, at].reshape(tokens, WIDTH_TILE)
                grad = dot_tn(grads[m, :, pl.ds(place, tile)], right)
                if not for_sibling:
                    grad = grad + fetched[n % 2, :, at].astype(F32)
                stage[slot, :, at] = grad.astype(BF16)

            if for_sibling:
                pairs[n].start()
                busy[slot] = pairs[n].wait_send
            else:
                target = mine if first < quarter else further
                write = pltpu.make_async_copy(
                    stage.at[slot],
                    target.at[m, pl.ds(first % quarter, tile)],
                    write_sem.at[slot],
                )
                write.start()
                busy[slot] = write.wait

    cube.sideways(0)
    cube.sideways(1)
    cube.corners(2)
    cube.corners(3)
    weight_grad(3)
    cube.across(0)
    weight_grad(1)
    cube.sideways(2)
    cube.across(1)
    weight_grad(1)
    cube.sideways(3)
    weight_grad(2 * len(tiles) - 5)
    cube.finish(out)
    for end in busy:
        end()


def ffn_backward(own, normed, gate, up, down, own_ffn, blocks):
    rows, width = own.shape
    hidden = blocks.shape[0] * blocks.shape[2]
    dma = pltpu.SemaphoreType.DMA
    anywhere = pl.BlockSpec(memory_space=pl.ANY)
    tile = 256
    n_tiles = 3 * (hidden // 2) // tile
    grad = jax.ShapeDtypeStruct((3, hidden // 4, width), BF16)
    landed = jax.ShapeDtypeStruct((3, hidden // 2, width), BF16)
    return pl.pallas_call(
        ffn_backward_kernel,
        out_shape=[jax.ShapeDtypeStruct((rows, width), F32), grad, grad, landed],
        in_specs=[anywhere] * 7,
        out_specs=[pl.BlockSpec(memory_space=pltpu.VMEM)] + [anywhere] * 3,
        scratch_shapes=[
            pltpu.VMEM((3, hidden, width), BF16),
            pltpu.VMEM((2, rows, hidden), F32),
            pltpu.VMEM((2, rows, hidden), F32),
            pltpu.VMEM((3, 8 * rows, hidden), BF16),
            pltpu.VMEM((2, tile, width), BF16),
            pltpu.VMEM((2, tile, width), BF16),
            dma((2, blocks.shape[0])),
            dma,
            dma((2, 2)),
            dma((2,)),
            dma,
            dma((n_tiles,)),
            dma((n_tiles,)),
            dma((2,)),
        ]
        + cube_scratch(rows, width),
        compiler_params=pltpu.CompilerParams(
            collective_id=3, has_side_effects=True, vmem_limit_bytes=62 * 2**20
        ),
        cost_estimate=pl.CostEstimate(
            flops=96 * rows * width * hidden, bytes_accessed=400 * 2**20, transcendentals=0
        ),
        name="ffn_backward",
    )(
        own,
        normed.reshape(8 * rows // hidden, hidden, width),
        gate,
        up,
        down,
        own_ffn,
        blocks,
    )


def inv_rms(field):
    return lax.rsqrt(jnp.mean(field * field, axis=-1, keepdims=True) + EPSILON)


def gelu_tanh(field):
    return jax.nn.gelu(field, approximate=True)


def layout(seq_lengths, seq_order, token_index):
    slot_ids = jnp.arange(seq_lengths.shape[0], dtype=jnp.int32)
    packed = jnp.sum(
        jnp.where(seq_order[:, None] == slot_ids[None, :], seq_lengths[None, :], 0), axis=1
    )
    starts = jnp.sum(jnp.where(slot_ids[None, :] < slot_ids[:, None], packed[None, :], 0), axis=1)
    segment = jnp.sum((token_index[:, None] >= starts[None, :]).astype(jnp.int32), axis=1) - 1
    offset = jnp.max(jnp.where(starts[None, :] <= token_index[:, None], starts[None, :], 0), axis=1)
    return (segment, token_index - offset)


def angles(position):
    half_width = HD // 2
    freq = ROPE_BASE ** (-2.0 * jnp.arange(half_width, dtype=jnp.float32) / HD)
    phase = position.astype(jnp.float32)[:, None] * freq[None, :]
    phase = jnp.concatenate([phase, phase], axis=-1)
    return (jnp.cos(phase)[:, None, :], jnp.sin(phase)[:, None, :])


def norm_back(grad_out, field, scale_inv, gain):
    weighted = grad_out * gain
    return scale_inv * weighted - field * scale_inv**3 * jnp.mean(
        weighted * field, axis=-1, keepdims=True
    )


def contract_rows(left_op, right_op):
    return lax.dot_general(
        left_op, right_op, (((0,), (0,)), ((), ())), preferred_element_type=jnp.float32
    )


def contract_cols(left_op, right_op):
    return lax.dot_general(
        left_op, right_op, (((1,), (1,)), ((), ())), preferred_element_type=jnp.float32
    )


def local(
    tokens,
    per_layer,
    cotangent,
    seq_lengths,
    seq_order,
    qkv_weight,
    out_weight,
    ffn_weights,
    side_weights,
    norm_gains,
):
    tok_rows = tokens.shape[0]
    my_index = lax.axis_index("fsdp")
    token_index = my_index * tok_rows + jnp.arange(tok_rows, dtype=jnp.int32)
    segment, position = layout(seq_lengths, seq_order, token_index)
    cosine, sine = angles(position)
    reach = (WINDOW + tok_rows - 2) // tok_rows
    assert reach == 2
    split_at = PL + RANK
    count = lax.axis_size("fsdp")
    bits = weight_bits(count)
    weight_rows = qkv_weight.shape[0]
    ffn_own = ffn_weights[:, :2].transpose(1, 0, 2)
    (
        qkv_gathered,
        out_gathered,
        ffn_blocks,
        gain_all,
        normed_b,
        projected,
        query_b,
        key_blocks,
        value_blocks,
        mixed_b,
        first_sum,
        normed_two,
    ) = attention_forward(
        jnp.concatenate([qkv_weight, placed_gains(norm_gains, weight_rows)], axis=1),
        jnp.concatenate([out_weight, side_weights], axis=1),
        ffn_own,
        tokens,
        cosine[:, 0, : HD // 2],
        sine[:, 0, : HD // 2],
        position[:, None],
    )
    side_all = out_gathered[:, D:]
    ffn_gain = gain_all[0, D : 2 * D]
    rms_two = inv_rms(first_sum)
    ffn_out, normed_all, gate_kept, up_kept, down_all = ffn_forward(
        normed_two, ffn_weights[:, 2], ffn_own, ffn_blocks
    )
    second_sum = first_sum + ffn_out
    second_b = second_sum.astype(jnp.bfloat16)
    side_in = jnp.dot(second_b, side_all[:, :split_at], preferred_element_type=jnp.float32)
    per_f = per_layer.astype(jnp.float32)
    gelu_per, pull_per = jax.vjp(gelu_tanh, side_in[:, :PL])
    combined = jnp.concatenate(
        [(gelu_per * per_f).astype(jnp.bfloat16), side_in[:, PL:].astype(jnp.bfloat16)], axis=1
    )
    output = (second_sum + contract_cols(combined, side_all[:, split_at:])).astype(jnp.bfloat16)
    back_side = side_all
    grad_y = cotangent.astype(jnp.float32)
    grad_comb = jnp.dot(cotangent, back_side[:, split_at:], preferred_element_type=jnp.float32)
    per_layer_grad = (grad_comb[:, :PL] * gelu_per).astype(jnp.bfloat16)
    grad_per = pull_per(grad_comb[:, :PL] * per_f)[0]
    grad_side = jnp.concatenate([grad_per, grad_comb[:, PL:]], axis=1).astype(jnp.bfloat16)
    grad_two = grad_y + contract_cols(grad_side, back_side[:, :split_at])
    grad_two_b = grad_two.astype(jnp.bfloat16)
    grad_h2, ffn_part, ffn_sent, _ = ffn_backward(
        grad_two_b, normed_all, gate_kept, up_kept, down_all, ffn_own, ffn_blocks
    )
    for bit in reversed(bits[:-1]):
        ffn_part = ffn_part.astype(F32) + swapped(ffn_sent, bit).astype(F32)
        if bit != bits[0]:
            half = ffn_part.shape[1] // 2
            ffn_sent = ffn_part[:, half:].astype(BF16)
            ffn_part = ffn_part[:, :half]
    ffn_grad = ffn_part.transpose(1, 0, 2)
    ffn_gain_grad = jnp.sum(grad_h2 * first_sum * rms_two, axis=0)
    grad_one = grad_two + norm_back(grad_h2, first_sum, rms_two, ffn_gain)
    grad_one_b = grad_one.astype(jnp.bfloat16)
    out_sum, grad_projected, input_grad, attn_gain_grad, head_gain_grad = attention_backward(
        qkv_gathered,
        out_gathered,
        grad_one_b,
        grad_one,
        tokens,
        mixed_b,
        second_b,
        jnp.pad(grad_side, ((0, 0), (0, split_at))),
        cotangent,
        jnp.pad(combined, ((0, 0), (split_at, 0))),
        query_b,
        key_blocks,
        value_blocks,
        projected,
        gain_all,
        cosine[:, 0, : HD // 2],
        sine[:, 0, : HD // 2],
        position[:, None],
    )
    gains_grad_full = jnp.concatenate([attn_gain_grad[0], ffn_gain_grad, head_gain_grad[0]])
    gain_rows = jnp.pad(
        gains_grad_full.astype(BF16).reshape(count, -1),
        ((0, 0), (0, weight_rows * LANES - norm_gains.shape[0])),
    ).reshape(count * weight_rows, LANES)
    qkv_sum = qkv_scatter(gain_rows, normed_b, grad_projected)
    qkv_grad = qkv_sum[:, : qkv_weight.shape[1]]
    gains_grad = qkv_sum[:, qkv_weight.shape[1] :].reshape(-1)[: norm_gains.shape[0]]
    out_grad, side_grad = out_sum[:, :D], out_sum[:, D:]
    return (output, input_grad, per_layer_grad, qkv_grad, out_grad, ffn_grad, side_grad, gains_grad)


def solution(mesh):
    return jax.shard_map(
        local,
        mesh=mesh,
        in_specs=(
            P("fsdp", None),
            P("fsdp", None),
            P("fsdp", None),
            P(),
            P(),
            P("fsdp", None),
            P("fsdp", None),
            P("fsdp", None, None),
            P("fsdp", None),
            P("fsdp"),
        ),
        out_specs=(
            P("fsdp", None),
            P("fsdp", None),
            P("fsdp", None),
            P("fsdp", None),
            P("fsdp", None),
            P("fsdp", None, None),
            P("fsdp", None),
            P("fsdp"),
        ),
        check_vma=False,
    )
```

```python
import functools

import jax
import jax.numpy as jnp
from jax import lax
from jax.experimental import pallas as pl
from jax.experimental.pallas import tpu as pltpu
from jax.sharding import PartitionSpec as P

D = 2048
HQ = 8
KVH = 2
HD = 256
PL = 256
RANK = 64
WINDOW = 512


EPSILON = 1e-06
NEGATIVE = -1e30
ROPE_BASE = 10000.0


PLANE = 8
LANES = 128
MESH = pl.DeviceIdType.MESH
BF16 = jnp.bfloat16
F32 = jnp.float32


def flipped(index, bit):
    return index + bit - 2 * bit * lax.rem(lax.div(index, bit), 2)


def swapped(block, bit):
    route = [(i, i ^ bit) for i in range(lax.axis_size("fsdp"))]
    return lax.ppermute(block, "fsdp", route)


def weight_bits(count):
    return [8] + [1 << i for i in range(5, count.bit_length() - 1)] + [1]


def greet(partners):
    barrier = pltpu.get_barrier_semaphore()
    for partner in partners:
        pl.semaphore_signal(barrier, inc=1, device_id=(partner,), device_id_type=MESH)
    pl.semaphore_wait(barrier, len(partners))


def remote(src, dst, send, recv, device):
    return pltpu.make_async_remote_copy(
        src_ref=src,
        dst_ref=dst,
        send_sem=send,
        recv_sem=recv,
        device_id=(device,),
        device_id_type=MESH,
    )


def half_split(width):
    return (width // LANES + 1) // 2 * LANES


def head_norm(field):
    return lax.rsqrt(jnp.mean(field * field, axis=-1, keepdims=True) + EPSILON)


def turn(field, cosine, sine):
    half = field.shape[1] // 2
    low, high = field[:, :half], field[:, half:]
    return jnp.concatenate([low * cosine - high * sine, high * cosine + low * sine], axis=1)


def gain_spans(count, total):
    per = total // count
    spans = []
    for d in range(count):
        first = per * d // LANES
        last = (per * (d + 1) - 1) // LANES
        spans.append((first, last - first + 1))
    return spans


def placed_gains(norm_gains, rows):
    per = norm_gains.shape[0]
    offset = lax.rem(per * lax.axis_index("fsdp"), LANES)
    return lax.dynamic_update_slice(
        jnp.zeros((rows * LANES,), norm_gains.dtype), norm_gains, (offset,)
    ).reshape(rows, LANES)


def soft_rows(query, keys, reach, gap):
    scores = dot_nt(query, keys) * HD ** (-0.5)
    scores = jnp.where((gap >= 0) & (gap <= reach), scores, NEGATIVE)
    exponent = jnp.exp(scores - jnp.max(scores, axis=-1, keepdims=True))
    return exponent / jnp.sum(exponent, axis=-1, keepdims=True)


class WeightGather:
    def __init__(self, chain, pairs):
        me = lax.axis_index("fsdp")
        core, x_at, y_at = lax.rem(me, 2), lax.rem(lax.div(me, 2), 2), lax.rem(lax.div(me, 4), 2)
        z_at = lax.div(me, PLANE)
        next_x, next_y, next_c = flipped(me, 2), flipped(me, 4), flipped(me, 1)
        z_peers = [me + (lax.rem(z_at + s, chain) - z_at) * PLANE for s in range(1, chain)]
        self.partners = [next_x, next_y, next_c] + z_peers
        self.order = sorted(range(chain), key=lambda s: (min(s, chain - s), s))
        self.waves = []
        for own, out, (local, zs, zr, xs, xr, ys, yr, a_s, ar, bs, br, cs, cr) in pairs:
            cut = half_split(own.shape[-1])
            left, right = pl.ds(0, cut), pl.ds(cut, own.shape[-1] - cut)
            ops = {"own": pltpu.make_async_copy(own, out.at[z_at, y_at, x_at, core], local)}
            ops["z"] = [None] + [
                remote(own, out.at[z_at, y_at, x_at, core], zs.at[s], zr.at[s], z_peers[s - 1])
                for s in self.order[1:]
            ]
            steps = []
            for s in self.order:
                k = lax.rem(z_at + chain - s, chain)
                here = out.at[k, y_at, x_at, core]
                src = own if s == 0 else here
                from_x = out.at[k, y_at, 1 - x_at, core]
                from_y = out.at[k, 1 - y_at, x_at, core]
                column = out.at[k, :, :, core]
                steps.append(
                    {
                        "x": remote(src, here, xs.at[s], xr.at[s], next_x),
                        "y": remote(src, here, ys.at[s], yr.at[s], next_y),
                        "a": remote(
                            from_x.at[:, left], from_x.at[:, left], a_s.at[s], ar.at[s], next_y
                        ),
                        "b": remote(
                            from_y.at[:, right], from_y.at[:, right], bs.at[s], br.at[s], next_x
                        ),
                        "c": remote(column, column, cs.at[s], cr.at[s], next_c),
                    }
                )
            ops["steps"] = steps
            self.waves.append(ops)

    def spread(self, w, s):
        ops = self.waves[w]
        if s == 0:
            ops["own"].start()
        else:
            ops["z"][s].wait_recv()
        if w == 0 and s + 1 < len(ops["z"]):
            ops["z"][s + 1].start()
        if w > 0 and s == 0:
            for copy in ops["z"][1:]:
                copy.start()
        ops["steps"][s]["x"].start()
        ops["steps"][s]["y"].start()

    def pass_on(self, w, s):
        step = self.waves[w]["steps"][s]
        step["x"].wait_recv()
        step["a"].start()
        step["y"].wait_recv()
        step["b"].start()

    def across(self, w, s):
        step = self.waves[w]["steps"][s]
        step["a"].wait_recv()
        step["b"].wait_recv()
        if s == 0:
            self.waves[w]["own"].wait()
        step["c"].start()

    def complete(self, w):
        for step in self.waves[w]["steps"]:
            step["c"].wait_recv()

    def drain(self):
        for ops in self.waves:
            for copy in ops["z"][1:]:
                copy.wait_send()
            for step in ops["steps"]:
                for name in "xyabc":
                    step[name].wait_send()


def attention_forward_kernel(
    count,
    own_a,
    own_b,
    own_ffn,
    tokens,
    cosine,
    sine,
    position,
    full_a,
    full_b,
    full_ffn,
    normed_out,
    projected_out,
    query_out,
    key_out,
    value_out,
    gains,
    mixed,
    first_sum,
    normed_two,
    wa,
    wb,
    normed,
    projected,
    query,
    key_rows,
    value_rows,
    *sems,
):
    me = lax.axis_index("fsdp")
    chain = count // PLANE
    bits = weight_bits(count)
    gather = WeightGather(chain, ((own_a, wa, sems[:13]), (own_b, wb, sems[13:26])))
    first_s, first_r, ffn_s, ffn_r, rest_s, rest_r, halo_s, halo_r, save, early = sems[26:]
    ahead = [lax.rem(me + d, count) for d in (1, 2)]
    behind = [lax.rem(me + count - d, count) for d in (1, 2)]
    greet(gather.partners + [flipped(me, bit) for bit in bits[:-1]] + ahead + behind)
    ffn_first, ffn_copies, ffn_rest = [], [], []
    piece = own_ffn.shape[1] // FFN_PIECES
    for j in range(2 * FFN_PIECES):
        at = pl.ds(j % FFN_PIECES * piece, piece)
        m = j // FFN_PIECES
        ffn_first.append(
            remote(
                own_ffn.at[m, at],
                full_ffn.at[1, m, at],
                first_s.at[j],
                first_r.at[j],
                flipped(me, bits[0]),
            )
        )
    for i, bit in enumerate(bits[1:]):
        size, partner = 2 << i, flipped(me, bit)
        ffn_copies.append(remote(own_ffn, full_ffn.at[size], ffn_s.at[i], ffn_r.at[i], partner))
        ffn_rest.append(
            remote(
                full_ffn.at[pl.ds(1, size - 1)],
                full_ffn.at[pl.ds(size + 1, size - 1)],
                rest_s.at[i],
                rest_r.at[i],
                partner,
            )
        )
    halo = []
    for d in (1, 2):
        for j, rows in enumerate((key_rows, value_rows)):
            at = 2 * (d - 1) + j
            halo.append(
                remote(rows.at[2], rows.at[2 - d], halo_s.at[at], halo_r.at[at], ahead[d - 1])
            )
    for s in range(chain):
        gather.spread(0, s)
        if s >= 1:
            gather.pass_on(0, s - 1)
        if s >= 2:
            gather.across(0, s - 2)
    gather.spread(1, 0)
    for copy in ffn_first + ffn_copies:
        copy.start()
    gather.pass_on(0, chain - 1)
    gather.across(0, chain - 2)
    gather.across(0, chain - 1)
    gather.complete(0)
    for s in range(1, chain):
        gather.spread(1, s)
    keep_a = pltpu.make_async_copy(wa, full_a, save.at[0])
    keep_a.start()

    width_a, per = QKV_WIDTH, gains.shape[1] // count
    spans = gain_spans(count, gains.shape[1])
    pieces = {}
    for d, (first, n_rows) in enumerate(spans):
        block = wa[
            d // PLANE, d // 4 % 2, d // 2 % 2, d % 2, 0:16, width_a : width_a + LANES
        ].astype(F32)
        for r in range(n_rows):
            pieces.setdefault(first + r, []).append(block[r : r + 1])
    for t, terms in pieces.items():
        total = terms[0]
        for term in terms[1:]:
            total = total + term
        gains[:, t * LANES : (t + 1) * LANES] = total

    rows, depth = tokens.shape

    @pl.loop(0, rows // 32)
    def _(i):
        at = pl.ds(pl.multiple_of(i * 32, 32), 32)
        field = tokens[at].astype(F32)
        normed[at] = (field * head_norm(field) * gains[:, :depth]).astype(BF16)

    def project(n):
        at = pl.ds(pl.multiple_of(n * 512, 512), 512)
        weight = wa[:, :, :, :, :, at].reshape(depth, 512)
        projected[:, at] = jnp.dot(normed[...], weight, preferred_element_type=F32)

    query_width = HQ * HD
    kv_width = KVH * HD

    @pl.loop(query_width // 512, (query_width + 2 * kv_width) // 512)
    def _(n):
        project(n)

    for g in range(KVH):
        at = slice(query_width + g * HD, query_width + (g + 1) * HD)
        field = projected[:, at]
        key_gain = gains[:, 2 * depth + HD :]
        key_rows[2, :, g * HD : (g + 1) * HD] = turn(
            field * head_norm(field) * key_gain, cosine[...], sine[...]
        ).astype(BF16)
    value_rows[2] = projected[:, query_width + kv_width :].astype(BF16)
    for copy in halo:
        copy.start()
    for s in range(chain - 3):
        gather.pass_on(1, s)

    @pl.loop(0, query_width // 512)
    def _(n):
        project(n)

    gather.pass_on(1, chain - 3)
    for s in range(chain - 3):
        gather.across(1, s)

    @pl.loop(0, HQ)
    def _(h):
        at = pl.ds(pl.multiple_of(h * HD, HD), HD)
        field = projected[:, at]
        query_gain = gains[:, 2 * depth : 2 * depth + HD]
        query[:, at] = turn(
            field * head_norm(field) * query_gain, cosine[...], sine[...]
        ).astype(BF16)

    gather.pass_on(1, chain - 2)
    gather.across(1, chain - 3)
    for copy in halo:
        copy.wait_recv()
    early_saves = [
        pltpu.make_async_copy(src, dst, early.at[i])
        for i, (src, dst) in enumerate(
            (
                (normed, normed_out),
                (projected, projected_out),
                (query, query_out),
                (key_rows, key_out),
                (value_rows, value_out),
            )
        )
    ]
    for copy in early_saves:
        copy.start()
    n_keys = 3 * rows
    gap = (
        lax.broadcasted_iota(jnp.int32, (rows, n_keys), 0)
        - lax.broadcasted_iota(jnp.int32, (rows, n_keys), 1)
        + 2 * rows
    )
    reach = jnp.minimum(position[...], WINDOW - 1)

    def heads(first, last):
        @pl.loop(first, last)
        def _(h):
            at = pl.ds(pl.multiple_of(h * HD, HD), HD)
            group = pl.ds(pl.multiple_of(lax.div(h, HQ // KVH) * HD, HD), HD)
            keys = key_rows[:, :, group].reshape(n_keys, HD)
            values = value_rows[:, :, group].reshape(n_keys, HD)
            probs = soft_rows(query[:, at], keys, reach, gap).astype(BF16)
            mixed[:, at] = jnp.dot(probs, values, preferred_element_type=F32).astype(BF16)

    heads(0, 1)
    gather.pass_on(1, chain - 1)
    heads(1, 2)
    gather.across(1, chain - 2)
    heads(2, 4)
    gather.across(1, chain - 1)
    heads(4, 8)
    gather.complete(1)
    keep_b = pltpu.make_async_copy(wb, full_b, save.at[1])
    keep_b.start()

    @pl.loop(0, depth // 512)
    def _(n):
        at = pl.ds(pl.multiple_of(n * 512, 512), 512)
        weight = wb[:, :, :, :, :, at].reshape(depth, 512)
        first_sum[:, at] = tokens[:, at].astype(F32) + jnp.dot(
            mixed[...], weight, preferred_element_type=F32
        )

    @pl.loop(0, rows // 32)
    def _(i):
        at = pl.ds(pl.multiple_of(i * 32, 32), 32)
        field = first_sum[at]
        normed_two[at] = (field * head_norm(field) * gains[:, depth : 2 * depth]).astype(BF16)

    for copy in ffn_first:
        copy.wait_recv()
    for copy, rest in zip(ffn_copies, ffn_rest):
        rest.start()
        copy.wait_recv()
        rest.wait_recv()
    for copy in ffn_first + ffn_copies + ffn_rest + halo:
        copy.wait_send()
    gather.drain()
    for copy in early_saves + [keep_a, keep_b]:
        copy.wait()


FFN_PIECES = 2
QKV_WIDTH = (HQ + 2 * KVH) * HD


def attention_forward(own_a, own_b, own_ffn, tokens, cosine, sine, position):
    count = lax.axis_size("fsdp")
    chain = count // PLANE
    rows, depth = tokens.shape
    n_blocks = 1 << len(weight_bits(count))
    dma = pltpu.SemaphoreType.DMA
    anywhere, vmem = pl.BlockSpec(memory_space=pl.ANY), pl.BlockSpec(memory_space=pltpu.VMEM)
    shape_a, shape_b = ((chain, 2, 2, 2) + own.shape for own in (own_a, own_b))
    kept = [
        jax.ShapeDtypeStruct((rows, depth), BF16),
        jax.ShapeDtypeStruct((rows, QKV_WIDTH), F32),
        jax.ShapeDtypeStruct((rows, HQ * HD), BF16),
        jax.ShapeDtypeStruct((3, rows, KVH * HD), BF16),
        jax.ShapeDtypeStruct((3, rows, KVH * HD), BF16),
    ]
    full_a, full_b, *rest = pl.pallas_call(
        functools.partial(attention_forward_kernel, count),
        out_shape=[
            jax.ShapeDtypeStruct(shape_a, BF16),
            jax.ShapeDtypeStruct(shape_b, BF16),
            jax.ShapeDtypeStruct((n_blocks,) + own_ffn.shape, BF16),
            *kept,
            jax.ShapeDtypeStruct((1, 2 * depth + 2 * HD), F32),
            jax.ShapeDtypeStruct((rows, HQ * HD), BF16),
            jax.ShapeDtypeStruct((rows, depth), F32),
            jax.ShapeDtypeStruct((rows, depth), BF16),
        ],
        in_specs=[anywhere] * 3 + [vmem] * 4,
        out_specs=[anywhere] * 8 + [vmem] * 4,
        scratch_shapes=[pltpu.VMEM(shape_a, BF16), pltpu.VMEM(shape_b, BF16)]
        + [pltpu.VMEM(array.shape, array.dtype) for array in kept]
        + ([dma] + [dma((chain,))] * 12) * 2
        + [dma((2 * FFN_PIECES,))] * 2
        + [dma((len(weight_bits(count)) - 1,))] * 4
        + [dma((4,)), dma((4,)), dma((2,)), dma((len(kept),))],
        compiler_params=pltpu.CompilerParams(
            collective_id=0, has_side_effects=True, vmem_limit_bytes=58 * 2**20
        ),
        name="attention_forward",
    )(own_a, own_b, own_ffn, tokens, cosine, sine, position)
    return (full_a.reshape(-1, own_a.shape[1]), full_b.reshape(-1, own_b.shape[1]), *rest)


def add_into(target, *terms):
    rows = target.shape[0]
    tile = 16

    @pl.loop(0, rows // tile)
    def _(i):
        at = pl.ds(pl.multiple_of(i * tile, tile), tile)
        if len(terms) == 1:
            target[at] = target[at] + terms[0][at]
        else:
            total = target[at].astype(F32)
            for term in terms:
                total = total + term[at].astype(F32)
            target[at] = total.astype(target.dtype)


class WeightScatter:
    def __init__(self, chain, part, out, sibling, in_a, in_b, in_x, in_y, in_z, *sems):
        cs, cr, a_s, ar, bs, br, xs, xr, ys, yr, zs, zr = sems
        me = lax.axis_index("fsdp")
        core, x_at, y_at = lax.rem(me, 2), lax.rem(lax.div(me, 2), 2), lax.rem(lax.div(me, 4), 2)
        z_at = lax.div(me, PLANE)
        next_x, next_y, next_c = flipped(me, 2), flipped(me, 4), flipped(me, 1)
        z_peers = [me + (lax.rem(z_at + s, chain) - z_at) * PLANE for s in range(1, chain)]
        self.partners = [next_x, next_y, next_c] + z_peers
        self.chain, self.out, self.in_z = chain, out, in_z
        cut = half_split(out.shape[-1])
        left, right = pl.ds(0, cut), pl.ds(cut, out.shape[-1] - cut)
        self.left, self.right = left, right
        self.order = list(range(1, chain)) + [0]
        self.blocks = [lax.rem(z_at + s, chain) for s in range(chain)]
        self.steps = []
        for s in range(chain):
            mine = part.at[s, :, :, core]
            step = {
                "mine": [part.at[s, j // 2, j % 2, core] for j in range(4)],
                "sibling": [sibling.at[s, j // 2, j % 2] for j in range(4)],
                "in": (in_a.at[s], in_b.at[s], in_x.at[s], in_y.at[s]),
                "here": part.at[s, y_at, x_at, core],
                "to_x": part.at[s, y_at, 1 - x_at, core],
                "to_y": part.at[s, 1 - y_at, x_at, core],
                "c": remote(
                    part.at[s, :, :, 1 - core], sibling.at[s], cs.at[s], cr.at[s], next_c
                ),
            }
            corner = part.at[s, 1 - y_at, 1 - x_at, core]
            step["a"] = remote(corner.at[:, left], in_a.at[s], a_s.at[s], ar.at[s], next_x)
            step["b"] = remote(corner.at[:, right], in_b.at[s], bs.at[s], br.at[s], next_y)
            step["x"] = remote(step["to_x"], in_x.at[s], xs.at[s], xr.at[s], next_x)
            step["y"] = remote(step["to_y"], in_y.at[s], ys.at[s], yr.at[s], next_y)
            if s > 0:
                step["z"] = remote(
                    step["here"], in_z.at[s - 1], zs.at[s - 1], zr.at[s - 1], z_peers[s - 1]
                )
            self.steps.append(step)

    def cross(self, i):
        self.steps[self.order[i]]["c"].start()

    def halve(self, i):
        step = self.steps[self.order[i]]
        step["c"].wait_recv()
        for mine, sibling in zip(step["mine"], step["sibling"]):
            add_into(mine, sibling)
        step["a"].start()
        step["b"].start()

    def sideways(self, i):
        step = self.steps[self.order[i]]
        in_a, in_b, _, _ = step["in"]
        step["a"].wait_recv()
        add_into(step["to_y"].at[:, self.left], in_a)
        step["y"].start()
        step["b"].wait_recv()
        add_into(step["to_x"].at[:, self.right], in_b)
        step["x"].start()

    def finish(self, i):
        step = self.steps[self.order[i]]
        step["x"].wait_recv()
        step["y"].wait_recv()
        add_into(step["here"], *step["in"][2:])
        if "z" in step:
            step["z"].start()

    def total(self):
        for step in self.steps[1:]:
            step["z"].wait_recv()

        @pl.loop(0, self.out.shape[0] // 16)
        def _(i):
            at = pl.ds(pl.multiple_of(i * 16, 16), 16)
            total = self.steps[0]["here"][at].astype(F32)
            for s in range(self.chain - 1):
                total = total + self.in_z[s, at].astype(F32)
            self.out[at] = total

        for step in self.steps:
            for name in "cabxyz":
                if name in step:
                    step[name].wait_send()


def scatter_scratch(chain, rows, width):
    cut = half_split(width)
    shapes = [
        (chain, 2, 2, 2, rows, width),
        (chain, 2, 2, rows, width),
        (chain, rows, cut),
        (chain, rows, width - cut),
        (chain, rows, width),
        (chain, rows, width),
        (chain - 1, rows, width),
    ]
    return [pltpu.VMEM(shape, BF16) for shape in shapes] + [
        pltpu.SemaphoreType.DMA((chain,))
    ] * 12


def turn_back(grad, cosine, sine):
    half = grad.shape[1] // 2
    low, high = grad[:, :half], grad[:, half:]
    return jnp.concatenate([low * cosine + high * sine, high * cosine - low * sine], axis=1)


def head_back(grad_rot, field, gain, cosine, sine):
    grad = turn_back(grad_rot, cosine, sine)
    scale = head_norm(field)
    weighted = grad * gain
    back = scale * weighted - field * (
        scale * scale * scale * jnp.mean(weighted * field, axis=-1, keepdims=True)
    )
    return back, jnp.sum(grad * field * scale, axis=0, keepdims=True)


def attention_backward_kernel(
    count,
    full_a,
    full_b,
    grad_one_in,
    tokens_in,
    query_in,
    key_in,
    value_in,
    projected_in,
    grad_one_b,
    mixed,
    second,
    grad_side,
    cotangent,
    combined,
    gains,
    cosine,
    sine,
    position,
    out_sum,
    grad_projected,
    input_grad,
    attn_gain_grad,
    head_gain_grad,
    weight,
    grad_mixed,
    grad_normed,
    grad_keys,
    grad_values,
    halo_out,
    halo_in,
    grad_one,
    tokens,
    query,
    key_rows,
    value_rows,
    projected,
    weight_sem,
    fill_sem,
    halo_s,
    halo_r,
    part,
    *scratch,
):
    me = lax.axis_index("fsdp")
    chain = count // PLANE
    scatter = WeightScatter(chain, part, out_sum, *scratch)
    ahead = [lax.rem(me + d, count) for d in (1, 2)]
    behind = [lax.rem(me + count - d, count) for d in (1, 2)]
    greet(scatter.partners + ahead + behind)
    rows, depth = tokens.shape
    query_width, kv_width = HQ * HD, KVH * HD
    out_width = depth
    load_out = pltpu.make_async_copy(
        full_b.at[:, :, :, :, :, pl.ds(0, out_width)],
        weight.at[:, :, :, :, :, pl.ds(0, out_width)],
        weight_sem,
    )
    load_out.start()
    fills = [
        pltpu.make_async_copy(src, dst, fill_sem.at[i])
        for i, (src, dst) in enumerate(
            (
                (query_in, query),
                (key_in, key_rows),
                (value_in, value_rows),
                (projected_in, projected),
                (tokens_in, tokens),
                (grad_one_in, grad_one),
            )
        )
    ]
    for fill in fills:
        fill.start()
    tile = depth // chain
    block_shape = part.shape[1:5]
    for i, s in enumerate(scatter.order):
        columns = pl.ds(pl.multiple_of(scatter.blocks[s] * tile, tile), tile)
        left = mixed[:, columns]

        @pl.loop(0, out_width // 512)
        def _(n):
            at = pl.ds(pl.multiple_of(n * 512, 512), 512)
            part[s, :, :, :, :, at] = (
                dot_tn(left, grad_one_b[:, at]).astype(BF16).reshape(block_shape + (512,))
            )

        side = dot_tn(second[:, columns], grad_side[...])
        side = side + dot_tn(cotangent[:, columns], combined[...])
        part[s, :, :, :, :, out_width:] = side.astype(BF16).reshape(
            block_shape + (part.shape[-1] - out_width,)
        )
        scatter.cross(i)
        if i >= 1:
            scatter.halve(i - 1)
        if i >= 3:
            scatter.sideways(i - 3)
        if i >= 5:
            scatter.finish(i - 5)
    load_out.wait()

    @pl.loop(0, chain)
    def _(k):
        at = pl.ds(pl.multiple_of(k * tile, tile), tile)
        grad_mixed[:, at] = dot_nt(
            grad_one_b[...], weight[k, :, :, :, :, 0:out_width].reshape(tile, out_width)
        ).astype(BF16)

    load_qkv = pltpu.make_async_copy(
        full_a.at[:, :, :, :, :, pl.ds(0, QKV_WIDTH)], weight, weight_sem
    )
    load_qkv.start()
    grad_keys[...] = jnp.zeros_like(grad_keys)
    grad_values[...] = jnp.zeros_like(grad_values)
    head_gain_grad[...] = jnp.zeros_like(head_gain_grad)
    n_keys = 3 * rows
    gap = (
        lax.broadcasted_iota(jnp.int32, (rows, n_keys), 0)
        - lax.broadcasted_iota(jnp.int32, (rows, n_keys), 1)
        + 2 * rows
    )
    reach = jnp.minimum(position[...], WINDOW - 1)
    query_gain = gains[:, 2 * depth : 2 * depth + HD]
    key_gain = gains[:, 2 * depth + HD :]
    scale = HD ** (-0.5)

    def heads(first, last):
        @pl.loop(first, last)
        def _(h):
            at = pl.ds(pl.multiple_of(h * HD, HD), HD)
            group = pl.ds(pl.multiple_of(lax.div(h, HQ // KVH) * HD, HD), HD)
            keys = key_rows[:, :, group].reshape(n_keys, HD)
            values = value_rows[:, :, group].reshape(n_keys, HD)
            probs = soft_rows(query[:, at], keys, reach, gap)
            grad_probs = dot_nt(grad_mixed[:, at], values)
            delta = jnp.sum(probs * grad_probs, axis=-1, keepdims=True)
            grad_scores = (probs * (grad_probs - delta)).astype(BF16)
            grad_rot = jnp.dot(grad_scores, keys, preferred_element_type=F32) * scale
            grad_keys[:, :, group] += (dot_tn(grad_scores, query[:, at]) * scale).reshape(
                3, rows, HD
            )
            grad_values[:, :, group] += dot_tn(probs.astype(BF16), grad_mixed[:, at]).reshape(
                3, rows, HD
            )
            back, gain_grad = head_back(
                grad_rot, projected[:, at], query_gain, cosine[...], sine[...]
            )
            grad_projected[:, at] = back.astype(BF16)
            head_gain_grad[:, 0:HD] += gain_grad

    halo = []

    def send_back(g):
        at = slice(g * HD, (g + 1) * HD)
        lanes = pl.ds(g * HD, HD)
        for d in (2, 1):
            for j, grad in enumerate((grad_keys, grad_values)):
                slot = 2 * (d - 1) + j
                halo_out[slot, :, at] = grad[2 - d, :, at].astype(BF16)
                halo.append(
                    remote(
                        halo_out.at[slot, :, lanes],
                        halo_in.at[slot, :, lanes],
                        halo_s.at[g, slot],
                        halo_r.at[g, slot],
                        behind[d - 1],
                    )
                )
                halo[-1].start()

    last = chain - 1
    scatter.sideways(last - 2)
    if chain > 4:
        scatter.finish(last - 4)
    scatter.halve(last)
    for fill in fills:
        fill.wait()
    heads(0, 1)
    scatter.sideways(last - 1)
    scatter.finish(last - 3)
    heads(1, 3)
    scatter.sideways(last)
    scatter.finish(last - 2)
    heads(3, 4)
    send_back(0)
    heads(4, 6)
    scatter.finish(last - 1)
    heads(6, 8)
    send_back(1)
    load_qkv.wait()

    @pl.loop(0, chain)
    def _(k):
        at = pl.ds(pl.multiple_of(k * tile, tile), tile)
        grad_normed[:, at] = dot_nt(
            grad_projected[:, 0:query_width],
            weight[k, :, :, :, :, 0:query_width].reshape(tile, query_width),
        )

    for copy in halo:
        copy.wait_recv()
    for g in range(KVH):
        at = slice(g * HD, (g + 1) * HD)
        place = slice(query_width + g * HD, query_width + (g + 1) * HD)
        grad_rot = (
            grad_keys[2, :, at] + halo_in[0, :, at].astype(F32) + halo_in[2, :, at].astype(F32)
        )
        back, gain_grad = head_back(
            grad_rot, projected[:, place], key_gain, cosine[...], sine[...]
        )
        grad_projected[:, place] = back.astype(BF16)
        head_gain_grad[:, HD : 2 * HD] += gain_grad
    grad_projected[:, query_width + kv_width :] = (
        grad_values[2] + halo_in[1].astype(F32) + halo_in[3].astype(F32)
    ).astype(BF16)

    @pl.loop(0, chain)
    def _(k):
        at = pl.ds(pl.multiple_of(k * tile, tile), tile)
        grad_normed[:, at] += dot_nt(
            grad_projected[:, query_width:],
            weight[k, :, :, :, :, query_width:].reshape(tile, 2 * kv_width),
        )

    attn_gain_grad[...] = jnp.zeros_like(attn_gain_grad)
    attn_gain = gains[:, :depth]

    @pl.loop(0, rows // 16)
    def _(i):
        at = pl.ds(pl.multiple_of(i * 16, 16), 16)
        field = tokens[at].astype(F32)
        rms = head_norm(field)
        grad = grad_normed[at]
        weighted = grad * attn_gain
        back = rms * weighted - field * (
            rms * rms * rms * jnp.mean(weighted * field, axis=-1, keepdims=True)
        )
        input_grad[at] = (grad_one[at] + back).astype(BF16)
        attn_gain_grad[...] += jnp.sum(grad * field * rms, axis=0, keepdims=True)

    scatter.finish(last)
    scatter.total()
    for copy in halo:
        copy.wait_send()


def attention_backward(
    full_a,
    full_b,
    grad_one_b,
    grad_one,
    tokens,
    mixed,
    second,
    grad_side,
    cotangent,
    combined,
    query,
    key_rows,
    value_rows,
    projected,
    gains,
    cosine,
    sine,
    position,
):
    count = lax.axis_size("fsdp")
    chain = count // PLANE
    rows, depth = tokens.shape
    weight_rows, out_width = full_b.shape[0] // count, full_b.shape[1]
    dma = pltpu.SemaphoreType.DMA
    anywhere, vmem = pl.BlockSpec(memory_space=pl.ANY), pl.BlockSpec(memory_space=pltpu.VMEM)
    blocked = [
        array.reshape(chain, 2, 2, 2, weight_rows, array.shape[1])
        for array in (full_a, full_b)
    ]
    kv_width = KVH * HD
    filled = (grad_one, tokens, query, key_rows, value_rows, projected)
    return pl.pallas_call(
        functools.partial(attention_backward_kernel, count),
        out_shape=[
            jax.ShapeDtypeStruct((weight_rows, out_width), F32),
            jax.ShapeDtypeStruct((rows, QKV_WIDTH), BF16),
            jax.ShapeDtypeStruct((rows, depth), BF16),
            jax.ShapeDtypeStruct((1, depth), F32),
            jax.ShapeDtypeStruct((1, 2 * HD), F32),
        ],
        in_specs=[anywhere] * 8 + [vmem] * 10,
        out_specs=[vmem] * 5,
        scratch_shapes=[
            pltpu.VMEM((chain, 2, 2, 2, weight_rows, QKV_WIDTH), BF16),
            pltpu.VMEM((rows, HQ * HD), BF16),
            pltpu.VMEM((rows, depth), F32),
            pltpu.VMEM((3, rows, kv_width), F32),
            pltpu.VMEM((3, rows, kv_width), F32),
            pltpu.VMEM((4, rows, kv_width), BF16),
            pltpu.VMEM((4, rows, kv_width), BF16),
            *(
                pltpu.VMEM(array.shape, array.dtype)
                for array in filled
            ),
            dma,
            dma((len(filled),)),
            dma((KVH, 4)),
            dma((KVH, 4)),
        ]
        + scatter_scratch(chain, weight_rows, out_width),
        compiler_params=pltpu.CompilerParams(
            collective_id=1, has_side_effects=True, vmem_limit_bytes=62 * 2**20
        ),
        cost_estimate=pl.CostEstimate(
            flops=40 * 10**9, bytes_accessed=180 * 2**20, transcendentals=0
        ),
        name="attention_backward",
    )(
        *blocked,
        grad_one,
        tokens,
        query,
        key_rows,
        value_rows,
        projected,
        grad_one_b,
        mixed,
        second,
        grad_side,
        cotangent,
        combined,
        gains,
        cosine,
        sine,
        position,
    )


def qkv_scatter_kernel(count, gain_part, normed, grad_projected, out_sum, gain_sem, part, *scratch):
    chain = count // PLANE
    scatter = WeightScatter(chain, part, out_sum, *scratch)
    greet(scatter.partners)
    width = grad_projected.shape[1]
    places = []
    for s in range(chain):
        places.append(
            pltpu.make_async_copy(
                gain_part.at[scatter.blocks[s]],
                part.at[s, :, :, :, :, pl.ds(width, LANES)],
                gain_sem.at[s],
            )
        )
        places[-1].start()
    tile = normed.shape[1] // chain
    block_shape = part.shape[1:5]
    for i in range(chain + 3):
        if i < chain:
            s = scatter.order[i]
            left = normed[:, pl.ds(pl.multiple_of(scatter.blocks[s] * tile, tile), tile)]

            @pl.loop(0, width // 512)
            def _(n):
                at = pl.ds(pl.multiple_of(n * 512, 512), 512)
                part[s, :, :, :, :, at] = (
                    dot_tn(left, grad_projected[:, at]).astype(BF16).reshape(block_shape + (512,))
                )

            places[s].wait()
            scatter.cross(i)
        if 1 <= i <= chain:
            scatter.halve(i - 1)
        if 2 <= i <= chain + 1:
            scatter.sideways(i - 2)
        if i >= 3:
            scatter.finish(i - 3)
    scatter.total()


def qkv_scatter(gain_part, normed, grad_projected):
    count = lax.axis_size("fsdp")
    chain = count // PLANE
    weight_rows, width = normed.shape[1] // count, grad_projected.shape[1] + LANES
    vmem = pl.BlockSpec(memory_space=pltpu.VMEM)
    return pl.pallas_call(
        functools.partial(qkv_scatter_kernel, count),
        out_shape=jax.ShapeDtypeStruct((weight_rows, width), F32),
        in_specs=[pl.BlockSpec(memory_space=pl.ANY)] + [vmem] * 2,
        out_specs=vmem,
        scratch_shapes=[pltpu.SemaphoreType.DMA((chain,))]
        + scatter_scratch(chain, weight_rows, width),
        compiler_params=pltpu.CompilerParams(
            collective_id=4, has_side_effects=True, vmem_limit_bytes=48 * 2**20
        ),
        cost_estimate=pl.CostEstimate(
            flops=40 * 10**9, bytes_accessed=180 * 2**20, transcendentals=0
        ),
        name="qkv_scatter",
    )(gain_part.reshape(chain, 2, 2, 2, weight_rows, LANES), normed, grad_projected)


class TokenCube:
    def __init__(self, own, held, part, in_half, in_x, in_y, in_z, gs, gr, ss, sr):
        me = lax.axis_index("fsdp")
        next_x, next_y, next_z = (flipped(me, bit) for bit in TOKEN_BITS)
        self.partners = [next_x, next_y, next_z]
        half = own.shape[0] // 2
        top, low = pl.ds(0, half), pl.ds(half, half)
        self.top, self.low = top, low
        plan = {
            "zt": (own.at[top], held.at[4, top], next_z),
            "zl": (own.at[low], held.at[4, low], next_z),
            "x": (own, held.at[1], next_x),
            "y": (own, held.at[2], next_y),
            "dt": (held.at[1, top], held.at[3, top], next_y),
            "dl": (held.at[2, low], held.at[3, low], next_x),
            "xt": (held.at[4, top], held.at[5, top], next_x),
            "yt": (held.at[4, top], held.at[6, top], next_y),
            "xl": (held.at[4, low], held.at[5, low], next_x),
            "yl": (held.at[4, low], held.at[6, low], next_y),
            "et": (held.at[5, top], held.at[7, top], next_y),
            "el": (held.at[6, low], held.at[7, low], next_x),
        }
        self.gather = {
            name: remote(src, dst, gs.at[i], gr.at[i], device)
            for i, (name, (src, dst, device)) in enumerate(plan.items())
        }
        self.part, self.in_half, self.in_x, self.in_y, self.in_z = part, in_half, in_x, in_y, in_z
        self.waves = []
        side = own.shape[1] // 2
        for w, (base, first) in enumerate(((4, 0), (4, side), (0, 0), (0, side))):
            at = pl.ds(first, side)
            corner = part.at[base + 3, :, at]
            to_x, to_y = part.at[base + 1, :, at], part.at[base + 2, :, at]
            here = part.at[base, :, at]
            wave = {
                "a": remote(corner.at[top], in_half.at[w, 0], ss.at[w, 0], sr.at[w, 0], next_x),
                "b": remote(corner.at[low], in_half.at[w, 1], ss.at[w, 1], sr.at[w, 1], next_y),
                "x": remote(to_x, in_x.at[w], ss.at[w, 2], sr.at[w, 2], next_x),
                "y": remote(to_y, in_y.at[w], ss.at[w, 3], sr.at[w, 3], next_y),
            }
            if base:
                wave["z"] = remote(here, in_z.at[w], ss.at[w, 4], sr.at[w, 4], next_z)
            self.waves.append((wave, at, to_x, to_y, here))

    def start(self, *names):
        for name in names:
            self.gather[name].start()

    def arrive(self, *names):
        for name in names:
            self.gather[name].wait_recv()

    def corners(self, w):
        wave = self.waves[w][0]
        wave["a"].start()
        wave["b"].start()

    def sideways(self, w):
        wave, _, to_x, to_y, _ = self.waves[w]
        wave["a"].wait_recv()
        add_into(to_y.at[self.top], self.in_half.at[w, 0])
        wave["y"].start()
        wave["b"].wait_recv()
        add_into(to_x.at[self.low], self.in_half.at[w, 1])
        wave["x"].start()

    def across(self, w):
        wave, _, _, _, here = self.waves[w]
        wave["x"].wait_recv()
        wave["y"].wait_recv()
        add_into(here, self.in_x.at[w], self.in_y.at[w])
        wave["z"].start()

    def finish(self, out):
        for w in (2, 3):
            wave, side = self.waves[w][:2]
            wave["x"].wait_recv()
            wave["y"].wait_recv()
            self.waves[w - 2][0]["z"].wait_recv()

            @pl.loop(0, out.shape[0] // 16)
            def _(i):
                at = pl.ds(pl.multiple_of(i * 16, 16), 16)
                out[at, side] = (
                    self.part[0, at, side].astype(F32)
                    + self.in_x[w, at].astype(F32)
                    + self.in_y[w, at].astype(F32)
                    + self.in_z[w - 2, at].astype(F32)
                )

        for copy in self.gather.values():
            copy.wait_send()
        for wave, *_ in self.waves:
            for copy in wave.values():
                copy.wait_send()


TOKEN_BITS = (2, 4, 16)
ORDER = (0, 1, 2, 4, 5, 6, 7, 3)


def cube_scratch(rows, width):
    dma = pltpu.SemaphoreType.DMA
    return [
        pltpu.VMEM((8, rows, width), BF16),
        pltpu.VMEM((8, rows, width), BF16),
        pltpu.VMEM((4, 2, rows // 2, width // 2), BF16),
        pltpu.VMEM((4, rows, width // 2), BF16),
        pltpu.VMEM((4, rows, width // 2), BF16),
        pltpu.VMEM((2, rows, width // 2), BF16),
        dma((12,)),
        dma((12,)),
        dma((4, 5)),
        dma((4, 5)),
        dma,
    ]


def load_weights(own, blocks, held, sems):
    rows = blocks.shape[2]
    loads = []
    for m in range(2):
        for i in range(blocks.shape[0]):
            loads.append(
                pltpu.make_async_copy(
                    own.at[m] if i == 0 else blocks.at[i, m],
                    held.at[m, pl.ds(i * rows, rows)],
                    sems.at[m, i],
                )
            )
            loads[-1].start()
    return loads


GELU_A = 0.7978845608028654
GELU_B = 0.044715


def tanh_inner(gate):
    return jnp.tanh(GELU_A * (gate + GELU_B * gate * gate * gate))


def dot_nt(left, right):
    return lax.dot_general(left, right, (((1,), (1,)), ((), ())), preferred_element_type=F32)


def dot_tn(left, right):
    return lax.dot_general(left, right, (((0,), (0,)), ((), ())), preferred_element_type=F32)


HIDDEN_TILE = 512
WIDTH_TILE = 1024


def ffn_forward_kernel(count, own, own_down, own_ffn, blocks, *refs):
    out, held_out, gate_out, up_out, down_out, weights, gate_st, up_st, act = refs[:9]
    load_sem, save_sem, keep_sem, down_local, down_s, down_r = refs[9:15]
    held, part, in_half, in_x, in_y, in_z, gs, gr, ss, sr, own_sem = refs[15:]
    me = lax.axis_index("fsdp")
    bits = weight_bits(count)
    cube = TokenCube(own, held, part, in_half, in_x, in_y, in_z, gs, gr, ss, sr)
    greet(cube.partners + [flipped(me, bit) for bit in bits])
    cube.start("zt", "zl", "x", "y")
    keep = pltpu.make_async_copy(own, held.at[0], own_sem)
    keep.start()
    block = own_down.shape[0]
    down_keep = pltpu.make_async_copy(own_down, weights.at[2, pl.ds(0, block)], down_local)
    down_keep.start()
    downs = []
    for i, bit in enumerate(bits):
        size = block << i
        src = own_down if i == 0 else weights.at[2, pl.ds(0, size)]
        downs.append(
            remote(
                src, weights.at[2, pl.ds(size, size)], down_s.at[i], down_r.at[i], flipped(me, bit)
            )
        )
    downs[0].start()
    loads = load_weights(own_ffn, blocks, weights, load_sem)
    hidden, width = weights.shape[1], weights.shape[2]
    saves = []

    def enter(step):
        j, slot, third = ORDER[step], step % 2, step % 3
        if step >= 2:
            for save in saves[step - 2]:
                save.wait()

        @pl.loop(0, hidden // HIDDEN_TILE)
        def _(n):
            at = pl.ds(pl.multiple_of(n * HIDDEN_TILE, HIDDEN_TILE), HIDDEN_TILE)
            gate = dot_nt(held[j], weights[0, at])
            up = dot_nt(held[j], weights[1, at])
            gate_st[slot, :, at] = gate
            up_st[slot, :, at] = up
            act[third, :, at] = (0.5 * gate * (1.0 + tanh_inner(gate)) * up).astype(BF16)

        saves.append(
            [
                pltpu.make_async_copy(gate_st.at[slot], gate_out.at[j], save_sem.at[0, slot]),
                pltpu.make_async_copy(up_st.at[slot], up_out.at[j], save_sem.at[1, slot]),
            ]
        )
        for save in saves[step]:
            save.start()

    def leave(step):
        j, third = ORDER[step], step % 3

        @pl.loop(0, width // WIDTH_TILE)
        def _(n):
            at = pl.ds(pl.multiple_of(n * WIDTH_TILE, WIDTH_TILE), WIDTH_TILE)
            part[j, :, at] = jnp.dot(
                act[third], weights[2, :, at], preferred_element_type=F32
            ).astype(BF16)

    keep.wait()
    for load in loads:
        load.wait()
    enter(0)
    cube.arrive("x", "y", "zt")
    cube.start("xt", "yt")
    enter(1)
    down_keep.wait()
    for i in range(1, len(downs)):
        downs[i - 1].wait_recv()
        downs[i].start()
    enter(2)
    cube.arrive("zl")
    cube.start("xl", "yl")
    cube.arrive("xt")
    cube.start("et")
    downs[-1].wait_recv()
    leave(0)
    leave(1)
    leave(2)
    save_down = pltpu.make_async_copy(weights.at[2], down_out, down_local)
    save_down.start()
    enter(3)
    cube.arrive("xl", "yt", "yl")
    cube.start("el", "dt", "dl")
    leave(3)
    for step in (4, 5):
        enter(step)
        leave(step)
    cube.arrive("et", "el")
    enter(6)
    leave(6)
    cube.corners(0)
    cube.corners(1)
    cube.arrive("dt", "dl")
    whole = pltpu.make_async_copy(held, held_out, keep_sem)
    whole.start()
    enter(7)
    leave(7)
    cube.sideways(0)
    cube.sideways(1)
    cube.corners(2)
    cube.corners(3)
    cube.across(0)
    cube.across(1)
    cube.sideways(2)
    cube.sideways(3)
    cube.finish(out)
    for save in saves[6] + saves[7] + [save_down, whole]:
        save.wait()
    for copy in downs:
        copy.wait_send()


def ffn_forward(own, own_down, own_ffn, blocks):
    count = lax.axis_size("fsdp")
    rows, width = own.shape
    hidden = blocks.shape[0] * blocks.shape[2]
    n_bits = len(weight_bits(count))
    dma = pltpu.SemaphoreType.DMA
    anywhere = pl.BlockSpec(memory_space=pl.ANY)
    return pl.pallas_call(
        functools.partial(ffn_forward_kernel, count),
        out_shape=[
            jax.ShapeDtypeStruct((rows, width), F32),
            jax.ShapeDtypeStruct((8, rows, width), BF16),
            jax.ShapeDtypeStruct((8, rows, hidden), F32),
            jax.ShapeDtypeStruct((8, rows, hidden), F32),
            jax.ShapeDtypeStruct((hidden, width), BF16),
        ],
        in_specs=[anywhere] * 4,
        out_specs=[pl.BlockSpec(memory_space=pltpu.VMEM)] + [anywhere] * 4,
        scratch_shapes=[
            pltpu.VMEM((3, hidden, width), BF16),
            pltpu.VMEM((2, rows, hidden), F32),
            pltpu.VMEM((2, rows, hidden), F32),
            pltpu.VMEM((3, rows, hidden), BF16),
            dma((2, blocks.shape[0])),
            dma((2, 2)),
            dma,
            dma,
            dma((n_bits,)),
            dma((n_bits,)),
        ]
        + cube_scratch(rows, width),
        compiler_params=pltpu.CompilerParams(
            collective_id=2, has_side_effects=True, vmem_limit_bytes=58 * 2**20
        ),
        cost_estimate=pl.CostEstimate(
            flops=48 * rows * width * hidden, bytes_accessed=300 * 2**20, transcendentals=0
        ),
        name="ffn_forward",
    )(own, own_down, own_ffn, blocks)


def ffn_backward_kernel(own, normed, gate_in, up_in, down, own_ffn, blocks, *refs):
    out, mine, further, landed, weights, gate_st, up_st, grads, stage, fetched = refs[:10]
    load_sem, down_sem, read_sem, write_sem, normed_sem, pair_s, pair_r, fetch_sem = refs[10:18]
    held, part, in_half, in_x, in_y, in_z, gs, gr, ss, sr, own_sem = refs[18:]
    sibling = flipped(lax.axis_index("fsdp"), 1)
    cube = TokenCube(own, held, part, in_half, in_x, in_y, in_z, gs, gr, ss, sr)
    greet(cube.partners + [sibling])
    cube.start("zt", "zl", "x", "y")
    keep = pltpu.make_async_copy(own, held.at[0], own_sem)
    keep.start()
    hidden, width = weights.shape[1], weights.shape[2]
    rows = own.shape[0]
    reads = []
    for step, j in enumerate(ORDER):
        slot = step % 2
        reads.append(
            [
                pltpu.make_async_copy(gate_in.at[j], gate_st.at[slot], read_sem.at[0, slot]),
                pltpu.make_async_copy(up_in.at[j], up_st.at[slot], read_sem.at[1, slot]),
            ]
        )
    for read in reads[0]:
        read.start()
    load_down = pltpu.make_async_copy(down, weights.at[2], down_sem)
    load_down.start()
    loads = load_weights(own_ffn, blocks, weights, load_sem)

    def compute(step):
        j, slot = ORDER[step], step % 2
        if step < 7:
            for read in reads[step + 1]:
                read.start()
        for read in reads[step]:
            read.wait()

        @pl.loop(0, hidden // HIDDEN_TILE)
        def _(n):
            at = pl.ds(pl.multiple_of(n * HIDDEN_TILE, HIDDEN_TILE), HIDDEN_TILE)
            grad_act = dot_nt(held[j], weights[2, at]).astype(BF16).astype(F32)
            gate, up = gate_st[slot, :, at], up_st[slot, :, at]
            inner = tanh_inner(gate)
            gelu = 0.5 * gate * (1.0 + inner)
            slope = 0.5 * (1.0 + inner) + 0.5 * gate * (1.0 - inner * inner) * GELU_A * (
                1.0 + 3.0 * GELU_B * gate * gate
            )
            token = pl.ds(j * rows, rows)
            grads[2, token, at] = (gelu * up).astype(BF16)
            grads[0, token, at] = (grad_act * up * slope).astype(BF16)
            grads[1, token, at] = (grad_act * gelu).astype(BF16)

        if step == 0:
            for load in loads:
                load.wait()
        token = pl.ds(j * rows, rows)

        @pl.loop(0, width // WIDTH_TILE)
        def _(n):
            at = pl.ds(pl.multiple_of(n * WIDTH_TILE, WIDTH_TILE), WIDTH_TILE)
            part[j, :, at] = (
                jnp.dot(grads[0, token], weights[0, :, at], preferred_element_type=F32)
                + jnp.dot(grads[1, token], weights[1, :, at], preferred_element_type=F32)
            ).astype(BF16)

    keep.wait()
    load_down.wait()
    compute(0)
    cube.arrive("x", "y", "zt")
    cube.start("xt", "yt")
    compute(1)
    compute(2)
    cube.arrive("zl")
    cube.start("xl", "yl")
    cube.arrive("xt")
    cube.start("et")
    compute(3)
    cube.arrive("xl", "yt", "yl")
    cube.start("el", "dt", "dl")
    compute(4)
    compute(5)
    cube.arrive("et", "el")
    compute(6)
    cube.corners(0)
    cube.corners(1)
    cube.arrive("dt", "dl")
    compute(7)
    tokens = 8 * rows
    refill = pltpu.make_async_copy(
        normed, weights.at[pl.ds(0, tokens // hidden)], normed_sem
    )
    refill.start()
    tile = stage.shape[1]
    half, quarter = hidden // 2, hidden // 4
    tiles = [(m, i * tile) for m in (2, 0, 1) for i in range(half // tile)]
    pairs, busy = [], [None, None]
    for n, (m, first) in enumerate(tiles):
        pairs.append(
            remote(
                stage.at[n % 2],
                landed.at[m, pl.ds(first, tile)],
                pair_s.at[n],
                pair_r.at[n],
                sibling,
            )
        )
    fetches = [
        pltpu.make_async_copy(
            landed.at[m, pl.ds(first, tile)], fetched.at[n % 2], fetch_sem.at[n % 2]
        )
        for n, (m, first) in enumerate(tiles)
    ]
    done = [0]

    def weight_grad(times):
        for _ in range(times):
            job = done[0]
            done[0] = job + 1
            n, for_sibling = job % len(tiles), job < len(tiles)
            m, first = tiles[n]
            slot = job % 2
            if job == len(tiles) // 3:
                refill.wait()
            if busy[slot] is not None:
                busy[slot]()
            if not for_sibling:
                pairs[n].wait_recv()
                fetches[n].start()
                fetches[n].wait()
            place = first + half if for_sibling else first

            @pl.loop(0, width // WIDTH_TILE)
            def _(k):
                at = pl.ds(pl.multiple_of(k * WIDTH_TILE, WIDTH_TILE), WIDTH_TILE)
                if m == 2:
                    right = held[:, :, at].reshape(tokens, WIDTH_TILE)
                else:
                    right = weights[: tokens // hidden, :, at].reshape(tokens, WIDTH_TILE)
                grad = dot_tn(grads[m, :, pl.ds(place, tile)], right)
                if not for_sibling:
                    grad = grad + fetched[n % 2, :, at].astype(F32)
                stage[slot, :, at] = grad.astype(BF16)

            if for_sibling:
                pairs[n].start()
                busy[slot] = pairs[n].wait_send
            else:
                target = mine if first < quarter else further
                write = pltpu.make_async_copy(
                    stage.at[slot],
                    target.at[m, pl.ds(first % quarter, tile)],
                    write_sem.at[slot],
                )
                write.start()
                busy[slot] = write.wait

    cube.sideways(0)
    cube.sideways(1)
    cube.corners(2)
    cube.corners(3)
    weight_grad(3)
    cube.across(0)
    weight_grad(1)
    cube.sideways(2)
    cube.across(1)
    weight_grad(1)
    cube.sideways(3)
    weight_grad(2 * len(tiles) - 5)
    cube.finish(out)
    for end in busy:
        end()


def ffn_backward(own, normed, gate, up, down, own_ffn, blocks):
    rows, width = own.shape
    hidden = blocks.shape[0] * blocks.shape[2]
    dma = pltpu.SemaphoreType.DMA
    anywhere = pl.BlockSpec(memory_space=pl.ANY)
    tile = 256
    n_tiles = 3 * (hidden // 2) // tile
    grad = jax.ShapeDtypeStruct((3, hidden // 4, width), BF16)
    landed = jax.ShapeDtypeStruct((3, hidden // 2, width), BF16)
    return pl.pallas_call(
        ffn_backward_kernel,
        out_shape=[jax.ShapeDtypeStruct((rows, width), F32), grad, grad, landed],
        in_specs=[anywhere] * 7,
        out_specs=[pl.BlockSpec(memory_space=pltpu.VMEM)] + [anywhere] * 3,
        scratch_shapes=[
            pltpu.VMEM((3, hidden, width), BF16),
            pltpu.VMEM((2, rows, hidden), F32),
            pltpu.VMEM((2, rows, hidden), F32),
            pltpu.VMEM((3, 8 * rows, hidden), BF16),
            pltpu.VMEM((2, tile, width), BF16),
            pltpu.VMEM((2, tile, width), BF16),
            dma((2, blocks.shape[0])),
            dma,
            dma((2, 2)),
            dma((2,)),
            dma,
            dma((n_tiles,)),
            dma((n_tiles,)),
            dma((2,)),
        ]
        + cube_scratch(rows, width),
        compiler_params=pltpu.CompilerParams(
            collective_id=3, has_side_effects=True, vmem_limit_bytes=62 * 2**20
        ),
        cost_estimate=pl.CostEstimate(
            flops=96 * rows * width * hidden, bytes_accessed=400 * 2**20, transcendentals=0
        ),
        name="ffn_backward",
    )(
        own,
        normed.reshape(8 * rows // hidden, hidden, width),
        gate,
        up,
        down,
        own_ffn,
        blocks,
    )


def inv_rms(field):
    return lax.rsqrt(jnp.mean(field * field, axis=-1, keepdims=True) + EPSILON)


def gelu_tanh(field):
    return jax.nn.gelu(field, approximate=True)


def layout(seq_lengths, seq_order, token_index):
    slot_ids = jnp.arange(seq_lengths.shape[0], dtype=jnp.int32)
    packed = jnp.sum(
        jnp.where(seq_order[:, None] == slot_ids[None, :], seq_lengths[None, :], 0), axis=1
    )
    starts = jnp.sum(jnp.where(slot_ids[None, :] < slot_ids[:, None], packed[None, :], 0), axis=1)
    segment = jnp.sum((token_index[:, None] >= starts[None, :]).astype(jnp.int32), axis=1) - 1
    offset = jnp.max(jnp.where(starts[None, :] <= token_index[:, None], starts[None, :], 0), axis=1)
    return (segment, token_index - offset)


def angles(position):
    half_width = HD // 2
    freq = ROPE_BASE ** (-2.0 * jnp.arange(half_width, dtype=jnp.float32) / HD)
    phase = position.astype(jnp.float32)[:, None] * freq[None, :]
    phase = jnp.concatenate([phase, phase], axis=-1)
    return (jnp.cos(phase)[:, None, :], jnp.sin(phase)[:, None, :])


def norm_back(grad_out, field, scale_inv, gain):
    weighted = grad_out * gain
    return scale_inv * weighted - field * scale_inv**3 * jnp.mean(
        weighted * field, axis=-1, keepdims=True
    )


def contract_rows(left_op, right_op):
    return lax.dot_general(
        left_op, right_op, (((0,), (0,)), ((), ())), preferred_element_type=jnp.float32
    )


def contract_cols(left_op, right_op):
    return lax.dot_general(
        left_op, right_op, (((1,), (1,)), ((), ())), preferred_element_type=jnp.float32
    )


def local(
    tokens,
    per_layer,
    cotangent,
    seq_lengths,
    seq_order,
    qkv_weight,
    out_weight,
    ffn_weights,
    side_weights,
    norm_gains,
):
    tok_rows = tokens.shape[0]
    my_index = lax.axis_index("fsdp")
    token_index = my_index * tok_rows + jnp.arange(tok_rows, dtype=jnp.int32)
    segment, position = layout(seq_lengths, seq_order, token_index)
    cosine, sine = angles(position)
    reach = (WINDOW + tok_rows - 2) // tok_rows
    assert reach == 2
    split_at = PL + RANK
    count = lax.axis_size("fsdp")
    bits = weight_bits(count)
    weight_rows = qkv_weight.shape[0]
    ffn_own = ffn_weights[:, :2].transpose(1, 0, 2)
    (
        qkv_gathered,
        out_gathered,
        ffn_blocks,
        normed_b,
        projected,
        query_b,
        key_blocks,
        value_blocks,
        gain_all,
        mixed_b,
        first_sum,
        normed_two,
    ) = attention_forward(
        jnp.concatenate([qkv_weight, placed_gains(norm_gains, weight_rows)], axis=1),
        jnp.concatenate([out_weight, side_weights], axis=1),
        ffn_own,
        tokens,
        cosine[:, 0, : HD // 2],
        sine[:, 0, : HD // 2],
        position[:, None],
    )
    side_all = out_gathered[:, D:]
    ffn_gain = gain_all[0, D : 2 * D]
    rms_two = inv_rms(first_sum)
    ffn_out, normed_all, gate_kept, up_kept, down_all = ffn_forward(
        normed_two, ffn_weights[:, 2], ffn_own, ffn_blocks
    )
    second_sum = first_sum + ffn_out
    second_b = second_sum.astype(jnp.bfloat16)
    side_in = jnp.dot(second_b, side_all[:, :split_at], preferred_element_type=jnp.float32)
    per_f = per_layer.astype(jnp.float32)
    gelu_per, pull_per = jax.vjp(gelu_tanh, side_in[:, :PL])
    combined = jnp.concatenate(
        [(gelu_per * per_f).astype(jnp.bfloat16), side_in[:, PL:].astype(jnp.bfloat16)], axis=1
    )
    output = (second_sum + contract_cols(combined, side_all[:, split_at:])).astype(jnp.bfloat16)
    back_side = side_all
    grad_y = cotangent.astype(jnp.float32)
    grad_comb = jnp.dot(cotangent, back_side[:, split_at:], preferred_element_type=jnp.float32)
    per_layer_grad = (grad_comb[:, :PL] * gelu_per).astype(jnp.bfloat16)
    grad_per = pull_per(grad_comb[:, :PL] * per_f)[0]
    grad_side = jnp.concatenate([grad_per, grad_comb[:, PL:]], axis=1).astype(jnp.bfloat16)
    grad_two = grad_y + contract_cols(grad_side, back_side[:, :split_at])
    grad_two_b = grad_two.astype(jnp.bfloat16)
    grad_h2, ffn_part, ffn_sent, _ = ffn_backward(
        grad_two_b, normed_all, gate_kept, up_kept, down_all, ffn_own, ffn_blocks
    )
    for bit in reversed(bits[:-1]):
        ffn_part = ffn_part.astype(F32) + swapped(ffn_sent, bit).astype(F32)
        if bit != bits[0]:
            half = ffn_part.shape[1] // 2
            ffn_sent = ffn_part[:, half:].astype(BF16)
            ffn_part = ffn_part[:, :half]
    ffn_grad = ffn_part.transpose(1, 0, 2)
    ffn_gain_grad = jnp.sum(grad_h2 * first_sum * rms_two, axis=0)
    grad_one = grad_two + norm_back(grad_h2, first_sum, rms_two, ffn_gain)
    grad_one_b = grad_one.astype(jnp.bfloat16)
    out_sum, grad_projected, input_grad, attn_gain_grad, head_gain_grad = attention_backward(
        qkv_gathered,
        out_gathered,
        grad_one_b,
        grad_one,
        tokens,
        mixed_b,
        second_b,
        jnp.pad(grad_side, ((0, 0), (0, split_at))),
        cotangent,
        jnp.pad(combined, ((0, 0), (split_at, 0))),
        query_b,
        key_blocks,
        value_blocks,
        projected,
        gain_all,
        cosine[:, 0, : HD // 2],
        sine[:, 0, : HD // 2],
        position[:, None],
    )
    gains_grad_full = jnp.concatenate([attn_gain_grad[0], ffn_gain_grad, head_gain_grad[0]])
    gain_rows = jnp.pad(
        gains_grad_full.astype(BF16).reshape(count, -1),
        ((0, 0), (0, weight_rows * LANES - norm_gains.shape[0])),
    ).reshape(count * weight_rows, LANES)
    qkv_sum = qkv_scatter(gain_rows, normed_b, grad_projected)
    qkv_grad = qkv_sum[:, : qkv_weight.shape[1]]
    gains_grad = qkv_sum[:, qkv_weight.shape[1] :].reshape(-1)[: norm_gains.shape[0]]
    out_grad, side_grad = out_sum[:, :D], out_sum[:, D:]
    return (output, input_grad, per_layer_grad, qkv_grad, out_grad, ffn_grad, side_grad, gains_grad)


def solution(mesh):
    return jax.shard_map(
        local,
        mesh=mesh,
        in_specs=(
            P("fsdp", None),
            P("fsdp", None),
            P("fsdp", None),
            P(),
            P(),
            P("fsdp", None),
            P("fsdp", None),
            P("fsdp", None, None),
            P("fsdp", None),
            P("fsdp"),
        ),
        out_specs=(
            P("fsdp", None),
            P("fsdp", None),
            P("fsdp", None),
            P("fsdp", None),
            P("fsdp", None),
            P("fsdp", None, None),
            P("fsdp", None),
            P("fsdp"),
        ),
        check_vma=False,
    )
```

```python
import functools

import jax
import jax.numpy as jnp
from jax import lax
from jax.experimental import pallas as pl
from jax.experimental.pallas import tpu as pltpu
from jax.sharding import PartitionSpec as P

D = 2048
HQ = 8
KVH = 2
HD = 256
PL = 256
RANK = 64
WINDOW = 512


EPSILON = 1e-06
NEGATIVE = -1e30
ROPE_BASE = 10000.0


PLANE = 8
LANES = 128
MESH = pl.DeviceIdType.MESH
BF16 = jnp.bfloat16
F32 = jnp.float32


def flipped(index, bit):
    return index + bit - 2 * bit * lax.rem(lax.div(index, bit), 2)


def swapped(block, bit):
    route = [(i, i ^ bit) for i in range(lax.axis_size("fsdp"))]
    return lax.ppermute(block, "fsdp", route)


def weight_bits(count):
    return [8] + [1 << i for i in range(5, count.bit_length() - 1)] + [1]


def greet(partners):
    barrier = pltpu.get_barrier_semaphore()
    for partner in partners:
        pl.semaphore_signal(barrier, inc=1, device_id=(partner,), device_id_type=MESH)
    pl.semaphore_wait(barrier, len(partners))


def remote(src, dst, send, recv, device):
    return pltpu.make_async_remote_copy(
        src_ref=src,
        dst_ref=dst,
        send_sem=send,
        recv_sem=recv,
        device_id=(device,),
        device_id_type=MESH,
    )


def half_split(width):
    return (width // LANES + 1) // 2 * LANES


def head_norm(field):
    return lax.rsqrt(jnp.mean(field * field, axis=-1, keepdims=True) + EPSILON)


def turn(field, cosine, sine):
    half = field.shape[1] // 2
    low, high = field[:, :half], field[:, half:]
    return jnp.concatenate([low * cosine - high * sine, high * cosine + low * sine], axis=1)


def gain_spans(count, total):
    per = total // count
    spans = []
    for d in range(count):
        first = per * d // LANES
        last = (per * (d + 1) - 1) // LANES
        spans.append((first, last - first + 1))
    return spans


def placed_gains(norm_gains, rows):
    per = norm_gains.shape[0]
    offset = lax.rem(per * lax.axis_index("fsdp"), LANES)
    return lax.dynamic_update_slice(
        jnp.zeros((rows * LANES,), norm_gains.dtype), norm_gains, (offset,)
    ).reshape(rows, LANES)


def soft_rows(query, keys, reach, gap):
    scores = dot_nt(query, keys) * HD ** (-0.5)
    scores = jnp.where((gap >= 0) & (gap <= reach), scores, NEGATIVE)
    exponent = jnp.exp(scores - jnp.max(scores, axis=-1, keepdims=True))
    return exponent / jnp.sum(exponent, axis=-1, keepdims=True)


class WeightGather:
    def __init__(self, chain, pairs):
        me = lax.axis_index("fsdp")
        core, x_at, y_at = lax.rem(me, 2), lax.rem(lax.div(me, 2), 2), lax.rem(lax.div(me, 4), 2)
        z_at = lax.div(me, PLANE)
        next_x, next_y, next_c = flipped(me, 2), flipped(me, 4), flipped(me, 1)
        z_peers = [me + (lax.rem(z_at + s, chain) - z_at) * PLANE for s in range(1, chain)]
        self.partners = [next_x, next_y, next_c] + z_peers
        self.order = sorted(range(chain), key=lambda s: (min(s, chain - s), s))
        self.waves = []
        for own, out, (local, zs, zr, xs, xr, ys, yr, a_s, ar, bs, br, cs, cr) in pairs:
            cut = half_split(own.shape[-1])
            left, right = pl.ds(0, cut), pl.ds(cut, own.shape[-1] - cut)
            ops = {"own": pltpu.make_async_copy(own, out.at[z_at, y_at, x_at, core], local)}
            ops["z"] = [None] + [
                remote(own, out.at[z_at, y_at, x_at, core], zs.at[s], zr.at[s], z_peers[s - 1])
                for s in self.order[1:]
            ]
            steps = []
            for s in self.order:
                k = lax.rem(z_at + chain - s, chain)
                here = out.at[k, y_at, x_at, core]
                src = own if s == 0 else here
                from_x = out.at[k, y_at, 1 - x_at, core]
                from_y = out.at[k, 1 - y_at, x_at, core]
                column = out.at[k, :, :, core]
                steps.append(
                    {
                        "x": remote(src, here, xs.at[s], xr.at[s], next_x),
                        "y": remote(src, here, ys.at[s], yr.at[s], next_y),
                        "a": remote(
                            from_x.at[:, left], from_x.at[:, left], a_s.at[s], ar.at[s], next_y
                        ),
                        "b": remote(
                            from_y.at[:, right], from_y.at[:, right], bs.at[s], br.at[s], next_x
                        ),
                        "c": remote(column, column, cs.at[s], cr.at[s], next_c),
                    }
                )
            ops["steps"] = steps
            self.waves.append(ops)

    def spread(self, w, s):
        ops = self.waves[w]
        if s == 0:
            ops["own"].start()
        else:
            ops["z"][s].wait_recv()
        if w == 0 and s + 1 < len(ops["z"]):
            ops["z"][s + 1].start()
        if w > 0 and s == 0:
            for copy in ops["z"][1:]:
                copy.start()
        ops["steps"][s]["x"].start()
        ops["steps"][s]["y"].start()

    def pass_on(self, w, s):
        step = self.waves[w]["steps"][s]
        step["x"].wait_recv()
        step["a"].start()
        step["y"].wait_recv()
        step["b"].start()

    def across(self, w, s):
        step = self.waves[w]["steps"][s]
        step["a"].wait_recv()
        step["b"].wait_recv()
        if s == 0:
            self.waves[w]["own"].wait()
        step["c"].start()

    def complete(self, w):
        for step in self.waves[w]["steps"]:
            step["c"].wait_recv()

    def drain(self):
        for ops in self.waves:
            for copy in ops["z"][1:]:
                copy.wait_send()
            for step in ops["steps"]:
                for name in "xyabc":
                    step[name].wait_send()


def attention_forward_kernel(
    count,
    own_a,
    own_b,
    own_ffn,
    tokens,
    cosine,
    sine,
    position,
    full_a,
    full_b,
    full_ffn,
    normed_out,
    projected_out,
    query_out,
    key_out,
    value_out,
    gains,
    mixed,
    first_sum,
    normed_two,
    wa,
    wb,
    normed,
    projected,
    query,
    key_rows,
    value_rows,
    *sems,
):
    me = lax.axis_index("fsdp")
    chain = count // PLANE
    bits = weight_bits(count)
    gather = WeightGather(chain, ((own_a, wa, sems[:13]), (own_b, wb, sems[13:26])))
    first_s, first_r, ffn_s, ffn_r, rest_s, rest_r, halo_s, halo_r, save, early = sems[26:]
    ahead = [lax.rem(me + d, count) for d in (1, 2)]
    behind = [lax.rem(me + count - d, count) for d in (1, 2)]
    greet(gather.partners + [flipped(me, bit) for bit in bits[:-1]] + ahead + behind)
    ffn_first, ffn_copies, ffn_rest = [], [], []
    piece = own_ffn.shape[1] // FFN_PIECES
    for j in range(2 * FFN_PIECES):
        at = pl.ds(j % FFN_PIECES * piece, piece)
        m = j // FFN_PIECES
        ffn_first.append(
            remote(
                own_ffn.at[m, at],
                full_ffn.at[1, m, at],
                first_s.at[j],
                first_r.at[j],
                flipped(me, bits[0]),
            )
        )
    for i, bit in enumerate(bits[1:]):
        size, partner = 2 << i, flipped(me, bit)
        ffn_copies.append(remote(own_ffn, full_ffn.at[size], ffn_s.at[i], ffn_r.at[i], partner))
        ffn_rest.append(
            remote(
                full_ffn.at[pl.ds(1, size - 1)],
                full_ffn.at[pl.ds(size + 1, size - 1)],
                rest_s.at[i],
                rest_r.at[i],
                partner,
            )
        )
    halo = []
    for d in (1, 2):
        for j, rows in enumerate((key_rows, value_rows)):
            at = 2 * (d - 1) + j
            halo.append(
                remote(rows.at[2], rows.at[2 - d], halo_s.at[at], halo_r.at[at], ahead[d - 1])
            )
    for s in range(chain):
        gather.spread(0, s)
        if s >= 1:
            gather.pass_on(0, s - 1)
        if s >= 2:
            gather.across(0, s - 2)
    gather.spread(1, 0)
    for copy in ffn_first + ffn_copies:
        copy.start()
    gather.pass_on(0, chain - 1)
    gather.across(0, chain - 2)
    gather.across(0, chain - 1)
    gather.complete(0)
    for s in range(1, chain):
        gather.spread(1, s)
    keep_a = pltpu.make_async_copy(wa, full_a, save.at[0])
    keep_a.start()

    width_a, per = QKV_WIDTH, gains.shape[1] // count
    spans = gain_spans(count, gains.shape[1])
    pieces = {}
    for d, (first, n_rows) in enumerate(spans):
        block = wa[
            d // PLANE, d // 4 % 2, d // 2 % 2, d % 2, 0:16, width_a : width_a + LANES
        ].astype(F32)
        for r in range(n_rows):
            pieces.setdefault(first + r, []).append(block[r : r + 1])
    for t, terms in pieces.items():
        total = terms[0]
        for term in terms[1:]:
            total = total + term
        gains[:, t * LANES : (t + 1) * LANES] = total

    rows, depth = tokens.shape

    @pl.loop(0, rows // 32)
    def _(i):
        at = pl.ds(pl.multiple_of(i * 32, 32), 32)
        field = tokens[at].astype(F32)
        normed[at] = (field * head_norm(field) * gains[:, :depth]).astype(BF16)

    def project(n):
        at = pl.ds(pl.multiple_of(n * 512, 512), 512)
        weight = wa[:, :, :, :, :, at].reshape(depth, 512)
        projected[:, at] = jnp.dot(normed[...], weight, preferred_element_type=F32)

    query_width = HQ * HD
    kv_width = KVH * HD

    @pl.loop(query_width // 512, (query_width + 2 * kv_width) // 512)
    def _(n):
        project(n)

    for g in range(KVH):
        at = slice(query_width + g * HD, query_width + (g + 1) * HD)
        field = projected[:, at]
        key_gain = gains[:, 2 * depth + HD :]
        key_rows[2, :, g * HD : (g + 1) * HD] = turn(
            field * head_norm(field) * key_gain, cosine[...], sine[...]
        ).astype(BF16)
    value_rows[2] = projected[:, query_width + kv_width :].astype(BF16)
    for copy in halo:
        copy.start()
    for s in range(chain - 3):
        gather.pass_on(1, s)

    @pl.loop(0, query_width // 512)
    def _(n):
        project(n)

    gather.pass_on(1, chain - 3)
    for s in range(chain - 3):
        gather.across(1, s)

    @pl.loop(0, HQ)
    def _(h):
        at = pl.ds(pl.multiple_of(h * HD, HD), HD)
        field = projected[:, at]
        query_gain = gains[:, 2 * depth : 2 * depth + HD]
        query[:, at] = turn(
            field * head_norm(field) * query_gain, cosine[...], sine[...]
        ).astype(BF16)

    gather.pass_on(1, chain - 2)
    gather.across(1, chain - 3)
    for copy in halo:
        copy.wait_recv()
    early_saves = [
        pltpu.make_async_copy(src, dst, early.at[i])
        for i, (src, dst) in enumerate(
            (
                (normed, normed_out),
                (projected, projected_out),
                (query, query_out),
                (key_rows, key_out),
                (value_rows, value_out),
            )
        )
    ]
    for copy in early_saves:
        copy.start()
    n_keys = 3 * rows
    gap = (
        lax.broadcasted_iota(jnp.int32, (rows, n_keys), 0)
        - lax.broadcasted_iota(jnp.int32, (rows, n_keys), 1)
        + 2 * rows
    )
    reach = jnp.minimum(position[...], WINDOW - 1)

    def heads(first, last):
        @pl.loop(first, last)
        def _(h):
            at = pl.ds(pl.multiple_of(h * HD, HD), HD)
            group = pl.ds(pl.multiple_of(lax.div(h, HQ // KVH) * HD, HD), HD)
            keys = key_rows[:, :, group].reshape(n_keys, HD)
            values = value_rows[:, :, group].reshape(n_keys, HD)
            probs = soft_rows(query[:, at], keys, reach, gap).astype(BF16)
            mixed[:, at] = jnp.dot(probs, values, preferred_element_type=F32).astype(BF16)

    heads(0, 1)
    gather.pass_on(1, chain - 1)
    heads(1, 2)
    gather.across(1, chain - 2)
    heads(2, 4)
    gather.across(1, chain - 1)
    heads(4, 8)
    gather.complete(1)
    keep_b = pltpu.make_async_copy(wb, full_b, save.at[1])
    keep_b.start()

    @pl.loop(0, depth // 512)
    def _(n):
        at = pl.ds(pl.multiple_of(n * 512, 512), 512)
        weight = wb[:, :, :, :, :, at].reshape(depth, 512)
        first_sum[:, at] = tokens[:, at].astype(F32) + jnp.dot(
            mixed[...], weight, preferred_element_type=F32
        )

    @pl.loop(0, rows // 32)
    def _(i):
        at = pl.ds(pl.multiple_of(i * 32, 32), 32)
        field = first_sum[at]
        normed_two[at] = (field * head_norm(field) * gains[:, depth : 2 * depth]).astype(BF16)

    for copy in ffn_first:
        copy.wait_recv()
    for copy, rest in zip(ffn_copies, ffn_rest):
        rest.start()
        copy.wait_recv()
        rest.wait_recv()
    for copy in ffn_first + ffn_copies + ffn_rest + halo:
        copy.wait_send()
    gather.drain()
    for copy in early_saves + [keep_a, keep_b]:
        copy.wait()


FFN_PIECES = 2
QKV_WIDTH = (HQ + 2 * KVH) * HD


def attention_forward(own_a, own_b, own_ffn, tokens, cosine, sine, position):
    count = lax.axis_size("fsdp")
    chain = count // PLANE
    rows, depth = tokens.shape
    n_blocks = 1 << len(weight_bits(count))
    dma = pltpu.SemaphoreType.DMA
    anywhere, vmem = pl.BlockSpec(memory_space=pl.ANY), pl.BlockSpec(memory_space=pltpu.VMEM)
    shape_a, shape_b = ((chain, 2, 2, 2) + own.shape for own in (own_a, own_b))
    kept = [
        jax.ShapeDtypeStruct((rows, depth), BF16),
        jax.ShapeDtypeStruct((rows, QKV_WIDTH), F32),
        jax.ShapeDtypeStruct((rows, HQ * HD), BF16),
        jax.ShapeDtypeStruct((3, rows, KVH * HD), BF16),
        jax.ShapeDtypeStruct((3, rows, KVH * HD), BF16),
    ]
    full_a, full_b, *rest = pl.pallas_call(
        functools.partial(attention_forward_kernel, count),
        out_shape=[
            jax.ShapeDtypeStruct(shape_a, BF16),
            jax.ShapeDtypeStruct(shape_b, BF16),
            jax.ShapeDtypeStruct((n_blocks,) + own_ffn.shape, BF16),
            *kept,
            jax.ShapeDtypeStruct((1, 2 * depth + 2 * HD), F32),
            jax.ShapeDtypeStruct((rows, HQ * HD), BF16),
            jax.ShapeDtypeStruct((rows, depth), F32),
            jax.ShapeDtypeStruct((rows, depth), BF16),
        ],
        in_specs=[anywhere] * 3 + [vmem] * 4,
        out_specs=[anywhere] * 8 + [vmem] * 4,
        scratch_shapes=[pltpu.VMEM(shape_a, BF16), pltpu.VMEM(shape_b, BF16)]
        + [pltpu.VMEM(array.shape, array.dtype) for array in kept]
        + ([dma] + [dma((chain,))] * 12) * 2
        + [dma((2 * FFN_PIECES,))] * 2
        + [dma((len(weight_bits(count)) - 1,))] * 4
        + [dma((4,)), dma((4,)), dma((2,)), dma((len(kept),))],
        compiler_params=pltpu.CompilerParams(
            collective_id=0, has_side_effects=True, vmem_limit_bytes=58 * 2**20
        ),
        name="attention_forward",
    )(own_a, own_b, own_ffn, tokens, cosine, sine, position)
    return (full_a.reshape(-1, own_a.shape[1]), full_b.reshape(-1, own_b.shape[1]), *rest)


def add_into(target, *terms):
    rows = target.shape[0]
    tile = 16

    @pl.loop(0, rows // tile)
    def _(i):
        at = pl.ds(pl.multiple_of(i * tile, tile), tile)
        if len(terms) == 1:
            target[at] = target[at] + terms[0][at]
        else:
            total = target[at].astype(F32)
            for term in terms:
                total = total + term[at].astype(F32)
            target[at] = total.astype(target.dtype)


class WeightScatter:
    def __init__(self, chain, part, out, sibling, in_a, in_b, in_x, in_y, in_z, *sems):
        cs, cr, a_s, ar, bs, br, xs, xr, ys, yr, zs, zr = sems
        me = lax.axis_index("fsdp")
        core, x_at, y_at = lax.rem(me, 2), lax.rem(lax.div(me, 2), 2), lax.rem(lax.div(me, 4), 2)
        z_at = lax.div(me, PLANE)
        next_x, next_y, next_c = flipped(me, 2), flipped(me, 4), flipped(me, 1)
        z_peers = [me + (lax.rem(z_at + s, chain) - z_at) * PLANE for s in range(1, chain)]
        self.partners = [next_x, next_y, next_c] + z_peers
        self.chain, self.out, self.in_z = chain, out, in_z
        cut = half_split(out.shape[-1])
        left, right = pl.ds(0, cut), pl.ds(cut, out.shape[-1] - cut)
        self.left, self.right = left, right
        self.order = list(range(1, chain)) + [0]
        self.blocks = [lax.rem(z_at + s, chain) for s in range(chain)]
        self.steps = []
        for s in range(chain):
            mine = part.at[s, :, :, core]
            step = {
                "mine": [part.at[s, j // 2, j % 2, core] for j in range(4)],
                "sibling": [sibling.at[s, j // 2, j % 2] for j in range(4)],
                "in": (in_a.at[s], in_b.at[s], in_x.at[s], in_y.at[s]),
                "here": part.at[s, y_at, x_at, core],
                "to_x": part.at[s, y_at, 1 - x_at, core],
                "to_y": part.at[s, 1 - y_at, x_at, core],
                "c": remote(
                    part.at[s, :, :, 1 - core], sibling.at[s], cs.at[s], cr.at[s], next_c
                ),
            }
            corner = part.at[s, 1 - y_at, 1 - x_at, core]
            step["a"] = remote(corner.at[:, left], in_a.at[s], a_s.at[s], ar.at[s], next_x)
            step["b"] = remote(corner.at[:, right], in_b.at[s], bs.at[s], br.at[s], next_y)
            step["x"] = remote(step["to_x"], in_x.at[s], xs.at[s], xr.at[s], next_x)
            step["y"] = remote(step["to_y"], in_y.at[s], ys.at[s], yr.at[s], next_y)
            if s > 0:
                step["z"] = remote(
                    step["here"], in_z.at[s - 1], zs.at[s - 1], zr.at[s - 1], z_peers[s - 1]
                )
            self.steps.append(step)

    def cross(self, i):
        self.steps[self.order[i]]["c"].start()

    def halve(self, i):
        step = self.steps[self.order[i]]
        step["c"].wait_recv()
        for mine, sibling in zip(step["mine"], step["sibling"]):
            add_into(mine, sibling)
        step["a"].start()
        step["b"].start()

    def sideways(self, i):
        step = self.steps[self.order[i]]
        in_a, in_b, _, _ = step["in"]
        step["a"].wait_recv()
        add_into(step["to_y"].at[:, self.left], in_a)
        step["y"].start()
        step["b"].wait_recv()
        add_into(step["to_x"].at[:, self.right], in_b)
        step["x"].start()

    def finish(self, i):
        step = self.steps[self.order[i]]
        step["x"].wait_recv()
        step["y"].wait_recv()
        add_into(step["here"], *step["in"][2:])
        if "z" in step:
            step["z"].start()

    def total(self):
        for step in self.steps[1:]:
            step["z"].wait_recv()

        @pl.loop(0, self.out.shape[0] // 16)
        def _(i):
            at = pl.ds(pl.multiple_of(i * 16, 16), 16)
            total = self.steps[0]["here"][at].astype(F32)
            for s in range(self.chain - 1):
                total = total + self.in_z[s, at].astype(F32)
            self.out[at] = total

        for step in self.steps:
            for name in "cabxyz":
                if name in step:
                    step[name].wait_send()


def scatter_scratch(chain, rows, width):
    cut = half_split(width)
    shapes = [
        (chain, 2, 2, 2, rows, width),
        (chain, 2, 2, rows, width),
        (chain, rows, cut),
        (chain, rows, width - cut),
        (chain, rows, width),
        (chain, rows, width),
        (chain - 1, rows, width),
    ]
    return [pltpu.VMEM(shape, BF16) for shape in shapes] + [
        pltpu.SemaphoreType.DMA((chain,))
    ] * 12


def turn_back(grad, cosine, sine):
    half = grad.shape[1] // 2
    low, high = grad[:, :half], grad[:, half:]
    return jnp.concatenate([low * cosine + high * sine, high * cosine - low * sine], axis=1)


def head_back(grad_rot, field, gain, cosine, sine):
    grad = turn_back(grad_rot, cosine, sine)
    scale = head_norm(field)
    weighted = grad * gain
    back = scale * weighted - field * (
        scale * scale * scale * jnp.mean(weighted * field, axis=-1, keepdims=True)
    )
    return back, jnp.sum(grad * field * scale, axis=0, keepdims=True)


def attention_backward_kernel(
    count,
    full_a,
    full_b,
    grad_one_in,
    tokens_in,
    query_in,
    key_in,
    value_in,
    projected_in,
    grad_one_b,
    mixed,
    second,
    grad_side,
    cotangent,
    combined,
    gains,
    cosine,
    sine,
    position,
    out_sum,
    grad_projected,
    input_grad,
    attn_gain_grad,
    head_gain_grad,
    weight,
    grad_mixed,
    grad_normed,
    grad_keys,
    grad_values,
    halo_out,
    halo_in,
    grad_one,
    tokens,
    query,
    key_rows,
    value_rows,
    projected,
    weight_sem,
    fill_sem,
    halo_s,
    halo_r,
    part,
    *scratch,
):
    me = lax.axis_index("fsdp")
    chain = count // PLANE
    scatter = WeightScatter(chain, part, out_sum, *scratch)
    ahead = [lax.rem(me + d, count) for d in (1, 2)]
    behind = [lax.rem(me + count - d, count) for d in (1, 2)]
    greet(scatter.partners + ahead + behind)
    rows, depth = tokens.shape
    query_width, kv_width = HQ * HD, KVH * HD
    out_width = depth
    load_out = pltpu.make_async_copy(
        full_b.at[:, :, :, :, :, pl.ds(0, out_width)],
        weight.at[:, :, :, :, :, pl.ds(0, out_width)],
        weight_sem,
    )
    load_out.start()
    fills = [
        pltpu.make_async_copy(src, dst, fill_sem.at[i])
        for i, (src, dst) in enumerate(
            (
                (query_in, query),
                (key_in, key_rows),
                (value_in, value_rows),
                (projected_in, projected),
                (tokens_in, tokens),
                (grad_one_in, grad_one),
            )
        )
    ]
    for fill in fills:
        fill.start()
    tile = depth // chain
    block_shape = part.shape[1:5]
    for i, s in enumerate(scatter.order):
        columns = pl.ds(pl.multiple_of(scatter.blocks[s] * tile, tile), tile)
        left = mixed[:, columns]

        @pl.loop(0, out_width // 512)
        def _(n):
            at = pl.ds(pl.multiple_of(n * 512, 512), 512)
            part[s, :, :, :, :, at] = (
                dot_tn(left, grad_one_b[:, at]).astype(BF16).reshape(block_shape + (512,))
            )

        side = dot_tn(second[:, columns], grad_side[...])
        side = side + dot_tn(cotangent[:, columns], combined[...])
        part[s, :, :, :, :, out_width:] = side.astype(BF16).reshape(
            block_shape + (part.shape[-1] - out_width,)
        )
        scatter.cross(i)
        if i >= 1:
            scatter.halve(i - 1)
        if i >= 3:
            scatter.sideways(i - 3)
        if i >= 5:
            scatter.finish(i - 5)
    load_out.wait()

    @pl.loop(0, chain)
    def _(k):
        at = pl.ds(pl.multiple_of(k * tile, tile), tile)
        grad_mixed[:, at] = dot_nt(
            grad_one_b[...], weight[k, :, :, :, :, 0:out_width].reshape(tile, out_width)
        ).astype(BF16)

    load_qkv = pltpu.make_async_copy(
        full_a.at[:, :, :, :, :, pl.ds(0, QKV_WIDTH)], weight, weight_sem
    )
    load_qkv.start()
    grad_keys[...] = jnp.zeros_like(grad_keys)
    grad_values[...] = jnp.zeros_like(grad_values)
    head_gain_grad[...] = jnp.zeros_like(head_gain_grad)
    n_keys = 3 * rows
    gap = (
        lax.broadcasted_iota(jnp.int32, (rows, n_keys), 0)
        - lax.broadcasted_iota(jnp.int32, (rows, n_keys), 1)
        + 2 * rows
    )
    reach = jnp.minimum(position[...], WINDOW - 1)
    query_gain = gains[:, 2 * depth : 2 * depth + HD]
    key_gain = gains[:, 2 * depth + HD :]
    scale = HD ** (-0.5)

    def heads(first, last):
        @pl.loop(first, last)
        def _(h):
            at = pl.ds(pl.multiple_of(h * HD, HD), HD)
            group = pl.ds(pl.multiple_of(lax.div(h, HQ // KVH) * HD, HD), HD)
            keys = key_rows[:, :, group].reshape(n_keys, HD)
            values = value_rows[:, :, group].reshape(n_keys, HD)
            probs = soft_rows(query[:, at], keys, reach, gap)
            grad_probs = dot_nt(grad_mixed[:, at], values)
            delta = jnp.sum(probs * grad_probs, axis=-1, keepdims=True)
            grad_scores = (probs * (grad_probs - delta)).astype(BF16)
            grad_rot = jnp.dot(grad_scores, keys, preferred_element_type=F32) * scale
            grad_keys[:, :, group] += (dot_tn(grad_scores, query[:, at]) * scale).reshape(
                3, rows, HD
            )
            grad_values[:, :, group] += dot_tn(probs.astype(BF16), grad_mixed[:, at]).reshape(
                3, rows, HD
            )
            back, gain_grad = head_back(
                grad_rot, projected[:, at], query_gain, cosine[...], sine[...]
            )
            grad_projected[:, at] = back.astype(BF16)
            head_gain_grad[:, 0:HD] += gain_grad

    halo = []

    def send_back(g):
        at = slice(g * HD, (g + 1) * HD)
        lanes = pl.ds(g * HD, HD)
        for d in (2, 1):
            for j, grad in enumerate((grad_keys, grad_values)):
                slot = 2 * (d - 1) + j
                halo_out[slot, :, at] = grad[2 - d, :, at].astype(BF16)
                halo.append(
                    remote(
                        halo_out.at[slot, :, lanes],
                        halo_in.at[slot, :, lanes],
                        halo_s.at[g, slot],
                        halo_r.at[g, slot],
                        behind[d - 1],
                    )
                )
                halo[-1].start()

    last = chain - 1
    scatter.sideways(last - 2)
    if chain > 4:
        scatter.finish(last - 4)
    scatter.halve(last)
    for fill in fills:
        fill.wait()
    heads(0, 1)
    scatter.sideways(last - 1)
    scatter.finish(last - 3)
    heads(1, 4)
    send_back(0)
    scatter.sideways(last)
    scatter.finish(last - 2)
    heads(4, 8)
    send_back(1)
    scatter.finish(last - 1)
    load_qkv.wait()

    @pl.loop(0, chain)
    def _(k):
        at = pl.ds(pl.multiple_of(k * tile, tile), tile)
        grad_normed[:, at] = dot_nt(
            grad_projected[:, 0:query_width],
            weight[k, :, :, :, :, 0:query_width].reshape(tile, query_width),
        )

    for copy in halo:
        copy.wait_recv()
    for g in range(KVH):
        at = slice(g * HD, (g + 1) * HD)
        place = slice(query_width + g * HD, query_width + (g + 1) * HD)
        grad_rot = (
            grad_keys[2, :, at] + halo_in[0, :, at].astype(F32) + halo_in[2, :, at].astype(F32)
        )
        back, gain_grad = head_back(
            grad_rot, projected[:, place], key_gain, cosine[...], sine[...]
        )
        grad_projected[:, place] = back.astype(BF16)
        head_gain_grad[:, HD : 2 * HD] += gain_grad
    grad_projected[:, query_width + kv_width :] = (
        grad_values[2] + halo_in[1].astype(F32) + halo_in[3].astype(F32)
    ).astype(BF16)

    @pl.loop(0, chain)
    def _(k):
        at = pl.ds(pl.multiple_of(k * tile, tile), tile)
        grad_normed[:, at] += dot_nt(
            grad_projected[:, query_width:],
            weight[k, :, :, :, :, query_width:].reshape(tile, 2 * kv_width),
        )

    attn_gain_grad[...] = jnp.zeros_like(attn_gain_grad)
    attn_gain = gains[:, :depth]

    @pl.loop(0, rows // 16)
    def _(i):
        at = pl.ds(pl.multiple_of(i * 16, 16), 16)
        field = tokens[at].astype(F32)
        rms = head_norm(field)
        grad = grad_normed[at]
        weighted = grad * attn_gain
        back = rms * weighted - field * (
            rms * rms * rms * jnp.mean(weighted * field, axis=-1, keepdims=True)
        )
        input_grad[at] = (grad_one[at] + back).astype(BF16)
        attn_gain_grad[...] += jnp.sum(grad * field * rms, axis=0, keepdims=True)

    scatter.finish(last)
    scatter.total()
    for copy in halo:
        copy.wait_send()


def attention_backward(
    full_a,
    full_b,
    grad_one_b,
    grad_one,
    tokens,
    mixed,
    second,
    grad_side,
    cotangent,
    combined,
    query,
    key_rows,
    value_rows,
    projected,
    gains,
    cosine,
    sine,
    position,
):
    count = lax.axis_size("fsdp")
    chain = count // PLANE
    rows, depth = tokens.shape
    weight_rows, out_width = full_b.shape[0] // count, full_b.shape[1]
    dma = pltpu.SemaphoreType.DMA
    anywhere, vmem = pl.BlockSpec(memory_space=pl.ANY), pl.BlockSpec(memory_space=pltpu.VMEM)
    blocked = [
        array.reshape(chain, 2, 2, 2, weight_rows, array.shape[1])
        for array in (full_a, full_b)
    ]
    kv_width = KVH * HD
    filled = (grad_one, tokens, query, key_rows, value_rows, projected)
    return pl.pallas_call(
        functools.partial(attention_backward_kernel, count),
        out_shape=[
            jax.ShapeDtypeStruct((weight_rows, out_width), F32),
            jax.ShapeDtypeStruct((rows, QKV_WIDTH), BF16),
            jax.ShapeDtypeStruct((rows, depth), BF16),
            jax.ShapeDtypeStruct((1, depth), F32),
            jax.ShapeDtypeStruct((1, 2 * HD), F32),
        ],
        in_specs=[anywhere] * 8 + [vmem] * 10,
        out_specs=[vmem] * 5,
        scratch_shapes=[
            pltpu.VMEM((chain, 2, 2, 2, weight_rows, QKV_WIDTH), BF16),
            pltpu.VMEM((rows, HQ * HD), BF16),
            pltpu.VMEM((rows, depth), F32),
            pltpu.VMEM((3, rows, kv_width), F32),
            pltpu.VMEM((3, rows, kv_width), F32),
            pltpu.VMEM((4, rows, kv_width), BF16),
            pltpu.VMEM((4, rows, kv_width), BF16),
            *(
                pltpu.VMEM(array.shape, array.dtype)
                for array in filled
            ),
            dma,
            dma((len(filled),)),
            dma((KVH, 4)),
            dma((KVH, 4)),
        ]
        + scatter_scratch(chain, weight_rows, out_width),
        compiler_params=pltpu.CompilerParams(
            collective_id=1, has_side_effects=True, vmem_limit_bytes=62 * 2**20
        ),
        cost_estimate=pl.CostEstimate(
            flops=40 * 10**9, bytes_accessed=180 * 2**20, transcendentals=0
        ),
        name="attention_backward",
    )(
        *blocked,
        grad_one,
        tokens,
        query,
        key_rows,
        value_rows,
        projected,
        grad_one_b,
        mixed,
        second,
        grad_side,
        cotangent,
        combined,
        gains,
        cosine,
        sine,
        position,
    )


def qkv_scatter_kernel(count, gain_part, normed, grad_projected, out_sum, gain_sem, part, *scratch):
    chain = count // PLANE
    scatter = WeightScatter(chain, part, out_sum, *scratch)
    greet(scatter.partners)
    width = grad_projected.shape[1]
    places = []
    for s in range(chain):
        places.append(
            pltpu.make_async_copy(
                gain_part.at[scatter.blocks[s]],
                part.at[s, :, :, :, :, pl.ds(width, LANES)],
                gain_sem.at[s],
            )
        )
        places[-1].start()
    tile = normed.shape[1] // chain
    block_shape = part.shape[1:5]
    for i in range(chain + 3):
        if i < chain:
            s = scatter.order[i]
            left = normed[:, pl.ds(pl.multiple_of(scatter.blocks[s] * tile, tile), tile)]

            @pl.loop(0, width // 512)
            def _(n):
                at = pl.ds(pl.multiple_of(n * 512, 512), 512)
                part[s, :, :, :, :, at] = (
                    dot_tn(left, grad_projected[:, at]).astype(BF16).reshape(block_shape + (512,))
                )

            places[s].wait()
            scatter.cross(i)
        if 1 <= i <= chain:
            scatter.halve(i - 1)
        if 2 <= i <= chain + 1:
            scatter.sideways(i - 2)
        if i >= 3:
            scatter.finish(i - 3)
    scatter.total()


def qkv_scatter(gain_part, normed, grad_projected):
    count = lax.axis_size("fsdp")
    chain = count // PLANE
    weight_rows, width = normed.shape[1] // count, grad_projected.shape[1] + LANES
    vmem = pl.BlockSpec(memory_space=pltpu.VMEM)
    return pl.pallas_call(
        functools.partial(qkv_scatter_kernel, count),
        out_shape=jax.ShapeDtypeStruct((weight_rows, width), F32),
        in_specs=[pl.BlockSpec(memory_space=pl.ANY)] + [vmem] * 2,
        out_specs=vmem,
        scratch_shapes=[pltpu.SemaphoreType.DMA((chain,))]
        + scatter_scratch(chain, weight_rows, width),
        compiler_params=pltpu.CompilerParams(
            collective_id=4, has_side_effects=True, vmem_limit_bytes=48 * 2**20
        ),
        cost_estimate=pl.CostEstimate(
            flops=40 * 10**9, bytes_accessed=180 * 2**20, transcendentals=0
        ),
        name="qkv_scatter",
    )(gain_part.reshape(chain, 2, 2, 2, weight_rows, LANES), normed, grad_projected)


class TokenCube:
    def __init__(self, own, held, part, in_half, in_x, in_y, in_z, gs, gr, ss, sr):
        me = lax.axis_index("fsdp")
        next_x, next_y, next_z = (flipped(me, bit) for bit in TOKEN_BITS)
        self.partners = [next_x, next_y, next_z]
        half = own.shape[0] // 2
        top, low = pl.ds(0, half), pl.ds(half, half)
        self.top, self.low = top, low
        plan = {
            "zt": (own.at[top], held.at[4, top], next_z),
            "zl": (own.at[low], held.at[4, low], next_z),
            "x": (own, held.at[1], next_x),
            "y": (own, held.at[2], next_y),
            "dt": (held.at[1, top], held.at[3, top], next_y),
            "dl": (held.at[2, low], held.at[3, low], next_x),
            "xt": (held.at[4, top], held.at[5, top], next_x),
            "yt": (held.at[4, top], held.at[6, top], next_y),
            "xl": (held.at[4, low], held.at[5, low], next_x),
            "yl": (held.at[4, low], held.at[6, low], next_y),
            "et": (held.at[5, top], held.at[7, top], next_y),
            "el": (held.at[6, low], held.at[7, low], next_x),
        }
        self.gather = {
            name: remote(src, dst, gs.at[i], gr.at[i], device)
            for i, (name, (src, dst, device)) in enumerate(plan.items())
        }
        self.part, self.in_half, self.in_x, self.in_y, self.in_z = part, in_half, in_x, in_y, in_z
        self.waves = []
        side = own.shape[1] // 2
        for w, (base, first) in enumerate(((4, 0), (4, side), (0, 0), (0, side))):
            at = pl.ds(first, side)
            corner = part.at[base + 3, :, at]
            to_x, to_y = part.at[base + 1, :, at], part.at[base + 2, :, at]
            here = part.at[base, :, at]
            wave = {
                "a": remote(corner.at[top], in_half.at[w, 0], ss.at[w, 0], sr.at[w, 0], next_x),
                "b": remote(corner.at[low], in_half.at[w, 1], ss.at[w, 1], sr.at[w, 1], next_y),
                "x": remote(to_x, in_x.at[w], ss.at[w, 2], sr.at[w, 2], next_x),
                "y": remote(to_y, in_y.at[w], ss.at[w, 3], sr.at[w, 3], next_y),
            }
            if base:
                wave["z"] = remote(here, in_z.at[w], ss.at[w, 4], sr.at[w, 4], next_z)
            self.waves.append((wave, at, to_x, to_y, here))

    def start(self, *names):
        for name in names:
            self.gather[name].start()

    def arrive(self, *names):
        for name in names:
            self.gather[name].wait_recv()

    def corners(self, w):
        wave = self.waves[w][0]
        wave["a"].start()
        wave["b"].start()

    def sideways(self, w):
        wave, _, to_x, to_y, _ = self.waves[w]
        wave["a"].wait_recv()
        add_into(to_y.at[self.top], self.in_half.at[w, 0])
        wave["y"].start()
        wave["b"].wait_recv()
        add_into(to_x.at[self.low], self.in_half.at[w, 1])
        wave["x"].start()

    def across(self, w):
        wave, _, _, _, here = self.waves[w]
        wave["x"].wait_recv()
        wave["y"].wait_recv()
        add_into(here, self.in_x.at[w], self.in_y.at[w])
        wave["z"].start()

    def finish(self, out):
        for w in (2, 3):
            wave, side = self.waves[w][:2]
            wave["x"].wait_recv()
            wave["y"].wait_recv()
            self.waves[w - 2][0]["z"].wait_recv()

            @pl.loop(0, out.shape[0] // 16)
            def _(i):
                at = pl.ds(pl.multiple_of(i * 16, 16), 16)
                out[at, side] = (
                    self.part[0, at, side].astype(F32)
                    + self.in_x[w, at].astype(F32)
                    + self.in_y[w, at].astype(F32)
                    + self.in_z[w - 2, at].astype(F32)
                )

        for copy in self.gather.values():
            copy.wait_send()
        for wave, *_ in self.waves:
            for copy in wave.values():
                copy.wait_send()


TOKEN_BITS = (2, 4, 16)
ORDER = (0, 1, 2, 4, 5, 6, 7, 3)


def cube_scratch(rows, width):
    dma = pltpu.SemaphoreType.DMA
    return [
        pltpu.VMEM((8, rows, width), BF16),
        pltpu.VMEM((8, rows, width), BF16),
        pltpu.VMEM((4, 2, rows // 2, width // 2), BF16),
        pltpu.VMEM((4, rows, width // 2), BF16),
        pltpu.VMEM((4, rows, width // 2), BF16),
        pltpu.VMEM((2, rows, width // 2), BF16),
        dma((12,)),
        dma((12,)),
        dma((4, 5)),
        dma((4, 5)),
        dma,
    ]


def load_weights(own, blocks, held, sems):
    rows = blocks.shape[2]
    loads = []
    for m in range(2):
        for i in range(blocks.shape[0]):
            loads.append(
                pltpu.make_async_copy(
                    own.at[m] if i == 0 else blocks.at[i, m],
                    held.at[m, pl.ds(i * rows, rows)],
                    sems.at[m, i],
                )
            )
            loads[-1].start()
    return loads


GELU_A = 0.7978845608028654
GELU_B = 0.044715


def tanh_inner(gate):
    return jnp.tanh(GELU_A * (gate + GELU_B * gate * gate * gate))


def dot_nt(left, right):
    return lax.dot_general(left, right, (((1,), (1,)), ((), ())), preferred_element_type=F32)


def dot_tn(left, right):
    return lax.dot_general(left, right, (((0,), (0,)), ((), ())), preferred_element_type=F32)


HIDDEN_TILE = 512
WIDTH_TILE = 1024


def ffn_forward_kernel(count, own, own_down, own_ffn, blocks, *refs):
    out, held_out, gate_out, up_out, down_out, weights, gate_st, up_st, act = refs[:9]
    load_sem, save_sem, keep_sem, down_local, down_s, down_r = refs[9:15]
    held, part, in_half, in_x, in_y, in_z, gs, gr, ss, sr, own_sem = refs[15:]
    me = lax.axis_index("fsdp")
    bits = weight_bits(count)
    cube = TokenCube(own, held, part, in_half, in_x, in_y, in_z, gs, gr, ss, sr)
    greet(cube.partners + [flipped(me, bit) for bit in bits])
    cube.start("zt", "zl", "x", "y")
    keep = pltpu.make_async_copy(own, held.at[0], own_sem)
    keep.start()
    block = own_down.shape[0]
    down_keep = pltpu.make_async_copy(own_down, weights.at[2, pl.ds(0, block)], down_local)
    down_keep.start()
    downs = []
    for i, bit in enumerate(bits):
        size = block << i
        src = own_down if i == 0 else weights.at[2, pl.ds(0, size)]
        downs.append(
            remote(
                src, weights.at[2, pl.ds(size, size)], down_s.at[i], down_r.at[i], flipped(me, bit)
            )
        )
    downs[0].start()
    loads = load_weights(own_ffn, blocks, weights, load_sem)
    hidden, width = weights.shape[1], weights.shape[2]
    saves = []

    def enter(step):
        j, slot, third = ORDER[step], step % 2, step % 3
        if step >= 2:
            for save in saves[step - 2]:
                save.wait()

        @pl.loop(0, hidden // HIDDEN_TILE)
        def _(n):
            at = pl.ds(pl.multiple_of(n * HIDDEN_TILE, HIDDEN_TILE), HIDDEN_TILE)
            gate = dot_nt(held[j], weights[0, at])
            up = dot_nt(held[j], weights[1, at])
            gate_st[slot, :, at] = gate
            up_st[slot, :, at] = up
            act[third, :, at] = (0.5 * gate * (1.0 + tanh_inner(gate)) * up).astype(BF16)

        saves.append(
            [
                pltpu.make_async_copy(gate_st.at[slot], gate_out.at[j], save_sem.at[0, slot]),
                pltpu.make_async_copy(up_st.at[slot], up_out.at[j], save_sem.at[1, slot]),
            ]
        )
        for save in saves[step]:
            save.start()

    def leave(step):
        j, third = ORDER[step], step % 3

        @pl.loop(0, width // WIDTH_TILE)
        def _(n):
            at = pl.ds(pl.multiple_of(n * WIDTH_TILE, WIDTH_TILE), WIDTH_TILE)
            part[j, :, at] = jnp.dot(
                act[third], weights[2, :, at], preferred_element_type=F32
            ).astype(BF16)

    keep.wait()
    for load in loads:
        load.wait()
    enter(0)
    cube.arrive("x", "y", "zt")
    cube.start("xt", "yt")
    enter(1)
    down_keep.wait()
    for i in range(1, len(downs)):
        downs[i - 1].wait_recv()
        downs[i].start()
    enter(2)
    cube.arrive("zl")
    cube.start("xl", "yl")
    cube.arrive("xt")
    cube.start("et")
    downs[-1].wait_recv()
    leave(0)
    leave(1)
    leave(2)
    save_down = pltpu.make_async_copy(weights.at[2], down_out, down_local)
    save_down.start()
    enter(3)
    cube.arrive("xl", "yt", "yl")
    cube.start("el", "dt", "dl")
    leave(3)
    for step in (4, 5):
        enter(step)
        leave(step)
    cube.arrive("et", "el")
    enter(6)
    leave(6)
    cube.corners(0)
    cube.corners(1)
    cube.arrive("dt", "dl")
    whole = pltpu.make_async_copy(held, held_out, keep_sem)
    whole.start()
    enter(7)
    leave(7)
    cube.sideways(0)
    cube.sideways(1)
    cube.corners(2)
    cube.corners(3)
    cube.across(0)
    cube.across(1)
    cube.sideways(2)
    cube.sideways(3)
    cube.finish(out)
    for save in saves[6] + saves[7] + [save_down, whole]:
        save.wait()
    for copy in downs:
        copy.wait_send()


def ffn_forward(own, own_down, own_ffn, blocks):
    count = lax.axis_size("fsdp")
    rows, width = own.shape
    hidden = blocks.shape[0] * blocks.shape[2]
    n_bits = len(weight_bits(count))
    dma = pltpu.SemaphoreType.DMA
    anywhere = pl.BlockSpec(memory_space=pl.ANY)
    return pl.pallas_call(
        functools.partial(ffn_forward_kernel, count),
        out_shape=[
            jax.ShapeDtypeStruct((rows, width), F32),
            jax.ShapeDtypeStruct((8, rows, width), BF16),
            jax.ShapeDtypeStruct((8, rows, hidden), F32),
            jax.ShapeDtypeStruct((8, rows, hidden), F32),
            jax.ShapeDtypeStruct((hidden, width), BF16),
        ],
        in_specs=[anywhere] * 4,
        out_specs=[pl.BlockSpec(memory_space=pltpu.VMEM)] + [anywhere] * 4,
        scratch_shapes=[
            pltpu.VMEM((3, hidden, width), BF16),
            pltpu.VMEM((2, rows, hidden), F32),
            pltpu.VMEM((2, rows, hidden), F32),
            pltpu.VMEM((3, rows, hidden), BF16),
            dma((2, blocks.shape[0])),
            dma((2, 2)),
            dma,
            dma,
            dma((n_bits,)),
            dma((n_bits,)),
        ]
        + cube_scratch(rows, width),
        compiler_params=pltpu.CompilerParams(
            collective_id=2, has_side_effects=True, vmem_limit_bytes=58 * 2**20
        ),
        cost_estimate=pl.CostEstimate(
            flops=48 * rows * width * hidden, bytes_accessed=300 * 2**20, transcendentals=0
        ),
        name="ffn_forward",
    )(own, own_down, own_ffn, blocks)


def ffn_backward_kernel(own, normed, gate_in, up_in, down, own_ffn, blocks, *refs):
    out, mine, further, landed, weights, gate_st, up_st, grads, stage, fetched = refs[:10]
    load_sem, down_sem, read_sem, write_sem, normed_sem, pair_s, pair_r, fetch_sem = refs[10:18]
    held, part, in_half, in_x, in_y, in_z, gs, gr, ss, sr, own_sem = refs[18:]
    sibling = flipped(lax.axis_index("fsdp"), 1)
    cube = TokenCube(own, held, part, in_half, in_x, in_y, in_z, gs, gr, ss, sr)
    greet(cube.partners + [sibling])
    cube.start("zt", "zl", "x", "y")
    keep = pltpu.make_async_copy(own, held.at[0], own_sem)
    keep.start()
    hidden, width = weights.shape[1], weights.shape[2]
    rows = own.shape[0]
    reads = []
    for step, j in enumerate(ORDER):
        slot = step % 2
        reads.append(
            [
                pltpu.make_async_copy(gate_in.at[j], gate_st.at[slot], read_sem.at[0, slot]),
                pltpu.make_async_copy(up_in.at[j], up_st.at[slot], read_sem.at[1, slot]),
            ]
        )
    for read in reads[0]:
        read.start()
    load_down = pltpu.make_async_copy(down, weights.at[2], down_sem)
    load_down.start()
    loads = load_weights(own_ffn, blocks, weights, load_sem)

    def compute(step):
        j, slot = ORDER[step], step % 2
        if step < 7:
            for read in reads[step + 1]:
                read.start()
        for read in reads[step]:
            read.wait()

        @pl.loop(0, hidden // HIDDEN_TILE)
        def _(n):
            at = pl.ds(pl.multiple_of(n * HIDDEN_TILE, HIDDEN_TILE), HIDDEN_TILE)
            grad_act = dot_nt(held[j], weights[2, at]).astype(BF16).astype(F32)
            gate, up = gate_st[slot, :, at], up_st[slot, :, at]
            inner = tanh_inner(gate)
            gelu = 0.5 * gate * (1.0 + inner)
            slope = 0.5 * (1.0 + inner) + 0.5 * gate * (1.0 - inner * inner) * GELU_A * (
                1.0 + 3.0 * GELU_B * gate * gate
            )
            token = pl.ds(j * rows, rows)
            grads[2, token, at] = (gelu * up).astype(BF16)
            grads[0, token, at] = (grad_act * up * slope).astype(BF16)
            grads[1, token, at] = (grad_act * gelu).astype(BF16)

        if step == 0:
            for load in loads:
                load.wait()
        token = pl.ds(j * rows, rows)

        @pl.loop(0, width // WIDTH_TILE)
        def _(n):
            at = pl.ds(pl.multiple_of(n * WIDTH_TILE, WIDTH_TILE), WIDTH_TILE)
            part[j, :, at] = (
                jnp.dot(grads[0, token], weights[0, :, at], preferred_element_type=F32)
                + jnp.dot(grads[1, token], weights[1, :, at], preferred_element_type=F32)
            ).astype(BF16)

    keep.wait()
    load_down.wait()
    compute(0)
    cube.arrive("x", "y", "zt")
    cube.start("xt", "yt")
    compute(1)
    compute(2)
    cube.arrive("zl")
    cube.start("xl", "yl")
    cube.arrive("xt")
    cube.start("et")
    compute(3)
    cube.arrive("xl", "yt", "yl")
    cube.start("el", "dt", "dl")
    compute(4)
    compute(5)
    cube.arrive("et", "el")
    compute(6)
    cube.corners(0)
    cube.corners(1)
    cube.arrive("dt", "dl")
    compute(7)
    tokens = 8 * rows
    refill = pltpu.make_async_copy(
        normed, weights.at[pl.ds(0, tokens // hidden)], normed_sem
    )
    refill.start()
    tile = stage.shape[1]
    half, quarter = hidden // 2, hidden // 4
    tiles = [(m, i * tile) for m in (2, 0, 1) for i in range(half // tile)]
    pairs, busy = [], [None, None]
    for n, (m, first) in enumerate(tiles):
        pairs.append(
            remote(
                stage.at[n % 2],
                landed.at[m, pl.ds(first, tile)],
                pair_s.at[n],
                pair_r.at[n],
                sibling,
            )
        )
    fetches = [
        pltpu.make_async_copy(
            landed.at[m, pl.ds(first, tile)], fetched.at[n % 2], fetch_sem.at[n % 2]
        )
        for n, (m, first) in enumerate(tiles)
    ]
    done = [0]

    def weight_grad(times):
        for _ in range(times):
            job = done[0]
            done[0] = job + 1
            n, for_sibling = job % len(tiles), job < len(tiles)
            m, first = tiles[n]
            slot = job % 2
            if job == len(tiles) // 3:
                refill.wait()
            if busy[slot] is not None:
                busy[slot]()
            if not for_sibling:
                pairs[n].wait_recv()
                fetches[n].start()
                fetches[n].wait()
            place = first + half if for_sibling else first

            @pl.loop(0, width // WIDTH_TILE)
            def _(k):
                at = pl.ds(pl.multiple_of(k * WIDTH_TILE, WIDTH_TILE), WIDTH_TILE)
                if m == 2:
                    right = held[:, :, at].reshape(tokens, WIDTH_TILE)
                else:
                    right = weights[: tokens // hidden, :, at].reshape(tokens, WIDTH_TILE)
                grad = dot_tn(grads[m, :, pl.ds(place, tile)], right)
                if not for_sibling:
                    grad = grad + fetched[n % 2, :, at].astype(F32)
                stage[slot, :, at] = grad.astype(BF16)

            if for_sibling:
                pairs[n].start()
                busy[slot] = pairs[n].wait_send
            else:
                target = mine if first < quarter else further
                write = pltpu.make_async_copy(
                    stage.at[slot],
                    target.at[m, pl.ds(first % quarter, tile)],
                    write_sem.at[slot],
                )
                write.start()
                busy[slot] = write.wait

    cube.sideways(0)
    cube.sideways(1)
    cube.corners(2)
    cube.corners(3)
    weight_grad(3)
    cube.across(0)
    weight_grad(1)
    cube.sideways(2)
    cube.across(1)
    weight_grad(1)
    cube.sideways(3)
    weight_grad(2 * len(tiles) - 5)
    cube.finish(out)
    for end in busy:
        end()


def ffn_backward(own, normed, gate, up, down, own_ffn, blocks):
    rows, width = own.shape
    hidden = blocks.shape[0] * blocks.shape[2]
    dma = pltpu.SemaphoreType.DMA
    anywhere = pl.BlockSpec(memory_space=pl.ANY)
    tile = 256
    n_tiles = 3 * (hidden // 2) // tile
    grad = jax.ShapeDtypeStruct((3, hidden // 4, width), BF16)
    landed = jax.ShapeDtypeStruct((3, hidden // 2, width), BF16)
    return pl.pallas_call(
        ffn_backward_kernel,
        out_shape=[jax.ShapeDtypeStruct((rows, width), F32), grad, grad, landed],
        in_specs=[anywhere] * 7,
        out_specs=[pl.BlockSpec(memory_space=pltpu.VMEM)] + [anywhere] * 3,
        scratch_shapes=[
            pltpu.VMEM((3, hidden, width), BF16),
            pltpu.VMEM((2, rows, hidden), F32),
            pltpu.VMEM((2, rows, hidden), F32),
            pltpu.VMEM((3, 8 * rows, hidden), BF16),
            pltpu.VMEM((2, tile, width), BF16),
            pltpu.VMEM((2, tile, width), BF16),
            dma((2, blocks.shape[0])),
            dma,
            dma((2, 2)),
            dma((2,)),
            dma,
            dma((n_tiles,)),
            dma((n_tiles,)),
            dma((2,)),
        ]
        + cube_scratch(rows, width),
        compiler_params=pltpu.CompilerParams(
            collective_id=3, has_side_effects=True, vmem_limit_bytes=62 * 2**20
        ),
        cost_estimate=pl.CostEstimate(
            flops=96 * rows * width * hidden, bytes_accessed=400 * 2**20, transcendentals=0
        ),
        name="ffn_backward",
    )(
        own,
        normed.reshape(8 * rows // hidden, hidden, width),
        gate,
        up,
        down,
        own_ffn,
        blocks,
    )


def inv_rms(field):
    return lax.rsqrt(jnp.mean(field * field, axis=-1, keepdims=True) + EPSILON)


def gelu_tanh(field):
    return jax.nn.gelu(field, approximate=True)


def layout(seq_lengths, seq_order, token_index):
    slot_ids = jnp.arange(seq_lengths.shape[0], dtype=jnp.int32)
    packed = jnp.sum(
        jnp.where(seq_order[:, None] == slot_ids[None, :], seq_lengths[None, :], 0), axis=1
    )
    starts = jnp.sum(jnp.where(slot_ids[None, :] < slot_ids[:, None], packed[None, :], 0), axis=1)
    segment = jnp.sum((token_index[:, None] >= starts[None, :]).astype(jnp.int32), axis=1) - 1
    offset = jnp.max(jnp.where(starts[None, :] <= token_index[:, None], starts[None, :], 0), axis=1)
    return (segment, token_index - offset)


def angles(position):
    half_width = HD // 2
    freq = ROPE_BASE ** (-2.0 * jnp.arange(half_width, dtype=jnp.float32) / HD)
    phase = position.astype(jnp.float32)[:, None] * freq[None, :]
    phase = jnp.concatenate([phase, phase], axis=-1)
    return (jnp.cos(phase)[:, None, :], jnp.sin(phase)[:, None, :])


def norm_back(grad_out, field, scale_inv, gain):
    weighted = grad_out * gain
    return scale_inv * weighted - field * scale_inv**3 * jnp.mean(
        weighted * field, axis=-1, keepdims=True
    )


def contract_rows(left_op, right_op):
    return lax.dot_general(
        left_op, right_op, (((0,), (0,)), ((), ())), preferred_element_type=jnp.float32
    )


def contract_cols(left_op, right_op):
    return lax.dot_general(
        left_op, right_op, (((1,), (1,)), ((), ())), preferred_element_type=jnp.float32
    )


def local(
    tokens,
    per_layer,
    cotangent,
    seq_lengths,
    seq_order,
    qkv_weight,
    out_weight,
    ffn_weights,
    side_weights,
    norm_gains,
):
    tok_rows = tokens.shape[0]
    my_index = lax.axis_index("fsdp")
    token_index = my_index * tok_rows + jnp.arange(tok_rows, dtype=jnp.int32)
    segment, position = layout(seq_lengths, seq_order, token_index)
    cosine, sine = angles(position)
    reach = (WINDOW + tok_rows - 2) // tok_rows
    assert reach == 2
    split_at = PL + RANK
    count = lax.axis_size("fsdp")
    bits = weight_bits(count)
    weight_rows = qkv_weight.shape[0]
    ffn_own = ffn_weights[:, :2].transpose(1, 0, 2)
    (
        qkv_gathered,
        out_gathered,
        ffn_blocks,
        normed_b,
        projected,
        query_b,
        key_blocks,
        value_blocks,
        gain_all,
        mixed_b,
        first_sum,
        normed_two,
    ) = attention_forward(
        jnp.concatenate([qkv_weight, placed_gains(norm_gains, weight_rows)], axis=1),
        jnp.concatenate([out_weight, side_weights], axis=1),
        ffn_own,
        tokens,
        cosine[:, 0, : HD // 2],
        sine[:, 0, : HD // 2],
        position[:, None],
    )
    side_all = out_gathered[:, D:]
    ffn_gain = gain_all[0, D : 2 * D]
    rms_two = inv_rms(first_sum)
    ffn_out, normed_all, gate_kept, up_kept, down_all = ffn_forward(
        normed_two, ffn_weights[:, 2], ffn_own, ffn_blocks
    )
    second_sum = first_sum + ffn_out
    second_b = second_sum.astype(jnp.bfloat16)
    side_in = jnp.dot(second_b, side_all[:, :split_at], preferred_element_type=jnp.float32)
    per_f = per_layer.astype(jnp.float32)
    gelu_per, pull_per = jax.vjp(gelu_tanh, side_in[:, :PL])
    combined = jnp.concatenate(
        [(gelu_per * per_f).astype(jnp.bfloat16), side_in[:, PL:].astype(jnp.bfloat16)], axis=1
    )
    output = (second_sum + contract_cols(combined, side_all[:, split_at:])).astype(jnp.bfloat16)
    back_side = side_all
    grad_y = cotangent.astype(jnp.float32)
    grad_comb = jnp.dot(cotangent, back_side[:, split_at:], preferred_element_type=jnp.float32)
    per_layer_grad = (grad_comb[:, :PL] * gelu_per).astype(jnp.bfloat16)
    grad_per = pull_per(grad_comb[:, :PL] * per_f)[0]
    grad_side = jnp.concatenate([grad_per, grad_comb[:, PL:]], axis=1).astype(jnp.bfloat16)
    grad_two = grad_y + contract_cols(grad_side, back_side[:, :split_at])
    grad_two_b = grad_two.astype(jnp.bfloat16)
    grad_h2, ffn_part, ffn_sent, _ = ffn_backward(
        grad_two_b, normed_all, gate_kept, up_kept, down_all, ffn_own, ffn_blocks
    )
    for bit in reversed(bits[:-1]):
        ffn_part = ffn_part.astype(F32) + swapped(ffn_sent, bit).astype(F32)
        if bit != bits[0]:
            half = ffn_part.shape[1] // 2
            ffn_sent = ffn_part[:, half:].astype(BF16)
            ffn_part = ffn_part[:, :half]
    ffn_grad = ffn_part.transpose(1, 0, 2)
    ffn_gain_grad = jnp.sum(grad_h2 * first_sum * rms_two, axis=0)
    grad_one = grad_two + norm_back(grad_h2, first_sum, rms_two, ffn_gain)
    grad_one_b = grad_one.astype(jnp.bfloat16)
    out_sum, grad_projected, input_grad, attn_gain_grad, head_gain_grad = attention_backward(
        qkv_gathered,
        out_gathered,
        grad_one_b,
        grad_one,
        tokens,
        mixed_b,
        second_b,
        jnp.pad(grad_side, ((0, 0), (0, split_at))),
        cotangent,
        jnp.pad(combined, ((0, 0), (split_at, 0))),
        query_b,
        key_blocks,
        value_blocks,
        projected,
        gain_all,
        cosine[:, 0, : HD // 2],
        sine[:, 0, : HD // 2],
        position[:, None],
    )
    gains_grad_full = jnp.concatenate([attn_gain_grad[0], ffn_gain_grad, head_gain_grad[0]])
    gain_rows = jnp.pad(
        gains_grad_full.astype(BF16).reshape(count, -1),
        ((0, 0), (0, weight_rows * LANES - norm_gains.shape[0])),
    ).reshape(count * weight_rows, LANES)
    qkv_sum = qkv_scatter(gain_rows, normed_b, grad_projected)
    qkv_grad = qkv_sum[:, : qkv_weight.shape[1]]
    gains_grad = qkv_sum[:, qkv_weight.shape[1] :].reshape(-1)[: norm_gains.shape[0]]
    out_grad, side_grad = out_sum[:, :D], out_sum[:, D:]
    return (output, input_grad, per_layer_grad, qkv_grad, out_grad, ffn_grad, side_grad, gains_grad)


def solution(mesh):
    return jax.shard_map(
        local,
        mesh=mesh,
        in_specs=(
            P("fsdp", None),
            P("fsdp", None),
            P("fsdp", None),
            P(),
            P(),
            P("fsdp", None),
            P("fsdp", None),
            P("fsdp", None, None),
            P("fsdp", None),
            P("fsdp"),
        ),
        out_specs=(
            P("fsdp", None),
            P("fsdp", None),
            P("fsdp", None),
            P("fsdp", None),
            P("fsdp", None),
            P("fsdp", None, None),
            P("fsdp", None),
            P("fsdp"),
        ),
        check_vma=False,
    )
```
